128 devices in a mesh: space: 4 (over x), kx: 4 (over y_hi, core), ky: 8 (over y_lo, z).
Axes of the slice: x: 4, y: 4 (y_hi: 2, y_lo: 2; y = y_hi * 2 + y_lo), z: 4, core: 2. Of those that a mesh axis runs over, the one named last changes fastest.
Arguments:
- action: float32 [64, 64, 64, 256], P('kx', 'ky', 'space'), may hold values from 0.05 to 2
- depth_cm: int32 [64, 256], P('space'), may hold values from 120 to 599
- inflow_mask: int32 [64, 256], P('space'), may hold values 0 or 1
- inflow: float32 [64, 64], replicated, may hold values from 0.05 to 2
Outputs:
- action_next: float32 [64, 64, 64, 256], P('kx', 'ky', 'space')
The draws below stay inside these ranges and needn't reach their ends.
All inputs are finite; a program needn't handle non-finite values. No bound on the sum of `inflow_mask` on one device may be relied on, other than what follows from the above.
Results may differ from the reference program's by a relative error of at most 0.035.
Values sent between devices are 32-bit elements; how exact they have to be, the bound alone decides.
No kernel may reach another device: no remote copies, remote signals or barrier semaphores. Data moves between devices by JAX's collectives and lax.ppermute only.
A program may use at most 128 MiB of HBM per device.

```python
import math
import jax
import jax.numpy as jnp
from jax import lax

NKX = 64
NKY = 64
NY = 256
NX = 64


def touch_ends(entries, key, smallest, largest):
    shape = entries.shape
    place = [jax.random.randint(jax.random.fold_in(key, axis), (), 0, shape[axis]) for axis in range(len(shape))]
    entries = entries.at[tuple(place)].set(smallest)
    longest = shape.index(max(shape))
    place[longest] = (place[longest] + 1) % shape[longest]
    return entries.at[tuple(place)].set(largest)


def block_levels(stream_key, shape, pieces, smallest, largest):
    def one(position, parts):
        steps = jax.random.uniform(jax.random.fold_in(jax.random.fold_in(stream_key, 6), position), (parts,), jnp.float32, smallest / len(pieces), largest / len(pieces))
        return jnp.repeat(jnp.exp(steps), shape[position] // parts).reshape((-1,) + (1,) * (len(shape) - position - 1))

    level = one(*pieces[0])
    for cut in pieces[1:]:
        level = level * one(*cut)
    return level


def setup_inputs(seed: int = 0) -> dict:
    arg_keys = jax.random.split(jax.random.key(seed), 5)
    action = jnp.clip(jnp.exp(math.log(2.0) - 3.6888794 * jax.random.uniform(arg_keys[0], (NKX, NKY, NX, NY), jnp.float32) ** block_levels(arg_keys[0], (NKX, NKY, NX, NY), ((0, 4), (1, 8), (2, 4)), -0.2, 0.2)), 0.05, 2.0)
    depth_cm = touch_ends(jax.random.randint(arg_keys[1], (NX, NY), 120, 600), jax.random.fold_in(arg_keys[1], 1), 120, 599).astype(jnp.int32)
    inflow_mask = touch_ends((jax.random.randint(arg_keys[2], (NX, NY), 0, 16) < 1).astype(jnp.int32), jax.random.fold_in(arg_keys[2], 1), 0, 1)
    inflow = jnp.clip(jnp.exp(jax.random.uniform(arg_keys[3], (NKX, NKY), jnp.float32, math.log(0.05), math.log(2.0))), 0.05, 2.0)
    return {"action": action, "depth_cm": depth_cm, "inflow_mask": inflow_mask, "inflow": inflow}


gravity = 9.81
spacing = 4.0
k_step = 0.04
time_step = 0.2
kx_block = 8

def group_speed(kx_value, ky_value, depth_m):
    modulus = jnp.sqrt(kx_value * kx_value + ky_value * ky_value)
    tangent = jnp.tanh(modulus * depth_m)
    frequency = jnp.sqrt(gravity * modulus * tangent)
    damping = 1.0 - tangent * tangent
    return gravity * (tangent + modulus * depth_m * damping) / (2.0 * frequency * modulus)

def refraction(kx_value, ky_value, depth_m):
    modulus = jnp.sqrt(kx_value * kx_value + ky_value * ky_value)
    tangent = jnp.tanh(modulus * depth_m)
    frequency = jnp.sqrt(gravity * modulus * tangent)
    damping = 1.0 - tangent * tangent
    return gravity * modulus * modulus * damping / (2.0 * frequency)

def centred(extended, kept_dim):
    for dimension in range(4):
        if dimension != kept_dim:
            extended = lax.slice_in_dim(extended, 2, extended.shape[dimension] - 2, axis=dimension)
    return extended

def upwind(padded, velocity, along_dim):
    extent = padded.shape[along_dim] - 4

    def section(first_cell, cell_count):
        return lax.slice_in_dim(padded, first_cell, first_cell + cell_count, axis=along_dim)
    left_side = 1.5 * section(1, extent + 1) - 0.5 * section(0, extent + 1)
    right_side = 1.5 * section(2, extent + 1) - 0.5 * section(3, extent + 1)
    face_flux = jnp.maximum(velocity, 0.0) * left_side + jnp.minimum(velocity, 0.0) * right_side
    return lax.slice_in_dim(face_flux, 1, extent + 1, axis=along_dim) - lax.slice_in_dim(face_flux, 0, extent, axis=along_dim)

def tendency(padded, depth_pad, kx_first, ky_first):
    extended = jnp.pad(padded, ((0, 0), (0, 0), (0, 0), (2, 2)))
    kx_rows = padded.shape[0] - 4
    ky_rows = padded.shape[1] - 4
    kx_centre = ((kx_first + jnp.arange(kx_rows, dtype=jnp.int32) - NKX // 2).astype(jnp.float32) + 0.5) * k_step
    kx_face = (kx_first + jnp.arange(kx_rows + 1, dtype=jnp.int32) - NKX // 2).astype(jnp.float32) * k_step
    ky_centre = ((ky_first + jnp.arange(ky_rows, dtype=jnp.int32) - NKY // 2).astype(jnp.float32) + 0.5) * k_step
    ky_face = (ky_first + jnp.arange(ky_rows + 1, dtype=jnp.int32) - NKY // 2).astype(jnp.float32) * k_step
    kx_centre = kx_centre.reshape(-1, 1, 1, 1)
    kx_face = kx_face.reshape(-1, 1, 1, 1)
    ky_centre = ky_centre.reshape(1, -1, 1, 1)
    ky_face = ky_face.reshape(1, -1, 1, 1)
    depth_centre = depth_pad[1:-1, 1:-1][None, None]
    depth_xface = (0.5 * (depth_pad[:-1, 1:-1] + depth_pad[1:, 1:-1]))[None, None]
    depth_yface = (0.5 * (depth_pad[1:-1, :-1] + depth_pad[1:-1, 1:]))[None, None]
    slope_x = ((depth_pad[2:, 1:-1] - depth_pad[:-2, 1:-1]) / (2.0 * spacing))[None, None]
    slope_y = ((depth_pad[1:-1, 2:] - depth_pad[1:-1, :-2]) / (2.0 * spacing))[None, None]
    speed_x = group_speed(kx_centre, ky_centre, depth_xface) * kx_centre
    speed_y = group_speed(kx_centre, ky_centre, depth_yface) * ky_centre
    speed_kx = -refraction(kx_face, ky_centre, depth_centre) * slope_x
    speed_ky = -refraction(kx_centre, ky_face, depth_centre) * slope_y
    total = upwind(centred(extended, 2), speed_x, 2) / spacing
    total = total + upwind(centred(extended, 3), speed_y, 3) / spacing
    total = total + upwind(centred(extended, 0), speed_kx, 0) / k_step
    total = total + upwind(centred(extended, 1), speed_ky, 1) / k_step
    return -total

def hold(values, mask_rows, spectrum):
    return jnp.where(mask_rows[None, None] == 1, spectrum[:, :, None, None], values)

def reference(action, depth_cm, inflow_mask, inflow):
    heights = jnp.pad(depth_cm.astype(jnp.float32) * 0.01, 1, mode='edge')

    def change(values):
        padded = jnp.pad(values, ((2, 2), (2, 2), (2, 2), (0, 0)))

        def kx_piece(offset):
            window = lax.dynamic_slice_in_dim(padded, offset, kx_block + 4, 0)
            return tendency(window, heights, offset, 0)
        offsets = jnp.arange(NKX // kx_block, dtype=jnp.int32) * kx_block
        return lax.map(kx_piece, offsets).reshape(values.shape)
    segment_one = hold(action + time_step * change(action), inflow_mask, inflow)
    return hold(0.5 * (action + segment_one + time_step * change(segment_one)), inflow_mask, inflow)
```

```python
import functools

import jax
import jax.numpy as jnp
from jax import lax
from jax.experimental import pallas as pl
from jax.experimental.pallas import tpu as pltpu
from jax.sharding import PartitionSpec as P

NKX = 64
NKY = 64

gravity = 9.81
spacing = 4.0
k_step = 0.04
time_step = 0.2

BX, BY, BS, NY = 16, 8, 16, 256
SLAB = BS
f32 = jnp.float32
VMEM = pltpu.VMEM
LIMIT = 48 * 2**20

X_SCALE = time_step / spacing * 0.5
K_SCALE = time_step / k_step * 0.5


def even_pairs(count):
    return [(i, i ^ 1) for i in range(count)]


def odd_pairs(count):
    pairs = []
    for i in range(1, count, 2):
        pairs += [(i, (i + 1) % count), ((i + 1) % count, i)]
    return pairs


def place():
    s, i, j = lax.axis_index("space"), lax.axis_index("kx"), lax.axis_index("ky")
    return s, i, j, i >= lax.axis_size("kx") // 2, j >= lax.axis_size("ky") // 2


def edge_rows(rows, base, x_up, refs):
    def one_kx(i, carry):
        for at, r in ((0, jnp.where(x_up, BS - 1, 0)), (BX * BY, jnp.where(x_up, BS - 2, 1))):
            for j in range(BY):
                slab = i * BY + j
                row = rows[pl.ds(base + slab * BS + r, 1), :]
                for ref in refs:
                    ref[pl.ds(at + slab, 1), :] = row
        return carry

    lax.fori_loop(0, BX, one_kx, 0)


def first_messages(a, depth, np_ref, ky_od, ky_ev, kx_od, kx_ev, x_od, x_ev, sems):
    s, i, j, x_up, _ = place()
    copies = []

    def copy(src, dst):
        c = pltpu.make_async_copy(src, dst, sems.at[len(copies)])
        c.start()
        copies.append(c)

    ky_even, kx_even, s_even = j % 2 == 0, i % 2 == 0, s % 2 == 0
    copy(a.at[:, pl.ds(jnp.where(ky_even, 0, BY - 2), 2)], ky_od)
    copy(a.at[:, pl.ds(jnp.where(ky_even, BY - 2, 0), 2)], ky_ev)
    copy(a, np_ref.at[pl.ds(2, BX)])
    copy(a.at[pl.ds(jnp.where(kx_even, 0, BX - 2), 2)], kx_od)
    copy(a.at[pl.ds(jnp.where(kx_even, BX - 2, 0), 2)], kx_ev)
    copies[2].wait()
    rows = np_ref.reshape((BX + 4) * BY * BS, NY)
    base = 2 * BY * BS
    edge_rows(rows, base, x_up, (x_od, x_ev))
    low = jnp.broadcast_to(depth[0:1, :].astype(f32), (8, NY))
    high = jnp.broadcast_to(depth[BS - 1 : BS, :].astype(f32), (8, NY))
    for ref, above in ((x_od, jnp.logical_not(s_even)), (x_ev, s_even)):
        ref[pl.ds(256, 8), :] = jnp.where(above, high, low)
    for c in (copies[0], copies[1], copies[3], copies[4]):
        c.wait()


def shifted(h, axis, up):
    size = h.shape[axis]
    place_of = lax.broadcasted_iota(jnp.int32, h.shape, axis)
    if up:
        return jnp.where(place_of == size - 1, h, pltpu.roll(h, size - 1, axis))
    return jnp.where(place_of == 0, h, pltpu.roll(h, 1, axis))


def group(k, c, h):
    kh = k * h
    t = jnp.tanh(kh)
    return c * ((t + kh * (1.0 - t * t)) * lax.rsqrt(t))


def refract(k, c, h):
    t = jnp.tanh(k * h)
    return c * ((1.0 - t * t) * lax.rsqrt(t))


def speeds(tab, depth, ax, ay, rkx, aky, gy, geo):
    _, _, _, x_up, y_up = place()
    h = depth[...].astype(f32) * 0.01
    hx = 0.5 * (h + jnp.where(x_up, shifted(h, 0, True), shifted(h, 0, False)))
    y_next, y_last = shifted(h, 1, True), shifted(h, 1, False)
    hy = 0.5 * (h + jnp.where(y_up, y_next, y_last))
    slope = (y_last - y_next) * (1.0 / (2.0 * spacing))
    gy[...] = slope
    geo[0] = h
    geo[1] = hx
    geo[2] = hy

    def one_kx(i, carry):
        for j in range(BY):
            n = i * BY + j
            r = pl.ds(pl.multiple_of(n * BS, BS), BS)
            k = tab[0, n]
            ax[r, :] = group(k, tab[1, n], geo[1])
            ay[r, :] = group(k, tab[2, n], geo[2])
            rkx[r, :] = refract(tab[3, n], tab[4, n], geo[0])
        for j in range(BY + 1):
            n = i * (BY + 1) + j
            r = pl.ds(pl.multiple_of(n * BS, BS), BS)
            aky[r, :] = refract(tab[5, n], tab[6, n], geo[0]) * gy[...]
        return carry

    lax.fori_loop(0, BX, one_kx, 0)
    for j in range(BY):
        n = BX * BY + j
        rkx[pl.ds(n * BS, BS), :] = refract(tab[3, n], tab[4, n], geo[0])


class Flow:
    def __init__(self, x_up, y_up):
        x0 = jnp.where(x_up, 0, 8)
        y0 = jnp.where(y_up, 0, 128)
        self.x = (pl.multiple_of(x0, 8), pl.multiple_of(8 - x0, 8))
        self.y = (pl.multiple_of(y0, 128), pl.multiple_of(128 - y0, 128))
        self.x_roll = jnp.where(x_up, 1, 7)
        self.y_roll = jnp.where(y_up, 1, 127)
        rows = lax.broadcasted_iota(jnp.int32, (8, 128), 0)
        lanes = lax.broadcasted_iota(jnp.int32, (8, 128), 1)
        self.x_first = rows == jnp.where(x_up, 0, 7)
        self.x_last = rows == jnp.where(x_up, 7, 0)
        self.y_first = lanes == jnp.where(y_up, 0, 127)

    def load(self, ref, slab):
        r = slab * BS
        return [
            [ref[pl.ds(pl.multiple_of(r + self.x[a], 8), 8), pl.ds(self.y[b], 128)] for b in range(2)]
            for a in range(2)
        ]

    def store(self, ref, slab, tiles):
        r = slab * BS
        for a in range(2):
            for b in range(2):
                ref[pl.ds(pl.multiple_of(r + self.x[a], 8), 8), pl.ds(self.y[b], 128)] = tiles[a][b]

    def row(self, ref, first, j, b):
        tile = ref[pl.ds(pl.multiple_of(first, 8), 8), pl.ds(self.y[b], 128)]
        return jnp.broadcast_to(tile[j : j + 1, :], (8, 128))

    def before_x(self, tiles, b, halo):
        first, second = (pltpu.roll(tiles[a][b], self.x_roll, 0) for a in range(2))
        return [jnp.where(self.x_first, halo, first), jnp.where(self.x_first, first, second)]

    def before_y(self, tiles, a):
        first, second = (pltpu.roll(tiles[a][b], self.y_roll, 1) for b in range(2))
        return [jnp.where(self.y_first, 0.0, first), jnp.where(self.y_first, first, second)]


def each(fn, *grids):
    return [[fn(*(g[a][b] for g in grids)) for b in range(2)] for a in range(2)]


def space_change(flow, n3, n, ax_ref, ay_ref, i, j, edge, halo_row, halo_flux):
    slab, first = i * BY + j, i * BY
    ax = flow.load(ax_ref, slab)
    ay = flow.load(ay_ref, slab)
    total = [[None, None], [None, None]]
    for b in range(2):
        ax[1][b] = jnp.where(flow.x_last, flow.row(edge, first, j, b), ax[1][b])
        before = flow.before_x(n, b, flow.row(halo_row, first, j, b))
        out = [[ax[a][b] * (n3[a][b] - before[a])] * 2 for a in range(2)]
        into = flow.before_x(out, b, flow.row(halo_flux, first, j, b))
        for a in range(2):
            total[a][b] = out[a][b] - into[a]
    for a in range(2):
        before = flow.before_y(n, a)
        out = [ay[a][b] * (n3[a][b] - before[b]) for b in range(2)]
        into = flow.before_y([out, out], 0)
        for b in range(2):
            total[a][b] = total[a][b] + (out[b] - into[b])
    return total


def face(up, speed, n_2, n_1, n1, n2):
    near = jnp.where(up, n_1, n1)
    far = jnp.where(up, n_2, n2)
    return speed * (3.0 * near - far)


def times3(tiles):
    return each(lambda v: 3.0 * v, tiles)


def edge_speeds(flow, kcol, ccol, h_row, out, i):
    for b in range(2):
        y = pl.ds(flow.y[b], 128)
        r = pl.ds(pl.multiple_of(i * BY, BY), BY)
        out[r, y] = group(kcol[r, :], ccol[r, :], flow.row(h_row, 0, 0, b))


def stage_one_space(
    np_in, ax, ay, rkx, aky, gy, geo, depth, mask, spec, kcol, ccol, kx_od, kx_ev, x_od, x_ev,
    np_ref, p_ref, gx, edge, halo_speed, ky2_od, ky2_ev, fk, hrow, xnear, xflux, sems,
):
    s, i, j, x_up, y_up = place()
    flow = Flow(x_up, y_up)
    s_count, kx_count = lax.axis_size("space"), lax.axis_size("kx")
    s_even, kx_even, ky_even = s % 2 == 0, i % 2 == 0, j % 2 == 0
    cells = BY * BS
    below = jnp.where(kx_even, kx_od[...], kx_ev[...])
    np_ref[pl.ds(0, 2 * cells), :] = jnp.where(i == 0, 0.0, below)
    above = jnp.where(kx_even, kx_ev[...], kx_od[...])
    np_ref[pl.ds((BX + 2) * cells, 2 * cells), :] = jnp.where(i == kx_count - 1, 0.0, above)
    h = geo[0]
    h_low = jnp.where(s_even, x_od[pl.ds(256, 1), :], x_ev[pl.ds(256, 1), :]) * 0.01
    h_low = jnp.where(s == 0, h[0:1, :], h_low)
    h_high = jnp.where(s_even, x_ev[pl.ds(256, 1), :], x_od[pl.ds(256, 1), :]) * 0.01
    h_high = jnp.where(s == s_count - 1, h[BS - 1 : BS, :], h_high)
    place_of = lax.broadcasted_iota(jnp.int32, (BS, NY), 0)
    before = jnp.where(place_of == 0, h_low, pltpu.roll(h, 1, 0))
    after = jnp.where(place_of == BS - 1, h_high, pltpu.roll(h, BS - 1, 0))
    gx[...] = (before - after) * (1.0 / (2.0 * spacing))
    face_low = 0.5 * (h_low + h[0:1, :])
    face_high = 0.5 * (h_high + h[BS - 1 : BS, :])
    hrow[0:1, :] = jnp.where(x_up, face_high, face_low)
    hrow[8:9, :] = jnp.where(x_up, face_low, face_high)
    none = jnp.logical_or(jnp.logical_and(x_up, s == 0), jnp.logical_and(jnp.logical_not(x_up), s == s_count - 1))
    use_od = s_even == x_up
    near = jnp.where(use_od, x_od[pl.ds(0, 128), :], x_ev[pl.ds(0, 128), :])
    far = jnp.where(use_od, x_od[pl.ds(128, 128), :], x_ev[pl.ds(128, 128), :])
    near = jnp.where(none, 0.0, near)
    xnear[...] = near
    xflux[...] = 3.0 * near - jnp.where(none, 0.0, far)
    out_row, in_row = hrow.at[pl.ds(0, 8)], hrow.at[pl.ds(8, 8)]

    def edges(i, carry):
        edge_speeds(flow, kcol, ccol, out_row, edge, i)
        edge_speeds(flow, kcol, ccol, in_row, halo_speed, i)
        r = pl.ds(pl.multiple_of(i * BY, BY), BY)
        xflux[r, :] = xflux[r, :] * halo_speed[r, :]
        return carry

    lax.fori_loop(0, BX, edges, 0)

    tgx = flow.load(gx, 0)

    def kx_flux(i, j):
        n = [flow.load(np_ref, (i + d) * BY + j) for d in range(4)]
        r = flow.load(rkx, i * BY + j)
        return each(lambda g, r, *n: face(g > 0, r * g, *n), tgx, r, *n)

    for j in range(BY):
        flow.store(fk, j, kx_flux(0, j))

    def one_kx(i, carry):
        hold = each(lambda m: m == 1, flow.load(mask, 0))
        layer = [flow.load(np_ref, (i + 2) * BY + j) for j in range(BY)]
        part = {}
        for j in range(BY):
            slab = i * BY + j
            n = layer[j]
            total = space_change(flow, times3(n), n, ax, ay, i, j, edge, xnear, xflux)
            upper = kx_flux(i + 1, j)
            lower = flow.load(fk, j)
            flow.store(fk, j, upper)
            p = each(lambda n, t, u, v: n - (t + (u - v)), n, total, upper, lower)
            flow.store(p_ref, slab, p)
            if j in (0, 1, BY - 2, BY - 1):
                part[j] = p

        def own(f, a, b):
            w = flow.load(aky, i * (BY + 1) + f)
            return each(lambda w, a, b: w * (3.0 * a - b), w, layer[a], layer[b])

        def send(j, low, high, ref, l):
            v = each(
                lambda m, p, u, v: jnp.where(m, spec[i * BY + j], p - (u - v)), hold, part[j], high, low
            )
            flow.store(ref, i * 2 + l, v)

        f = [own(0, 0, 1), own(1, 1, 2), own(2, 2, 3)]
        down = [(0, f[0], f[1]), (1, f[1], f[2])]
        g = [own(BY - 2, BY - 3, BY - 4), own(BY - 1, BY - 2, BY - 3), own(BY, BY - 1, BY - 2)]
        up = [(BY - 2, g[0], g[1]), (BY - 1, g[1], g[2])]

        @pl.when(ky_even)
        def _():
            for l in range(2):
                send(*down[l], ky2_od, l)
                send(*up[l], ky2_ev, l)

        @pl.when(jnp.logical_not(ky_even))
        def _():
            for l in range(2):
                send(*down[l], ky2_ev, l)
                send(*up[l], ky2_od, l)

        return carry

    lax.fori_loop(0, BX, one_kx, 0)


def ky_halos(od, ev, low, high):
    j = lax.axis_index("ky")
    last = lax.axis_size("ky") - 1
    even = j % 2 == 0

    def fill(ref, first, second, empty):
        @pl.when(empty)
        def _():
            ref[...] = jnp.zeros(ref.shape, f32)

        @pl.when(jnp.logical_and(even, jnp.logical_not(empty)))
        def _():
            ref[...] = first[...]

        @pl.when(jnp.logical_and(jnp.logical_not(even), jnp.logical_not(empty)))
        def _():
            ref[...] = second[...]

    fill(low, od, ev, j == 0)
    fill(high, ev, od, j == last)


def ky_column(flow, n_ref, low, high, i):
    layers = [flow.load(low, i * 2 + l) for l in range(2)]
    layers += [flow.load(n_ref, (i + 2) * BY + j) for j in range(BY)]
    return layers + [flow.load(high, i * 2 + l) for l in range(2)]


def ky_flux(flow, aky, tgy, layers, i, f):
    w = flow.load(aky, i * (BY + 1) + f)
    return each(lambda g, w, *n: face(g > 0, w, *n), tgy, w, *layers[f : f + 4])


def stage_one_ky(np_ref, p_ref, aky, gy, mask, spec, ky_od, ky_ev, sp_ref, kx2_od, kx2_ev, x2, low, high):
    s, i, j, x_up, y_up = place()
    flow = Flow(x_up, y_up)
    ky_halos(ky_od, ky_ev, low, high)
    tgy = flow.load(gy, 0)

    def one_kx(i, carry):
        hold = each(lambda m: m == 1, flow.load(mask, 0))
        layers = ky_column(flow, np_ref, low, high, i)
        lower = ky_flux(flow, aky, tgy, layers, i, 0)
        for j in range(BY):
            upper = ky_flux(flow, aky, tgy, layers, i, j + 1)
            slab = i * BY + j
            p = flow.load(p_ref, slab)
            v = each(lambda m, p, u, v: jnp.where(m, spec[slab], p - (u - v)), hold, p, upper, lower)
            flow.store(sp_ref, slab + 2 * BY, v)
            lower = upper
        return carry

    lax.fori_loop(0, BX, one_kx, 0)
    cells = BY * BS
    base = 2 * cells
    low_rows, high_rows = pl.ds(base, base), pl.ds(base + (BX - 2) * cells, base)
    kx_even = i % 2 == 0

    @pl.when(kx_even)
    def _():
        kx2_od[...] = sp_ref[low_rows, :]
        kx2_ev[...] = sp_ref[high_rows, :]

    @pl.when(jnp.logical_not(kx_even))
    def _():
        kx2_od[...] = sp_ref[high_rows, :]
        kx2_ev[...] = sp_ref[low_rows, :]

    edge_rows(sp_ref, base, x_up, (x2,))


def stage_two(
    np_ref, sp_in, ax, ay, rkx, aky, gx, gy, edge, halo_speed, mask, spec, ky_od, ky_ev, kx_od, kx_ev, x2,
    out, sp_ref, fk, xnear, xflux, low, high, sem,
):
    s, i, j, x_up, y_up = place()
    flow = Flow(x_up, y_up)
    s_count, kx_count = lax.axis_size("space"), lax.axis_size("kx")
    kx_even = i % 2 == 0
    cells = BY * BS
    inner = pl.ds(2 * cells, BX * cells)
    copy = pltpu.make_async_copy(sp_in.at[inner], sp_ref.at[inner], sem)
    copy.start()
    ky_halos(ky_od, ky_ev, low, high)
    below = jnp.where(kx_even, kx_od[...], kx_ev[...])
    sp_ref[pl.ds(0, 2 * cells), :] = jnp.where(i == 0, 0.0, below)
    above = jnp.where(kx_even, kx_ev[...], kx_od[...])
    sp_ref[pl.ds((BX + 2) * cells, 2 * cells), :] = jnp.where(i == kx_count - 1, 0.0, above)
    none = jnp.logical_or(jnp.logical_and(x_up, s == 0), jnp.logical_and(jnp.logical_not(x_up), s == s_count - 1))
    near = jnp.where(none, 0.0, x2[pl.ds(0, 128), :])
    far = jnp.where(none, 0.0, x2[pl.ds(128, 128), :])
    xnear[...] = near
    xflux[...] = (3.0 * near - far) * halo_speed[...]
    copy.wait()

    tgx = flow.load(gx, 0)
    tgy = flow.load(gy, 0)

    def kx_flux(i, j):
        n = [flow.load(sp_ref, (i + d) * BY + j) for d in range(4)]
        r = flow.load(rkx, i * BY + j)
        return each(lambda g, r, *n: face(g > 0, r * g, *n), tgx, r, *n)

    for j in range(BY):
        flow.store(fk, j, kx_flux(0, j))

    def one_kx(i, carry):
        hold = each(lambda m: m == 1, flow.load(mask, 0))
        layers = ky_column(flow, sp_ref, low, high, i)
        lower_y = ky_flux(flow, aky, tgy, layers, i, 0)
        for j in range(BY):
            slab = i * BY + j
            n = layers[j + 2]
            total = space_change(flow, times3(n), n, ax, ay, i, j, edge, xnear, xflux)
            upper = kx_flux(i + 1, j)
            lower = flow.load(fk, j)
            flow.store(fk, j, upper)
            upper_y = ky_flux(flow, aky, tgy, layers, i, j + 1)
            first = flow.load(np_ref, slab + 2 * BY)
            v = each(
                lambda m, a, n, t, u, v, p, q: jnp.where(
                    m, spec[slab], 0.5 * ((a + n) - ((t + (u - v)) + (p - q)))
                ),
                hold, first, n, total, upper, lower, upper_y, lower_y,
            )
            flow.store(out, slab, v)
            lower_y = upper_y
        return carry

    lax.fori_loop(0, BX, one_kx, 0)


def call(kernel, outs, operands, spaces, scratch=(), alias=None, flops=0):
    whole = {
        "v": pl.BlockSpec(memory_space=pltpu.VMEM),
        "s": pl.BlockSpec(memory_space=pltpu.SMEM),
        "h": pl.BlockSpec(memory_space=pltpu.HBM),
    }
    return pl.pallas_call(
        kernel,
        out_shape=outs,
        in_specs=[whole[c] for c in spaces],
        out_specs=jax.tree.map(lambda _: whole["v"], outs),
        scratch_shapes=list(scratch),
        input_output_aliases=alias or {},
        compiler_params=pltpu.CompilerParams(vmem_limit_bytes=LIMIT),
        cost_estimate=pl.CostEstimate(flops=flops, bytes_accessed=0, transcendentals=0),
        name=kernel.__name__,
    )(*operands)


def wave_tables(kx_first, ky_first):
    kx = ((kx_first + jnp.arange(BX) - NKX // 2).astype(f32) + 0.5) * k_step
    kxf = (kx_first + jnp.arange(BX + 1) - NKX // 2).astype(f32) * k_step
    ky = ((ky_first + jnp.arange(BY) - NKY // 2).astype(f32) + 0.5) * k_step
    kyf = (ky_first + jnp.arange(BY + 1) - NKY // 2).astype(f32) * k_step

    def modulus(a, b):
        return jnp.sqrt(a[:, None] * a[:, None] + b[None, :] * b[None, :])

    k = modulus(kx, ky)
    c = (0.5 * X_SCALE) * jnp.sqrt(gravity / k) / k
    cx = c * jnp.abs(kx)[:, None]
    cy = c * jnp.abs(ky)[None, :]
    kf = modulus(kxf, ky)
    kg = modulus(kx, kyf)
    rows = [k, cx, cy, kf, (0.5 * K_SCALE) * jnp.sqrt(gravity * kf) * kf, kg, (0.5 * K_SCALE) * jnp.sqrt(gravity * kg) * kg]
    flat = [jnp.pad(r.reshape(-1), (0, 144 - r.size)) for r in rows]
    column = [jnp.broadcast_to(r.reshape(-1, 1), (BX * BY, 128)) for r in (k, cx)]
    return jnp.stack(flat), column[0], column[1]


def per_device(action, depth_cm, inflow_mask, inflow):
    kx_first = lax.axis_index("kx") * BX
    ky_first = lax.axis_index("ky") * BY
    spec = lax.dynamic_slice(inflow, (kx_first, ky_first), (BX, BY)).reshape(-1)
    tab, kcol, ccol = wave_tables(kx_first, ky_first)
    rows = BX * BY * BS
    padded = (BX + 4) * BY * BS
    ky_rows, kx_rows = BX * 2 * BS, 2 * BY * BS

    def v(*shape):
        return pltpu.VMEM(shape, f32)

    def swap(od, ev, axis):
        n = lax.axis_size(axis)
        return lax.ppermute(od, axis, odd_pairs(n)), lax.ppermute(ev, axis, even_pairs(n))

    np4, ky_od, ky_ev, kx_od, kx_ev, x_od, x_ev = call(
        first_messages,
        (v(BX + 4, BY, BS, NY), v(BX, 2, BS, NY), v(BX, 2, BS, NY), v(2, BY, BS, NY), v(2, BY, BS, NY), v(264, NY), v(264, NY)),
        (action, depth_cm),
        "hv",
        [pltpu.SemaphoreType.DMA((5,))],
    )
    ky_od, ky_ev = swap(ky_od, ky_ev, "ky")
    kx_od, kx_ev = swap(kx_od, kx_ev, "kx")
    x_od, x_ev = swap(x_od, x_ev, "space")
    ax, ay, rkx, aky, gy, geo = call(
        speeds,
        (v(rows, NY), v(rows, NY), v((BX + 1) * BY * BS, NY), v(BX * (BY + 1) * BS, NY), v(BS, NY), v(3, BS, NY)),
        (tab, depth_cm),
        "sv",
        flops=10_000_000,
    )
    np2 = np4.reshape(padded, NY)
    np2, part, gx, edge, halo_speed, ky2_od, ky2_ev = call(
        stage_one_space,
        (v(padded, NY), v(rows, NY), v(BS, NY), v(BX * BY, NY), v(BX * BY, NY), v(ky_rows, NY), v(ky_rows, NY)),
        (np2, ax, ay, rkx, aky, gy, geo, depth_cm, inflow_mask, spec, kcol, ccol,
         kx_od.reshape(kx_rows, NY), kx_ev.reshape(kx_rows, NY), x_od, x_ev),
        "vvvvvvvvvsvvvvvv",
        [v(BY * BS, NY), v(16, NY), v(BX * BY, NY), v(BX * BY, NY), pltpu.SemaphoreType.DMA((2,))],
        alias={0: 0},
    )
    ky2_od, ky2_ev = swap(ky2_od, ky2_ev, "ky")
    sp, kx2_od, kx2_ev, x2 = call(
        stage_one_ky,
        (v(padded, NY), v(kx_rows, NY), v(kx_rows, NY), v(256, NY)),
        (np2, part, aky, gy, inflow_mask, spec, ky_od.reshape(ky_rows, NY), ky_ev.reshape(ky_rows, NY)),
        "vvvvvsvv",
        [v(ky_rows, NY), v(ky_rows, NY)],
    )
    kx2_od, kx2_ev = swap(kx2_od, kx2_ev, "kx")
    n_space, n_kx = lax.axis_size("space"), lax.axis_size("kx")
    ring = []
    for a in range(n_space):
        for b in range(n_kx):
            to = (a + (1 if b >= n_kx // 2 else -1)) % n_space
            ring.append((a * n_kx + b, to * n_kx + b))
    x2 = lax.ppermute(x2, ("space", "kx"), ring)
    out = call(
        stage_two,
        jax.ShapeDtypeStruct((rows, NY), f32),
        (np2, sp, ax, ay, rkx, aky, gx, gy, edge, halo_speed, inflow_mask, spec,
         ky2_od, ky2_ev, kx2_od, kx2_ev, x2),
        "vvvvvvvvvvvsvvvvv",
        [v(padded, NY), v(BY * BS, NY), v(BX * BY, NY), v(BX * BY, NY), v(ky_rows, NY), v(ky_rows, NY), pltpu.SemaphoreType.DMA],
    )
    return out.reshape(BX, BY, BS, NY)


def solution(mesh):
    in_specs = (P("kx", "ky", "space", None), P("space", None), P("space", None), P())
    out_specs = P("kx", "ky", "space", None)
    return jax.shard_map(
        per_device, mesh=mesh, in_specs=in_specs, out_specs=out_specs, check_vma=False
    )
```

```python
import jax
import jax.numpy as jnp
from jax import lax
from jax.experimental import pallas as pl
from jax.experimental.pallas import tpu as pltpu
from jax.sharding import PartitionSpec as P

NKX = 64
NKY = 64

gravity = 9.81
spacing = 4.0
k_step = 0.04
time_step = 0.2

BX, BY, BS, NY = 16, 8, 16, 256
T = 4
f32 = jnp.float32
LIMIT = 8 * 2**20
EDGES = (0, 1, BY - 2, BY - 1)
MIDDLE = tuple(range(2, BY - 2))

X_SCALE = time_step / spacing * 0.5
K_SCALE = time_step / k_step * 0.5


def even_pairs(count):
    return [(i, i ^ 1) for i in range(count)]


def odd_pairs(count):
    pairs = []
    for i in range(1, count, 2):
        pairs += [(i, (i + 1) % count), ((i + 1) % count, i)]
    return pairs


def place():
    s, i, j = lax.axis_index("space"), lax.axis_index("kx"), lax.axis_index("ky")
    return s, i, j, i >= lax.axis_size("kx") // 2, j >= lax.axis_size("ky") // 2


def is_even(i):
    return i % 2 == 0


class Flow:
    def __init__(self):
        _, _, _, x_up, y_up = place()
        x0 = jnp.where(x_up, 0, 8)
        y0 = jnp.where(y_up, 0, 128)
        self.x_up = x_up
        self.x = (pl.multiple_of(x0, 8), pl.multiple_of(8 - x0, 8))
        self.y = (pl.multiple_of(y0, 128), pl.multiple_of(128 - y0, 128))
        self.x_roll = jnp.where(x_up, 1, 7)
        self.y_roll = jnp.where(y_up, 1, 127)
        self.rows = lax.broadcasted_iota(jnp.int32, (8, 128), 0)
        lanes = lax.broadcasted_iota(jnp.int32, (8, 128), 1)
        self.x_first = self.rows == jnp.where(x_up, 0, 7)
        self.x_last = self.rows == jnp.where(x_up, 7, 0)
        self.y_first = lanes == jnp.where(y_up, 0, 127)

    def natural(self, a, b):
        return pl.ds(self.x[a], 8), pl.ds(self.y[b], 128)

    def before_x(self, tiles, b, halo):
        first, second = (pltpu.roll(tiles[a][b], self.x_roll, 0) for a in range(2))
        return [jnp.where(self.x_first, halo, first), jnp.where(self.x_first, first, second)]

    def before_y(self, tiles, a):
        first, second = (pltpu.roll(tiles[a][b], self.y_roll, 1) for b in range(2))
        return [jnp.where(self.y_first, 0.0, first), jnp.where(self.y_first, first, second)]

    def edge_rows(self, tiles):
        out = []
        for up, down in ((7, 0), (6, 1)):
            rows = None
            for j in range(BY):
                shift = jnp.where(self.x_up, (j - up) % 8, (j - down) % 8)
                turned = pltpu.roll(tiles[j], shift, 0)
                rows = turned if rows is None else jnp.where(self.rows == j, turned, rows)
            out.append(rows)
        return out


def load(ref, slab):
    return [[ref[slab * T + 2 * a + b] for b in range(2)] for a in range(2)]


def store(ref, slab, tiles):
    for a in range(2):
        for b in range(2):
            ref[slab * T + 2 * a + b] = tiles[a][b]


def each(fn, *grids):
    return [[fn(*(g[a][b] for g in grids)) for b in range(2)] for a in range(2)]


def row(ref, i, j, b):
    return jnp.broadcast_to(ref[i * 2 + b][j : j + 1, :], (8, 128))


class Copies:
    def __init__(self, sems):
        self.sems, self.started = sems, []

    def start(self, src, dst):
        c = pltpu.make_async_copy(src, dst, self.sems.at[len(self.started)])
        c.start()
        self.started.append(c)

    def wait(self):
        for c in self.started:
            c.wait()


def first_messages(a_ref, depth, np_ref, ky_od, ky_ev, kx_od, kx_ev, x_od, x_ev, sems):
    s, i, j, x_up, _ = place()
    flow = Flow()
    copies = Copies(sems)
    tiles = [(a, b) for a in range(2) for b in range(2)]

    for a, b in tiles:
        x, y = flow.natural(a, b)
        copies.start(a_ref.at[:, pl.ds(jnp.where(is_even(j), 0, BY - 2), 2), x, y], ky_od.at[:, :, 2 * a + b])
        copies.start(a_ref.at[:, pl.ds(jnp.where(is_even(j), BY - 2, 0), 2), x, y], ky_ev.at[:, :, 2 * a + b])
    for a, b in tiles:
        x, y = flow.natural(a, b)
        copies.start(a_ref.at[:, :, x, y], np_ref.at[pl.ds(2, BX), :, 2 * a + b])
    for a, b in tiles:
        x, y = flow.natural(a, b)
        copies.start(a_ref.at[pl.ds(jnp.where(is_even(i), 0, BX - 2), 2), :, x, y], kx_od.at[:, :, 2 * a + b])
        copies.start(a_ref.at[pl.ds(jnp.where(is_even(i), BX - 2, 0), 2), :, x, y], kx_ev.at[:, :, 2 * a + b])
    for b in range(2):
        y = pl.ds(flow.y[b], 128)
        low = jnp.broadcast_to(depth[0:1, y].astype(f32), (8, 128))
        high = jnp.broadcast_to(depth[BS - 1 : BS, y].astype(f32), (8, 128))
        x_od[4 * BX + b] = jnp.where(is_even(s), low, high)
        x_ev[4 * BX + b] = jnp.where(is_even(s), high, low)
    copies.wait()

    def one_kx(i, carry):
        for b in range(2):
            rows = flow.edge_rows([np_ref[i + 2, j, 2 + b] for j in range(BY)])
            for l in range(2):
                x_od[l * 2 * BX + i * 2 + b] = rows[l]
                x_ev[l * 2 * BX + i * 2 + b] = rows[l]
        return carry

    lax.fori_loop(0, BX, one_kx, 0)


def shifted(h, axis, up):
    size = h.shape[axis]
    place_of = lax.broadcasted_iota(jnp.int32, h.shape, axis)
    if up:
        return jnp.where(place_of == size - 1, h, pltpu.roll(h, size - 1, axis))
    return jnp.where(place_of == 0, h, pltpu.roll(h, 1, axis))


def centre(first, i):
    return ((first + i - NKX // 2).astype(f32) + 0.5) * k_step


def lower_face(first, i):
    return (first + i - NKX // 2).astype(f32) * k_step


def wave(kx, ky):
    square = jnp.broadcast_to(kx * kx + ky * ky, (8, 128))
    inverse = lax.rsqrt(square)
    return square * inverse, inverse


def group_factor(k, inverse):
    return (0.5 * X_SCALE * gravity**0.5) * inverse * (inverse * jnp.sqrt(k))


def refract_factor(k):
    return (0.5 * K_SCALE * gravity**0.5) * k * jnp.sqrt(k)


def group(k, c, h):
    kh = k * h
    t = jnp.tanh(kh)
    return c * ((t + kh * (1.0 - t * t)) * lax.rsqrt(t))


def refract(k, c, h):
    t = jnp.tanh(k * h)
    return c * ((1.0 - t * t) * lax.rsqrt(t))


def speeds(depth, mask, ax, ay, rkx, aky, gy, heights, hold, geo):
    _, kx_place, ky_place, x_up, y_up = place()
    flow = Flow()
    kx_first, ky_first = kx_place * BX, ky_place * BY
    h = depth[...].astype(f32) * 0.01
    heights[...] = h
    y_next, y_last = shifted(h, 1, True), shifted(h, 1, False)
    hx = 0.5 * (h + jnp.where(x_up, shifted(h, 0, True), shifted(h, 0, False)))
    hy = 0.5 * (h + jnp.where(y_up, y_next, y_last))
    slope = (y_last - y_next) * (1.0 / (2.0 * spacing))
    x_flip, y_flip = jnp.where(x_up, 0, 1), jnp.where(y_up, 0, 1)
    for a in range(2):
        for b in range(2):
            at = (a ^ x_flip) * 2 + (b ^ y_flip)
            part = (slice(8 * a, 8 * a + 8), slice(128 * b, 128 * b + 128))
            gy[at] = slope[part]
            hold[at] = mask[part]
            geo[at] = h[part]
            geo[T + at] = hx[part]
            geo[2 * T + at] = hy[part]

    def kx_faces(i, j):
        k, _ = wave(lower_face(kx_first, i), centre(ky_first, j))
        c = refract_factor(k)
        store(rkx, i * BY + j, each(lambda h: refract(k, c, h), load(geo, 0)))

    def one_kx(i, carry):
        kx = centre(kx_first, i)
        for j in range(BY):
            ky = centre(ky_first, j)
            k, inverse = wave(kx, ky)
            c = group_factor(k, inverse)
            cx, cy = c * jnp.abs(kx), c * jnp.abs(ky)
            store(ax, i * BY + j, each(lambda h: group(k, cx, h), load(geo, 1)))
            store(ay, i * BY + j, each(lambda h: group(k, cy, h), load(geo, 2)))
            kx_faces(i, j)
        for j in range(BY + 1):
            k, _ = wave(kx, lower_face(ky_first, j))
            c = refract_factor(k)
            store(aky, i * (BY + 1) + j, each(lambda h, g: refract(k, c, h) * g, load(geo, 0), load(gy, 0)))
        return carry

    lax.fori_loop(0, BX, one_kx, 0)
    for j in range(BY):
        kx_faces(BX, j)


def space_change(flow, n, ax_ref, ay_ref, i, j, edge, halo_row, halo_flux):
    slab = i * BY + j
    ax, ay = load(ax_ref, slab), load(ay_ref, slab)
    n3 = each(lambda v: 3.0 * v, n)
    total = [[None, None], [None, None]]
    for b in range(2):
        ax[1][b] = jnp.where(flow.x_last, row(edge, i, j, b), ax[1][b])
        before = flow.before_x(n, b, row(halo_row, i, j, b))
        out = [[ax[a][b] * (n3[a][b] - before[a])] * 2 for a in range(2)]
        into = flow.before_x(out, b, row(halo_flux, i, j, b))
        for a in range(2):
            total[a][b] = out[a][b] - into[a]
    for a in range(2):
        before = flow.before_y(n, a)
        out = [ay[a][b] * (n3[a][b] - before[b]) for b in range(2)]
        into = flow.before_y([out, out], 0)
        for b in range(2):
            total[a][b] = total[a][b] + (out[b] - into[b])
    return total


def face(up, speed, n_2, n_1, n1, n2):
    near = jnp.where(up, n_1, n1)
    far = jnp.where(up, n_2, n2)
    return speed * (3.0 * near - far)


def kx_flux(gx, rkx, n_ref, i, j):
    n = [load(n_ref, (i + d) * BY + j) for d in range(4)]
    return each(lambda g, r, *n: face(g > 0, r * g, *n), gx, load(rkx, i * BY + j), *n)


def ky_flux(gy, aky, layers, i, f):
    return each(lambda g, w, *n: face(g > 0, w, *n), gy, load(aky, i * (BY + 1) + f), *layers[f : f + 4])


def halos(copies, od, ev, low, high, axis, flip):
    p, last = lax.axis_index(axis), lax.axis_size(axis) - 1
    middle = (last + 1) // 2
    todo = []
    for dst, src_even, src_odd, empty, turned in (
        (low, od, ev, p == 0, p == middle),
        (high, ev, od, p == last, p == middle - 1),
    ):
        full = jnp.logical_not(empty)

        @pl.when(empty)
        def _():
            dst[...] = jnp.zeros(dst.shape, f32)

        for t in range(T):
            at = jnp.where(turned, t ^ flip, t)
            sem = copies.sems.at[len(todo)]
            pair = [pltpu.make_async_copy(src.at[:, :, at], dst.at[:, :, t], sem) for src in (src_even, src_odd)]
            pl.when(jnp.logical_and(full, is_even(p)))(pair[0].start)
            pl.when(jnp.logical_and(full, jnp.logical_not(is_even(p))))(pair[1].start)
            todo.append((full, pair[0]))

    def wait():
        for full, c in todo:
            pl.when(full)(c.wait)

    return wait


def no_inflow(x_up):
    s = lax.axis_index("space")
    return s == jnp.where(x_up, 0, lax.axis_size("space") - 1)


def stage_one_edges(
    np_in, ax, ay, rkx, aky, heights, hold_ref, spec, kx_od, kx_ev, x_od, x_ev,
    np_ref, p_ref, gx, edge, halo_speed, xnear, xflux, ky2_od, ky2_ev, fk, hrow, sems,
):
    s, kx_place, ky_place, x_up, y_up = place()
    flow = Flow()
    slabs = (BX + 4) * BY
    kx_first, ky_first = kx_place * BX, ky_place * BY
    np5 = np_ref.reshape(BX + 4, BY, T, 8, 128)
    wait = halos(Copies(sems), kx_od, kx_ev, np5.at[pl.ds(0, 2)], np5.at[pl.ds(BX + 2, 2)], "kx", 2)
    h = heights[...]
    x_flip, y_flip = jnp.where(x_up, 0, 1), jnp.where(y_up, 0, 1)
    none = no_inflow(x_up)
    use_od = is_even(s) == x_up
    for b in range(2):
        y = b ^ y_flip
        at = 4 * BX + y
        mine = h[:, 128 * b : 128 * b + 128]
        od, ev = x_od[at][0:1, :] * 0.01, x_ev[at][0:1, :] * 0.01
        low = jnp.where(s == 0, mine[0:1, :], jnp.where(is_even(s), od, ev))
        high = jnp.where(s == lax.axis_size("space") - 1, mine[BS - 1 : BS, :], jnp.where(is_even(s), ev, od))
        place_of = lax.broadcasted_iota(jnp.int32, (BS, 128), 0)
        before = jnp.where(place_of == 0, low, pltpu.roll(mine, 1, 0))
        after = jnp.where(place_of == BS - 1, high, pltpu.roll(mine, BS - 1, 0))
        slope = (before - after) * (1.0 / (2.0 * spacing))
        for a in range(2):
            gx[(a ^ x_flip) * 2 + y] = slope[8 * a : 8 * a + 8, :]
        face_low = jnp.broadcast_to(0.5 * (low + mine[0:1, :]), (8, 128))
        face_high = jnp.broadcast_to(0.5 * (high + mine[BS - 1 : BS, :]), (8, 128))
        hrow[y] = jnp.where(x_up, face_high, face_low)
        hrow[2 + y] = jnp.where(x_up, face_low, face_high)
    ky = ((ky_first + flow.rows - NKY // 2).astype(f32) + 0.5) * k_step

    def edges(i, carry):
        kx = centre(kx_first, i)
        k, inverse = wave(kx, ky)
        c = group_factor(k, inverse) * jnp.abs(kx)
        for b in range(2):
            at = i * 2 + b
            near = jnp.where(use_od, x_od[at], x_ev[at])
            far = jnp.where(use_od, x_od[2 * BX + at], x_ev[2 * BX + at])
            edge[at] = group(k, c, hrow[b])
            speed = group(k, c, hrow[2 + b])
            halo_speed[at] = speed
            xnear[at] = jnp.where(none, 0.0, near)
            xflux[at] = jnp.where(none, 0.0, speed * (3.0 * near - far))
        return carry

    lax.fori_loop(0, BX, edges, 0)
    wait()

    g = load(gx, 0)
    for e, j in enumerate(EDGES):
        store(fk, e, kx_flux(g, rkx, np_ref, 0, j))

    def one_kx(i, carry):
        hold = each(lambda m: m == 1, load(hold_ref, 0))
        g = load(gx, 0)
        part = {}
        for e, j in enumerate(EDGES):
            n = load(np_ref, (i + 2) * BY + j)
            total = space_change(flow, n, ax, ay, i, j, edge, xnear, xflux)
            upper = kx_flux(g, rkx, np_ref, i + 1, j)
            lower = load(fk, e)
            store(fk, e, upper)
            part[j] = each(lambda n, t, u, v: n - (t + (u - v)), n, total, upper, lower)
            store(p_ref, i * len(EDGES) + e, part[j])

        def own(f, a, b):
            w = load(aky, i * (BY + 1) + f)
            a, b = (load(np_ref, (i + 2) * BY + j) for j in (a, b))
            return each(lambda w, a, b: w * (3.0 * a - b), w, a, b)

        def send(j, low, high, l, to):
            v = each(
                lambda m, p, u, v: jnp.where(m, spec[kx_first + i, ky_first + j], p - (u - v)), hold, part[j], high, low
            )
            for ref, here in ((ky2_od, to), (ky2_ev, jnp.logical_not(to))):
                @pl.when(here)
                def _():
                    store(ref, i * 2 + l, v)

        f = [own(0, 0, 1), own(1, 1, 2), own(2, 2, 3)]
        send(0, f[0], f[1], 0, is_even(ky_place))
        send(1, f[1], f[2], 1, is_even(ky_place))
        f = [own(BY - 2, BY - 3, BY - 4), own(BY - 1, BY - 2, BY - 3), own(BY, BY - 1, BY - 2)]
        send(BY - 2, f[0], f[1], 0, jnp.logical_not(is_even(ky_place)))
        send(BY - 1, f[1], f[2], 1, jnp.logical_not(is_even(ky_place)))
        return carry

    lax.fori_loop(0, BX, one_kx, 0)


def ky_column(n_ref, low, high, i):
    layers = [load(low, i * 2 + l) for l in range(2)]
    layers += [load(n_ref, (i + 2) * BY + j) for j in range(BY)]
    return layers + [load(high, i * 2 + l) for l in range(2)]


def stage_one_rest(
    np_ref, p_ref, ax, ay, rkx, aky, gx, gy, edge, xnear, xflux, hold_ref, spec, ky_od, ky_ev,
    sp_ref, kx2_od, kx2_ev, x2, fk, low, high, sems,
):
    s, kx_place, ky_place, x_up, y_up = place()
    flow = Flow()
    kx_first, ky_first = kx_place * BX, ky_place * BY
    wait = halos(
        Copies(sems), ky_od, ky_ev, low.reshape(BX, 2, T, 8, 128), high.reshape(BX, 2, T, 8, 128), "ky", 1
    )
    g = load(gx, 0)
    for e, j in enumerate(MIDDLE):
        store(fk, e, kx_flux(g, rkx, np_ref, 0, j))
    wait()

    def one_kx(i, carry):
        hold = each(lambda m: m == 1, load(hold_ref, 0))
        g, gk = load(gx, 0), load(gy, 0)
        layers = ky_column(np_ref, low, high, i)
        lower_y = ky_flux(gk, aky, layers, i, 0)
        last = [[], []]
        for j in range(BY):
            n = layers[j + 2]
            if j in EDGES:
                p = load(p_ref, i * len(EDGES) + EDGES.index(j))
            else:
                e = MIDDLE.index(j)
                total = space_change(flow, n, ax, ay, i, j, edge, xnear, xflux)
                upper = kx_flux(g, rkx, np_ref, i + 1, j)
                lower = load(fk, e)
                store(fk, e, upper)
                p = each(lambda n, t, u, v: n - (t + (u - v)), n, total, upper, lower)
            upper_y = ky_flux(gk, aky, layers, i, j + 1)
            v = each(
                lambda m, p, u, v: jnp.where(m, spec[kx_first + i, ky_first + j], p - (u - v)), hold, p, upper_y, lower_y
            )
            store(sp_ref, (i + 2) * BY + j, v)
            lower_y = upper_y
            for b in range(2):
                last[b].append(v[1][b])
        for b in range(2):
            rows = flow.edge_rows(last[b])
            for l in range(2):
                x2[l * 2 * BX + i * 2 + b] = rows[l]
        return carry

    lax.fori_loop(0, BX, one_kx, 0)
    size = 2 * BY * T
    copies = Copies(sems)
    copies.start(sp_ref.at[pl.ds(size + jnp.where(is_even(kx_place), 0, (BX - 2) * BY * T), size)], kx2_od)
    copies.start(sp_ref.at[pl.ds(size + jnp.where(is_even(kx_place), (BX - 2) * BY * T, 0), size)], kx2_ev)
    copies.wait()


def send_out(buffer, out, sems, i, layers, first):
    flow = Flow()
    todo = []
    for a in range(2):
        for b in range(2):
            x, y = flow.natural(a, b)
            t = 2 * a + b
            todo.append(
                pltpu.make_async_copy(
                    buffer.at[i, pl.ds(first, len(layers)), t],
                    out.at[i, pl.ds(layers[0], len(layers)), x, y],
                    sems.at[i, first, t],
                )
            )
    return todo


def stage_two_most(
    np_ref, sp_in, ax, ay, rkx, aky, gx, gy, edge, halo_speed, hold_ref, spec, kx_od, kx_ev, x2,
    sp_ref, q_ref, out, fk, xnear, xflux, done, sems, out_sems,
):
    s, kx_place, ky_place, x_up, y_up = place()
    flow = Flow()
    kx_first, ky_first = kx_place * BX, ky_place * BY
    sp5 = sp_ref.reshape(BX + 4, BY, T, 8, 128)
    wait = halos(Copies(sems), kx_od, kx_ev, sp5.at[pl.ds(0, 2)], sp5.at[pl.ds(BX + 2, 2)], "kx", 2)
    none = no_inflow(x_up)
    near = jnp.where(none, 0.0, x2[pl.ds(0, 2 * BX)])
    xnear[...] = near
    xflux[...] = (3.0 * near - jnp.where(none, 0.0, x2[pl.ds(2 * BX, 2 * BX)])) * halo_speed[...]
    wait()
    g = load(gx, 0)
    for j in range(BY):
        store(fk, j, kx_flux(g, rkx, sp_ref, 0, j))

    def one_kx(i, carry):
        hold = each(lambda m: m == 1, load(hold_ref, 0))
        g, gk = load(gx, 0), load(gy, 0)
        layers = [None, None] + [load(sp_ref, (i + 2) * BY + j) for j in range(BY)]
        lower_y = None
        for j in range(BY):
            n = layers[j + 2]
            total = space_change(flow, n, ax, ay, i, j, edge, xnear, xflux)
            upper = kx_flux(g, rkx, sp_ref, i + 1, j)
            lower = load(fk, j)
            store(fk, j, upper)
            first = load(np_ref, (i + 2) * BY + j)
            upper_y = ky_flux(gk, aky, layers, i, j + 1) if 2 <= j + 1 <= BY - 2 else None
            total = each(lambda t, u, v: t + (u - v), total, upper, lower)
            if upper_y is not None:
                total = each(lambda t, u: t + u, total, upper_y)
            if lower_y is not None:
                total = each(lambda t, u: t - u, total, lower_y)
            v = each(lambda a, n, t: 0.5 * ((a + n) - t), first, n, total)
            if j in EDGES:
                store(q_ref, i * len(EDGES) + EDGES.index(j), v)
            else:
                v = each(lambda m, v: jnp.where(m, spec[kx_first + i, ky_first + j], v), hold, v)
                for a in range(2):
                    for b in range(2):
                        done[i, MIDDLE.index(j), 2 * a + b] = v[a][b]
            lower_y = upper_y
        for c in send_out(done, out, out_sems, i, MIDDLE, 0):
            c.start()
        return carry

    lax.fori_loop(0, BX, one_kx, 0)

    def finish(i, carry):
        for c in send_out(done, out, out_sems, i, MIDDLE, 0):
            c.wait()
        return carry

    lax.fori_loop(0, BX, finish, 0)


def stage_two_edges(sp_ref, q_ref, aky, gy, hold_ref, spec, ky_od, ky_ev, out_in, out, low, high, done, sems, out_sems):
    s, kx_place, ky_place, x_up, y_up = place()
    kx_first, ky_first = kx_place * BX, ky_place * BY
    halos(
        Copies(sems), ky_od, ky_ev, low.reshape(BX, 2, T, 8, 128), high.reshape(BX, 2, T, 8, 128), "ky", 1
    )()
    parts = ((EDGES[:2], 0), (EDGES[2:], 2))

    def one_kx(i, carry):
        hold = each(lambda m: m == 1, load(hold_ref, 0))
        gk = load(gy, 0)
        layers = ky_column(sp_ref, low, high, i)
        flux = {f: ky_flux(gk, aky, layers, i, f) for f in (0, 1, BY - 1, BY)}
        for e, j in enumerate(EDGES):
            q = load(q_ref, i * len(EDGES) + e)
            if j in flux:
                q = each(lambda q, v: q + 0.5 * v, q, flux[j])
            if j + 1 in flux:
                q = each(lambda q, u: q - 0.5 * u, q, flux[j + 1])
            v = each(lambda m, v: jnp.where(m, spec[kx_first + i, ky_first + j], v), hold, q)
            for a in range(2):
                for b in range(2):
                    done[i, e, 2 * a + b] = v[a][b]
        for layers_of, first in parts:
            for c in send_out(done, out, out_sems, i, layers_of, first):
                c.start()
        return carry

    lax.fori_loop(0, BX, one_kx, 0)

    def finish(i, carry):
        for layers_of, first in parts:
            for c in send_out(done, out, out_sems, i, layers_of, first):
                c.wait()
        return carry

    lax.fori_loop(0, BX, finish, 0)


def call(kernel, outs, operands, spaces, out_spaces, scratch=(), alias=None, flops=0):
    whole = {
        "v": pl.BlockSpec(memory_space=pltpu.VMEM),
        "s": pl.BlockSpec(memory_space=pltpu.SMEM),
        "h": pl.BlockSpec(memory_space=pltpu.HBM),
    }
    return pl.pallas_call(
        kernel,
        out_shape=tuple(outs),
        in_specs=[whole[c] for c in spaces],
        out_specs=tuple(whole[c] for c in out_spaces),
        scratch_shapes=list(scratch),
        input_output_aliases=alias or {},
        compiler_params=pltpu.CompilerParams(vmem_limit_bytes=LIMIT),
        cost_estimate=pl.CostEstimate(flops=flops, bytes_accessed=0, transcendentals=0),
        name=kernel.__name__,
    )(*operands)


def per_device(action, depth_cm, inflow_mask, inflow):
    slabs, padded = BX * BY * T, (BX + 4) * BY * T
    edge_slabs = BX * len(EDGES) * T

    def v(*shape):
        return pltpu.VMEM(shape + (8, 128), f32)

    def swap(od, ev, axis):
        n = lax.axis_size(axis)
        return lax.ppermute(od, axis, odd_pairs(n)), lax.ppermute(ev, axis, even_pairs(n))

    sem = pltpu.SemaphoreType.DMA
    ky_shape, kx_shape = (BX, 2, T), (2, BY, T)
    np5, ky_od, ky_ev, kx_od, kx_ev, x_od, x_ev = call(
        first_messages,
        (v(BX + 4, BY, T), v(*ky_shape), v(*ky_shape), v(*kx_shape), v(*kx_shape), v(4 * BX + 2), v(4 * BX + 2)),
        (action, depth_cm),
        "hv",
        "v" * 7,
        [sem((20,))],
    )
    ky_od, ky_ev = swap(ky_od, ky_ev, "ky")
    kx_od, kx_ev = swap(kx_od, kx_ev, "kx")
    x_od, x_ev = swap(x_od, x_ev, "space")
    ax, ay, rkx, aky, gy, heights, hold = call(
        speeds,
        (v(slabs), v(slabs), v((BX + 1) * BY * T), v(BX * (BY + 1) * T), v(T), pltpu.VMEM((BS, NY), f32),
         pltpu.VMEM((T, 8, 128), jnp.int32)),
        (depth_cm, inflow_mask),
        "vv",
        "v" * 7,
        [v(3 * T)],
        flops=10_000_000,
    )
    np3 = np5.reshape(padded, 8, 128)
    np3, part, gx, edge, halo_speed, xnear, xflux, ky2_od, ky2_ev = call(
        stage_one_edges,
        (v(padded), v(edge_slabs), v(T), v(2 * BX), v(2 * BX), v(2 * BX), v(2 * BX), v(BX * 2 * T), v(BX * 2 * T)),
        (np3, ax, ay, rkx, aky, heights, hold, inflow, kx_od, kx_ev, x_od, x_ev),
        "vvvvvvvsvvvv",
        "v" * 9,
        [v(len(EDGES) * T), v(4), sem((2 * T,))],
        alias={0: 0},
    )
    ky2_od, ky2_ev = swap(ky2_od, ky2_ev, "ky")
    sp, kx2_od, kx2_ev, x2 = call(
        stage_one_rest,
        (v(padded), v(2 * BY * T), v(2 * BY * T), v(4 * BX)),
        (np3, part, ax, ay, rkx, aky, gx, gy, edge, xnear, xflux, hold, inflow, ky_od, ky_ev),
        "vvvvvvvvvvvvsvv",
        "v" * 4,
        [v(len(MIDDLE) * T), v(BX * 2 * T), v(BX * 2 * T), sem((2 * T,))],
    )
    kx2_od, kx2_ev = swap(kx2_od, kx2_ev, "kx")
    n_space, n_kx = lax.axis_size("space"), lax.axis_size("kx")
    ring = []
    for a in range(n_space):
        for b in range(n_kx):
            to = (a + (1 if b >= n_kx // 2 else -1)) % n_space
            ring.append((a * n_kx + b, to * n_kx + b))
    x2 = lax.ppermute(x2, ("space", "kx"), ring)
    sp, q, out = call(
        stage_two_most,
        (v(padded), v(edge_slabs), jax.ShapeDtypeStruct(action.shape, f32)),
        (np3, sp, ax, ay, rkx, aky, gx, gy, edge, halo_speed, hold, inflow,
         kx2_od.reshape(*kx_shape, 8, 128), kx2_ev.reshape(*kx_shape, 8, 128), x2),
        "vvvvvvvvvvvsvvv",
        "vvh",
        [v(BY * T), v(2 * BX), v(2 * BX), v(BX, len(MIDDLE), T), sem((2 * T,)), sem((BX, 1, T))],
        alias={1: 0},
    )
    (out,) = call(
        stage_two_edges,
        (jax.ShapeDtypeStruct(action.shape, f32),),
        (sp, q, aky, gy, hold, inflow, ky2_od.reshape(*ky_shape, 8, 128), ky2_ev.reshape(*ky_shape, 8, 128), out),
        "vvvvvsvvh",
        "h",
        [v(BX * 2 * T), v(BX * 2 * T), v(BX, len(EDGES), T), sem((2 * T,)), sem((BX, 4, T))],
        alias={8: 0},
    )
    return out


def solution(mesh):
    in_specs = (P("kx", "ky", "space", None), P("space", None), P("space", None), P())
    out_specs = P("kx", "ky", "space", None)
    return jax.shard_map(
        per_device, mesh=mesh, in_specs=in_specs, out_specs=out_specs, check_vma=False
    )
```

```python
import jax
import jax.numpy as jnp
from jax import lax
from jax.experimental import pallas as pl
from jax.experimental.pallas import tpu as pltpu
from jax.sharding import PartitionSpec as P

NKX = 64
NKY = 64

gravity = 9.81
spacing = 4.0
k_step = 0.04
time_step = 0.2

BX, BY, BS, NY = 16, 8, 16, 256
T = 4
f32 = jnp.float32
LIMIT = 8 * 2**20
FIRST_LIMIT = 54 * 2**20
EDGES = (0, 1, BY - 2, BY - 1)
MIDDLE = tuple(range(2, BY - 2))

X_SCALE = time_step / spacing * 0.5
K_SCALE = time_step / k_step * 0.5


AXES = ("space", "kx", "ky")


def swaps(sizes, axis, odd, spare):
    pairs = []
    for n in range(sizes[0] * sizes[1] * sizes[2]):
        at = [n // (sizes[1] * sizes[2]), n // sizes[2] % sizes[1], n % sizes[2]]
        other = ((at[axis] + odd) ^ 1) - odd
        if 0 <= other < sizes[axis]:
            at[axis] = other
        else:
            at[spare] ^= 1
        pairs.append((n, (at[0] * sizes[1] + at[1]) * sizes[2] + at[2]))
    return pairs


def ring(sizes):
    pairs = []
    for a in range(sizes[0]):
        for b in range(sizes[1]):
            to = (a + (1 if b >= sizes[1] // 2 else -1)) % sizes[0]
            pairs.append((a * sizes[1] + b, to * sizes[1] + b))
    return pairs


def place():
    s, i, j = lax.axis_index("space"), lax.axis_index("kx"), lax.axis_index("ky")
    return s, i, j, i >= lax.axis_size("kx") // 2, j >= lax.axis_size("ky") // 2


def is_even(i):
    return i % 2 == 0


class Flow:
    def __init__(self):
        _, _, _, x_up, y_up = place()
        x0 = jnp.where(x_up, 0, 8)
        y0 = jnp.where(y_up, 0, 128)
        self.x_up = x_up
        self.x = (pl.multiple_of(x0, 8), pl.multiple_of(8 - x0, 8))
        self.y = (pl.multiple_of(y0, 128), pl.multiple_of(128 - y0, 128))
        self.x_roll = jnp.where(x_up, 1, 7)
        self.y_roll = jnp.where(y_up, 1, 127)
        self.rows = lax.broadcasted_iota(jnp.int32, (8, 128), 0)
        lanes = lax.broadcasted_iota(jnp.int32, (8, 128), 1)
        self.x_first = self.rows == jnp.where(x_up, 0, 7)
        self.x_last = self.rows == jnp.where(x_up, 7, 0)
        self.y_first = lanes == jnp.where(y_up, 0, 127)

    def natural(self, a, b):
        return pl.ds(self.x[a], 8), pl.ds(self.y[b], 128)

    def before_x(self, tiles, b, halo):
        first, second = (pltpu.roll(tiles[a][b], self.x_roll, 0) for a in range(2))
        return [jnp.where(self.x_first, halo, first), jnp.where(self.x_first, first, second)]

    def before_y(self, tiles, a):
        first, second = (pltpu.roll(tiles[a][b], self.y_roll, 1) for b in range(2))
        return [jnp.where(self.y_first, 0.0, first), jnp.where(self.y_first, first, second)]

    def edge_rows(self, tiles):
        out = []
        for up, down in ((7, 0), (6, 1)):
            rows = None
            for j in range(BY):
                shift = jnp.where(self.x_up, (j - up) % 8, (j - down) % 8)
                turned = pltpu.roll(tiles[j], shift, 0)
                rows = turned if rows is None else jnp.where(self.rows == j, turned, rows)
            out.append(rows)
        return out


def load(ref, slab):
    return [[ref[slab * T + 2 * a + b] for b in range(2)] for a in range(2)]


def store(ref, slab, tiles):
    for a in range(2):
        for b in range(2):
            ref[slab * T + 2 * a + b] = tiles[a][b]


def each(fn, *grids):
    return [[fn(*(g[a][b] for g in grids)) for b in range(2)] for a in range(2)]


def row(ref, i, j, b):
    return jnp.broadcast_to(ref[i * 2 + b][j : j + 1, :], (8, 128))


def wait_all(dst, sem):
    pltpu.make_async_copy(dst, dst, sem).wait()


def shifted(h, axis, up):
    size = h.shape[axis]
    place_of = lax.broadcasted_iota(jnp.int32, h.shape, axis)
    if up:
        return jnp.where(place_of == size - 1, h, pltpu.roll(h, size - 1, axis))
    return jnp.where(place_of == 0, h, pltpu.roll(h, 1, axis))


def centre(first, i):
    return ((first + i - NKX // 2).astype(f32) + 0.5) * k_step


def lower_face(first, i):
    return (first + i - NKX // 2).astype(f32) * k_step


def wave(kx, ky):
    square = jnp.broadcast_to(kx * kx + ky * ky, (8, 128))
    inverse = lax.rsqrt(square)
    return square * inverse, inverse


def group_factor(k, inverse):
    return (0.5 * X_SCALE * gravity**0.5) * inverse * (inverse * jnp.sqrt(k))


def refract_factor(k):
    return (0.5 * K_SCALE * gravity**0.5) * k * jnp.sqrt(k)


def group(k, c, h):
    kh = k * h
    t = jnp.tanh(kh)
    return c * ((t + kh * (1.0 - t * t)) * lax.rsqrt(t))


def refract(k, c, h):
    t = jnp.tanh(k * h)
    return c * ((1.0 - t * t) * lax.rsqrt(t))


def first_messages(
    a_ref, depth_ref, mask_ref, inflow_ref,
    np_ref, ky_od, ky_ev, kx_od, kx_ev, x_od, x_ev, depth, mask, inflow, ay, geo, sems,
):
    s, i, j, x_up, y_up = place()
    flow = Flow()
    own = np_ref.at[pl.ds(2, BX)]
    small = [
        pltpu.make_async_copy(src, dst, sems.at[n])
        for n, (src, dst) in enumerate(((depth_ref, depth), (mask_ref, mask), (inflow_ref, inflow)))
    ]
    for c in small:
        c.start()
    for a in range(2):
        for b in range(2):
            x, y = flow.natural(a, b)
            pltpu.make_async_copy(a_ref.at[:, :, x, y], own.at[:, :, 2 * a + b], sems.at[3]).start()
    for c in small:
        c.wait()
    h = depth[...].astype(f32) * 0.01
    hy = 0.5 * (h + jnp.where(y_up, shifted(h, 1, True), shifted(h, 1, False)))
    x_flip, y_flip = jnp.where(x_up, 0, 1), jnp.where(y_up, 0, 1)
    for a in range(2):
        for b in range(2):
            geo[(a ^ x_flip) * 2 + (b ^ y_flip)] = hy[8 * a : 8 * a + 8, 128 * b : 128 * b + 128]
    kx_first, ky_first = i * BX, j * BY

    def y_speeds(i, carry):
        kx = centre(kx_first, i)
        for j in range(BY):
            ky = centre(ky_first, j)
            k, inverse = wave(kx, ky)
            c = group_factor(k, inverse) * jnp.abs(ky)
            store(ay, i * BY + j, each(lambda h: group(k, c, h), load(geo, 0)))
        return carry

    lax.fori_loop(0, BX, y_speeds, 0)
    wait_all(own, sems.at[3])
    low = {"kx": jnp.where(is_even(i), 0, BX - 2), "ky": jnp.where(is_even(j), 0, BY - 2)}
    high = {"kx": jnp.where(is_even(i), BX - 2, 0), "ky": jnp.where(is_even(j), BY - 2, 0)}
    messages = [
        pltpu.make_async_copy(src, dst, sems.at[n])
        for n, (src, dst) in enumerate(
            (
                (own.at[:, pl.ds(low["ky"], 2)], ky_od),
                (own.at[:, pl.ds(high["ky"], 2)], ky_ev),
                (own.at[pl.ds(low["kx"], 2)], kx_od),
                (own.at[pl.ds(high["kx"], 2)], kx_ev),
            ),
            4,
        )
    ]
    for c in messages:
        c.start()
    for b in range(2):
        y = pl.ds(flow.y[b], 128)
        first = jnp.broadcast_to(depth[0:1, y].astype(f32), (8, 128))
        last = jnp.broadcast_to(depth[BS - 1 : BS, y].astype(f32), (8, 128))
        x_od[4 * BX + b] = jnp.where(is_even(s), first, last)
        x_ev[4 * BX + b] = jnp.where(is_even(s), last, first)

    def one_kx(i, carry):
        for b in range(2):
            rows = flow.edge_rows([np_ref[i + 2, j, 2 + b] for j in range(BY)])
            for l in range(2):
                x_od[l * 2 * BX + i * 2 + b] = rows[l]
                x_ev[l * 2 * BX + i * 2 + b] = rows[l]
        return carry

    lax.fori_loop(0, BX, one_kx, 0)
    for c in messages:
        c.wait()


def speeds(depth, mask, inflow, ax, rkx, aky, gy, heights, hold, spec, geo):
    _, kx_place, ky_place, x_up, y_up = place()
    flow = Flow()
    kx_first, ky_first = kx_place * BX, ky_place * BY
    h = depth[...].astype(f32) * 0.01
    heights[...] = h
    y_next, y_last = shifted(h, 1, True), shifted(h, 1, False)
    hx = 0.5 * (h + jnp.where(x_up, shifted(h, 0, True), shifted(h, 0, False)))
    slope = (y_last - y_next) * (1.0 / (2.0 * spacing))
    x_flip, y_flip = jnp.where(x_up, 0, 1), jnp.where(y_up, 0, 1)
    for a in range(2):
        for b in range(2):
            at = (a ^ x_flip) * 2 + (b ^ y_flip)
            part = (slice(8 * a, 8 * a + 8), slice(128 * b, 128 * b + 128))
            gy[at] = slope[part]
            hold[at] = mask[part]
            geo[at] = h[part]
            geo[T + at] = hx[part]

    lanes = lax.broadcasted_iota(jnp.int32, (8, NKY), 1)
    for half in range(BX // 8):
        rows = inflow[pl.ds(pl.multiple_of(kx_first + 8 * half, 8), 8), :]
        for j in range(BY):
            column = jnp.sum(jnp.where(lanes == ky_first + j, rows, 0.0), axis=1, keepdims=True)
            column = jnp.broadcast_to(column, (8, 128))
            for r in range(8):
                spec[(8 * half + r) * BY + j] = jnp.broadcast_to(column[r : r + 1, :], (8, 128))

    def kx_faces(i, j):
        k, _ = wave(lower_face(kx_first, i), centre(ky_first, j))
        c = refract_factor(k)
        store(rkx, i * BY + j, each(lambda h: refract(k, c, h), load(geo, 0)))

    def one_kx(i, carry):
        kx = centre(kx_first, i)
        for j in range(BY):
            ky = centre(ky_first, j)
            k, inverse = wave(kx, ky)
            c = group_factor(k, inverse)
            cx = c * jnp.abs(kx)
            store(ax, i * BY + j, each(lambda h: group(k, cx, h), load(geo, 1)))
            kx_faces(i, j)
        for j in range(BY + 1):
            k, _ = wave(kx, lower_face(ky_first, j))
            c = refract_factor(k)
            store(aky, i * (BY + 1) + j, each(lambda h, g: refract(k, c, h) * g, load(geo, 0), load(gy, 0)))
        return carry

    lax.fori_loop(0, BX, one_kx, 0)
    for j in range(BY):
        kx_faces(BX, j)


def space_change(flow, n, ax_ref, ay_ref, i, j, edge, halo_row, halo_flux):
    slab = i * BY + j
    ax, ay = load(ax_ref, slab), load(ay_ref, slab)
    n3 = each(lambda v: 3.0 * v, n)
    total = [[None, None], [None, None]]
    for b in range(2):
        ax[1][b] = jnp.where(flow.x_last, row(edge, i, j, b), ax[1][b])
        before = flow.before_x(n, b, 0.0 if halo_row is None else row(halo_row, i, j, b))
        out = [[ax[a][b] * (n3[a][b] - before[a])] * 2 for a in range(2)]
        into = flow.before_x(out, b, 0.0 if halo_flux is None else row(halo_flux, i, j, b))
        for a in range(2):
            total[a][b] = out[a][b] - into[a]
    for a in range(2):
        before = flow.before_y(n, a)
        out = [ay[a][b] * (n3[a][b] - before[b]) for b in range(2)]
        into = flow.before_y([out, out], 0)
        for b in range(2):
            total[a][b] = total[a][b] + (out[b] - into[b])
    return total


def face(up, speed, n_2, n_1, n1, n2):
    near = jnp.where(up, n_1, n1)
    far = jnp.where(up, n_2, n2)
    return speed * (3.0 * near - far)


def kx_flux(gx, rkx, n_ref, i, j):
    n = [load(n_ref, (i + d) * BY + j) for d in range(4)]
    return each(lambda g, r, *n: face(g > 0, r * g, *n), gx, load(rkx, i * BY + j), *n)


def ky_flux(gy, aky, layers, i, f):
    return each(lambda g, w, *n: face(g > 0, w, *n), gy, load(aky, i * (BY + 1) + f), *layers[f : f + 4])


class Halo:
    def __init__(self, od, ev, axis, flip):
        p, last = lax.axis_index(axis), lax.axis_size(axis) - 1
        middle = (last + 1) // 2
        self.od, self.ev, self.even = od, ev, is_even(p)
        self.low_empty, self.high_empty = p == 0, p == last
        self.low_at = [jnp.where(p == middle, t ^ flip, t) for t in range(T)]
        self.high_at = [jnp.where(p == middle - 1, t ^ flip, t) for t in range(T)]

    def take(self, first, second, slab, at, empty):
        def tile(t):
            r = slab * T + at[t]
            return jnp.where(empty, 0.0, jnp.where(self.even, first[r], second[r]))

        return [[tile(2 * a + b) for b in range(2)] for a in range(2)]

    def low(self, slab):
        return self.take(self.od, self.ev, slab, self.low_at, self.low_empty)

    def high(self, slab):
        return self.take(self.ev, self.od, slab, self.high_at, self.high_empty)


def pad_kx(n_ref, od, ev):
    halo = Halo(od, ev, "kx", 2)

    def one(r, carry):
        store(n_ref, r, halo.low(r))
        store(n_ref, (BX + 2) * BY + r, halo.high(r))
        return carry

    lax.fori_loop(0, 2 * BY, one, 0)


def no_inflow(x_up):
    s = lax.axis_index("space")
    return s == jnp.where(x_up, 0, lax.axis_size("space") - 1)


def stage_one_edges(
    np_in, ax, ay, rkx, aky, heights, hold_ref, spec, kx_od, kx_ev, x_od, x_ev,
    np_ref, p_ref, gx, edge, halo_speed, xnear, xflux, ky2_od, ky2_ev, fk, hrow,
):
    s, kx_place, ky_place, x_up, y_up = place()
    flow = Flow()
    kx_first, ky_first = kx_place * BX, ky_place * BY
    pad_kx(np_ref, kx_od, kx_ev)
    h = heights[...]
    x_flip, y_flip = jnp.where(x_up, 0, 1), jnp.where(y_up, 0, 1)
    none = no_inflow(x_up)
    use_od = is_even(s) == x_up
    for b in range(2):
        y = b ^ y_flip
        at = 4 * BX + y
        mine = h[:, 128 * b : 128 * b + 128]
        od, ev = x_od[at][0:1, :] * 0.01, x_ev[at][0:1, :] * 0.01
        low = jnp.where(s == 0, mine[0:1, :], jnp.where(is_even(s), od, ev))
        high = jnp.where(s == lax.axis_size("space") - 1, mine[BS - 1 : BS, :], jnp.where(is_even(s), ev, od))
        place_of = lax.broadcasted_iota(jnp.int32, (BS, 128), 0)
        before = jnp.where(place_of == 0, low, pltpu.roll(mine, 1, 0))
        after = jnp.where(place_of == BS - 1, high, pltpu.roll(mine, BS - 1, 0))
        slope = (before - after) * (1.0 / (2.0 * spacing))
        for a in range(2):
            gx[(a ^ x_flip) * 2 + y] = slope[8 * a : 8 * a + 8, :]
        face_low = jnp.broadcast_to(0.5 * (low + mine[0:1, :]), (8, 128))
        face_high = jnp.broadcast_to(0.5 * (high + mine[BS - 1 : BS, :]), (8, 128))
        hrow[y] = jnp.where(x_up, face_high, face_low)
        hrow[2 + y] = jnp.where(x_up, face_low, face_high)
    ky = ((ky_first + flow.rows - NKY // 2).astype(f32) + 0.5) * k_step

    def edges(i, carry):
        kx = centre(kx_first, i)
        k, inverse = wave(kx, ky)
        c = group_factor(k, inverse) * jnp.abs(kx)
        for b in range(2):
            at = i * 2 + b
            near = jnp.where(use_od, x_od[at], x_ev[at])
            far = jnp.where(use_od, x_od[2 * BX + at], x_ev[2 * BX + at])
            edge[at] = group(k, c, hrow[b])
            speed = group(k, c, hrow[2 + b])
            halo_speed[at] = speed
            xnear[at] = jnp.where(none, 0.0, near)
            xflux[at] = jnp.where(none, 0.0, speed * (3.0 * near - far))
        return carry

    lax.fori_loop(0, BX, edges, 0)

    g = load(gx, 0)
    for e, j in enumerate(EDGES):
        store(fk, e, kx_flux(g, rkx, np_ref, 0, j))

    def one_kx(i, carry):
        hold = each(lambda m: m == 1, load(hold_ref, 0))
        g = load(gx, 0)
        part = {}
        for e, j in enumerate(EDGES):
            n = load(np_ref, (i + 2) * BY + j)
            total = space_change(flow, n, ax, ay, i, j, edge, xnear, xflux)
            upper = kx_flux(g, rkx, np_ref, i + 1, j)
            lower = load(fk, e)
            store(fk, e, upper)
            part[j] = each(lambda n, t, u, v: n - (t + (u - v)), n, total, upper, lower)
            store(p_ref, i * len(EDGES) + e, part[j])

        def own(f, a, b):
            w = load(aky, i * (BY + 1) + f)
            a, b = (load(np_ref, (i + 2) * BY + j) for j in (a, b))
            return each(lambda w, a, b: w * (3.0 * a - b), w, a, b)

        def send(j, low, high, l, to):
            v = each(
                lambda m, p, u, v: jnp.where(m, spec[i * BY + j], p - (u - v)), hold, part[j], high, low
            )
            for ref, here in ((ky2_od, to), (ky2_ev, jnp.logical_not(to))):
                @pl.when(here)
                def _():
                    store(ref, i * 2 + l, v)

        f = [own(0, 0, 1), own(1, 1, 2), own(2, 2, 3)]
        send(0, f[0], f[1], 0, is_even(ky_place))
        send(1, f[1], f[2], 1, is_even(ky_place))
        f = [own(BY - 2, BY - 3, BY - 4), own(BY - 1, BY - 2, BY - 3), own(BY, BY - 1, BY - 2)]
        send(BY - 2, f[0], f[1], 0, jnp.logical_not(is_even(ky_place)))
        send(BY - 1, f[1], f[2], 1, jnp.logical_not(is_even(ky_place)))
        return carry

    lax.fori_loop(0, BX, one_kx, 0)


def ky_column(n_ref, halo, i):
    layers = [halo.low(i * 2 + l) for l in range(2)]
    layers += [load(n_ref, (i + 2) * BY + j) for j in range(BY)]
    return layers + [halo.high(i * 2 + l) for l in range(2)]


def stage_one_rest(
    np_ref, p_ref, ax, ay, rkx, aky, gx, gy, edge, xnear, xflux, hold_ref, spec, ky_od, ky_ev,
    sp_ref, kx2_od, kx2_ev, x2, fk, sems,
):
    s, kx_place, ky_place, x_up, y_up = place()
    flow = Flow()
    halo = Halo(ky_od, ky_ev, "ky", 1)
    g = load(gx, 0)
    for e, j in enumerate(MIDDLE):
        store(fk, e, kx_flux(g, rkx, np_ref, 0, j))

    def one_kx(i, carry):
        hold = each(lambda m: m == 1, load(hold_ref, 0))
        g, gk = load(gx, 0), load(gy, 0)
        layers = ky_column(np_ref, halo, i)
        lower_y = ky_flux(gk, aky, layers, i, 0)
        last = [[], []]
        for j in range(BY):
            n = layers[j + 2]
            if j in EDGES:
                p = load(p_ref, i * len(EDGES) + EDGES.index(j))
            else:
                e = MIDDLE.index(j)
                total = space_change(flow, n, ax, ay, i, j, edge, xnear, xflux)
                upper = kx_flux(g, rkx, np_ref, i + 1, j)
                lower = load(fk, e)
                store(fk, e, upper)
                p = each(lambda n, t, u, v: n - (t + (u - v)), n, total, upper, lower)
            upper_y = ky_flux(gk, aky, layers, i, j + 1)
            v = each(
                lambda m, p, u, v: jnp.where(m, spec[i * BY + j], p - (u - v)), hold, p, upper_y, lower_y
            )
            store(sp_ref, (i + 2) * BY + j, v)
            lower_y = upper_y
            for b in range(2):
                last[b].append(v[1][b])
        for b in range(2):
            rows = flow.edge_rows(last[b])
            for l in range(2):
                x2[l * 2 * BX + i * 2 + b] = rows[l]
        return carry

    lax.fori_loop(0, BX, one_kx, 0)
    size = 2 * BY * T
    low, high = 0, (BX - 2) * BY * T
    copies = [
        pltpu.make_async_copy(sp_ref.at[pl.ds(size + jnp.where(is_even(kx_place), *at), size)], ref, sems.at[n])
        for n, (ref, at) in enumerate(((kx2_od, (low, high)), (kx2_ev, (high, low))))
    ]
    for c in copies:
        c.start()
    for c in copies:
        c.wait()


STEP = 4


def send_out(buffer, out, sem, i):
    @pl.when(i % STEP == STEP - 1)
    def _():
        flow = Flow()
        rows = pl.ds(i - (STEP - 1), STEP)
        for a in range(2):
            for b in range(2):
                x, y = flow.natural(a, b)
                pltpu.make_async_copy(buffer.at[rows, :, 2 * a + b], out.at[rows, :, x, y], sem).start()


def stage_two_inner(np_ref, sp_in, ax, ay, rkx, aky, gx, gy, edge, sp_ref, q_ref, fk):
    flow = Flow()
    nothing = each(lambda v: jnp.zeros_like(v), load(gx, 0))

    def clear(r, carry):
        store(sp_ref, r, nothing)
        store(sp_ref, (BX + 2) * BY + r, nothing)
        return carry

    lax.fori_loop(0, 2 * BY, clear, 0)
    g = load(gx, 0)
    for j in range(BY):
        store(fk, j, kx_flux(g, rkx, sp_ref, 0, j))

    def one_kx(i, carry):
        g, gk = load(gx, 0), load(gy, 0)
        layers = [nothing] * 2 + [load(sp_ref, (i + 2) * BY + j) for j in range(BY)] + [nothing] * 2
        lower_y = ky_flux(gk, aky, layers, i, 0)
        for j in range(BY):
            slab = i * BY + j
            n = layers[j + 2]
            total = space_change(flow, n, ax, ay, i, j, edge, None, None)
            upper = kx_flux(g, rkx, sp_ref, i + 1, j)
            lower = load(fk, j)
            store(fk, j, upper)
            upper_y = ky_flux(gk, aky, layers, i, j + 1)
            v = each(
                lambda a, n, t, u, v, p, q: 0.5 * ((a + n) - ((t + (u - v)) + (p - q))),
                load(np_ref, (i + 2) * BY + j), n, total, upper, lower, upper_y, lower_y,
            )
            store(q_ref, slab, v)
            lower_y = upper_y
        return carry

    lax.fori_loop(0, BX, one_kx, 0)


def halo_terms(g, low_speeds, high_speeds, low, high):
    up = [each(lambda g, w: jnp.where(g > 0, 0.5 * w, 0.0), g, w) for w in low_speeds]
    down = [each(lambda g, w: jnp.where(g > 0, 0.0, 0.5 * w), g, w) for w in high_speeds]
    end = each(lambda w, a, b: w * (3.0 * a - b), up[0], low[1], low[0])
    second = each(lambda w, a: w * a, up[1], low[1])
    top = each(lambda w, a, b: w * (3.0 * a - b), down[1], high[0], high[1])
    below_top = each(lambda w, a: w * a, down[0], high[0])
    return (
        each(lambda a, b: a + b, end, second),
        each(lambda b: -b, second),
        below_top,
        each(lambda a, b: -(a + b), top, below_top),
    )


def stage_two_outer(
    q_in, ax, rkx, aky, gx, gy, halo_speed, hold_ref, spec, kx_od, kx_ev, x2, ky_od, ky_ev,
    q_ref, out, xnear, xflux, done, sem,
):
    _, _, _, x_up, _ = place()
    flow = Flow()
    none = no_inflow(x_up)
    near = jnp.where(none, 0.0, x2[pl.ds(0, 2 * BX)])
    xnear[...] = 0.5 * near
    xflux[...] = (3.0 * near - jnp.where(none, 0.0, x2[pl.ds(2 * BX, 2 * BX)])) * (0.5 * halo_speed[...])
    kx_halo, ky_halo = Halo(kx_od, kx_ev, "kx", 2), Halo(ky_od, ky_ev, "ky", 1)

    def kx_ends(j, carry):
        g = load(gx, 0)
        speed = [each(lambda r, g: r * g, load(rkx, f * BY + j), g) for f in (0, 1, BX - 1, BX)]
        low = [kx_halo.low(l * BY + j) for l in range(2)]
        high = [kx_halo.high(l * BY + j) for l in range(2)]
        terms = halo_terms(g, speed[:2], speed[2:], low, high)
        for i, term in zip((0, 1, BX - 2, BX - 1), terms):
            slab = i * BY + j
            store(q_ref, slab, each(lambda q, t: q + t, load(q_ref, slab), term))
        return carry

    lax.fori_loop(0, BY, kx_ends, 0)
    second = flow.rows == jnp.where(x_up, 1, 6)

    def one_kx(i, carry):
        hold = each(lambda m: m == 1, load(hold_ref, 0))
        gk = load(gy, 0)
        speed = [load(aky, i * (BY + 1) + f) for f in (0, 1, BY - 1, BY)]
        low = [ky_halo.low(i * 2 + l) for l in range(2)]
        high = [ky_halo.high(i * 2 + l) for l in range(2)]
        terms = dict(zip(EDGES, halo_terms(gk, speed[:2], speed[2:], low, high)))
        for j in range(BY):
            slab = i * BY + j
            q = load(q_ref, slab)
            if j in terms:
                q = each(lambda q, t: q + t, q, terms[j])
            for b in range(2):
                less = ax[slab * T + b] * row(xnear, i, j, b)
                into = less + row(xflux, i, j, b)
                q[0][b] = q[0][b] + jnp.where(
                    flow.x_first, into, jnp.where(second, -pltpu.roll(less, flow.x_roll, 0), 0.0)
                )
            for a in range(2):
                for b in range(2):
                    done[i, j, 2 * a + b] = jnp.where(hold[a][b], spec[slab], q[a][b])
        send_out(done, out, sem, i)
        return carry

    lax.fori_loop(0, BX, one_kx, 0)
    wait_all(done, sem)


def call(kernel, outs, operands, spaces, out_spaces, scratch=(), alias=None, us=1, limit=LIMIT):
    whole = {
        "v": pl.BlockSpec(memory_space=pltpu.VMEM),
        "h": pl.BlockSpec(memory_space=pltpu.HBM),
    }
    return pl.pallas_call(
        kernel,
        out_shape=tuple(outs),
        in_specs=[whole[c] for c in spaces],
        out_specs=tuple(whole[c] for c in out_spaces),
        scratch_shapes=list(scratch),
        input_output_aliases=alias or {},
        compiler_params=pltpu.CompilerParams(vmem_limit_bytes=limit),
        cost_estimate=pl.CostEstimate(flops=int(us * 1e9), bytes_accessed=0, transcendentals=0),
        name=kernel.__name__,
    )(*operands)


def per_device(action, depth_cm, inflow_mask, inflow):
    slabs, padded = BX * BY * T, (BX + 4) * BY * T
    edge_slabs, ky_tiles, kx_tiles = BX * len(EDGES) * T, BX * 2 * T, 2 * BY * T
    sizes = [lax.axis_size(axis) for axis in AXES]

    def v(*shape):
        return pltpu.VMEM(shape + (8, 128), f32)

    def swap(od, ev, axis, spare):
        at, beside = AXES.index(axis), AXES.index(spare)
        return (
            lax.ppermute(od, AXES, swaps(sizes, at, 1, beside)),
            lax.ppermute(ev, AXES, swaps(sizes, at, 0, beside)),
        )

    sem = pltpu.SemaphoreType.DMA
    np5, ky_od, ky_ev, kx_od, kx_ev, x_od, x_ev, depth, mask, spectrum, ay = call(
        first_messages,
        (v(BX + 4, BY, T), v(BX, 2, T), v(BX, 2, T), v(2, BY, T), v(2, BY, T), v(4 * BX + 2), v(4 * BX + 2),
         pltpu.VMEM((BS, NY), jnp.int32), pltpu.VMEM((BS, NY), jnp.int32), pltpu.VMEM((NKX, NKY), f32), v(slabs)),
        (action, depth_cm, inflow_mask, inflow),
        "hhhh",
        "v" * 11,
        [v(T), sem((8,))],
        us=0,
        limit=FIRST_LIMIT,
    )
    ky_od, ky_ev = (m.reshape(ky_tiles, 8, 128) for m in swap(ky_od, ky_ev, "ky", "kx"))
    kx_od, kx_ev = (m.reshape(kx_tiles, 8, 128) for m in swap(kx_od, kx_ev, "kx", "space"))
    x_od, x_ev = swap(x_od, x_ev, "space", "kx")
    ax, rkx, aky, gy, heights, hold, spec = call(
        speeds,
        (v(slabs), v((BX + 1) * BY * T), v(BX * (BY + 1) * T), v(T), pltpu.VMEM((BS, NY), f32),
         pltpu.VMEM((T, 8, 128), jnp.int32), v(BX * BY)),
        (depth, mask, spectrum),
        "vvv",
        "v" * 7,
        [v(2 * T)],
        us=4,
    )
    np3 = np5.reshape(padded, 8, 128)
    np3, part, gx, edge, halo_speed, xnear, xflux, ky2_od, ky2_ev = call(
        stage_one_edges,
        (v(padded), v(edge_slabs), v(T), v(2 * BX), v(2 * BX), v(2 * BX), v(2 * BX), v(ky_tiles), v(ky_tiles)),
        (np3, ax, ay, rkx, aky, heights, hold, spec, kx_od, kx_ev, x_od, x_ev),
        "v" * 12,
        "v" * 9,
        [v(len(EDGES) * T), v(4)],
        alias={0: 0},
        us=0,
    )
    ky2_od, ky2_ev = swap(ky2_od, ky2_ev, "ky", "kx")
    sp, kx2_od, kx2_ev, x2 = call(
        stage_one_rest,
        (v(padded), v(kx_tiles), v(kx_tiles), v(4 * BX)),
        (np3, part, ax, ay, rkx, aky, gx, gy, edge, xnear, xflux, hold, spec, ky_od, ky_ev),
        "v" * 15,
        "v" * 4,
        [v(len(MIDDLE) * T), sem((2,))],
        us=0,
    )
    kx2_od, kx2_ev = swap(kx2_od, kx2_ev, "kx", "space")
    x2 = lax.ppermute(x2, AXES[:2], ring(sizes))
    sp, q = call(
        stage_two_inner,
        (v(padded), v(slabs)),
        (np3, sp, ax, ay, rkx, aky, gx, gy, edge),
        "v" * 9,
        "vv",
        [v(BY * T)],
        alias={1: 0},
        us=4,
    )
    _, out = call(
        stage_two_outer,
        (v(slabs), jax.ShapeDtypeStruct(action.shape, f32)),
        (q, ax, rkx, aky, gx, gy, halo_speed, hold, spec, kx2_od, kx2_ev, x2, ky2_od, ky2_ev),
        "v" * 14,
        "vh",
        [v(2 * BX), v(2 * BX), v(BX, BY, T), sem],
        alias={0: 0},
        us=0,
    )
    return out


def solution(mesh):
    in_specs = (P("kx", "ky", "space", None), P("space", None), P("space", None), P())
    out_specs = P("kx", "ky", "space", None)
    return jax.shard_map(
        per_device, mesh=mesh, in_specs=in_specs, out_specs=out_specs, check_vma=False
    )
```

```python
import jax
import jax.numpy as jnp
from jax import lax
from jax.experimental import pallas as pl
from jax.experimental.pallas import tpu as pltpu
from jax.sharding import PartitionSpec as P

NKX = 64
NKY = 64

gravity = 9.81
spacing = 4.0
k_step = 0.04
time_step = 0.2

BX, BY, BS, NY = 16, 8, 16, 256
T = 4
SPARE = 3
f32 = jnp.float32
LIMIT = 8 * 2**20
FIRST_LIMIT = 54 * 2**20
EDGES = (0, 1, BY - 2, BY - 1)
MIDDLE = tuple(range(2, BY - 2))

X_SCALE = time_step / spacing * 0.5
K_SCALE = time_step / k_step * 0.5


AXES = ("space", "kx", "ky")


def swaps(sizes, axis, odd, spare):
    pairs = []
    for n in range(sizes[0] * sizes[1] * sizes[2]):
        at = [n // (sizes[1] * sizes[2]), n // sizes[2] % sizes[1], n % sizes[2]]
        other = ((at[axis] + odd) ^ 1) - odd
        if 0 <= other < sizes[axis]:
            at[axis] = other
        else:
            at[spare] ^= 1
        pairs.append((n, (at[0] * sizes[1] + at[1]) * sizes[2] + at[2]))
    return pairs


def ring(sizes, way):
    pairs = []
    for a in range(sizes[0]):
        for b in range(sizes[1]):
            to = (a + (way if b >= sizes[1] // 2 else -way)) % sizes[0]
            pairs.append((a * sizes[1] + b, to * sizes[1] + b))
    return pairs


def place():
    s, i, j = lax.axis_index("space"), lax.axis_index("kx"), lax.axis_index("ky")
    return s, i, j, i >= lax.axis_size("kx") // 2, j >= lax.axis_size("ky") // 2


def is_even(i):
    return i % 2 == 0


class Flow:
    def __init__(self):
        _, _, _, x_up, y_up = place()
        x0 = jnp.where(x_up, 0, 8)
        y0 = jnp.where(y_up, 0, 128)
        self.x_up = x_up
        self.x = (pl.multiple_of(x0, 8), pl.multiple_of(8 - x0, 8))
        self.y = (pl.multiple_of(y0, 128), pl.multiple_of(128 - y0, 128))
        self.x_roll = jnp.where(x_up, 1, 7)
        self.y_roll = jnp.where(y_up, 1, 127)
        self.rows = lax.broadcasted_iota(jnp.int32, (8, 128), 0)
        lanes = lax.broadcasted_iota(jnp.int32, (8, 128), 1)
        self.x_first = self.rows == jnp.where(x_up, 0, 7)
        self.x_last = self.rows == jnp.where(x_up, 7, 0)
        self.y_first = lanes == jnp.where(y_up, 0, 127)

    def natural(self, a, b):
        return pl.ds(self.x[a], 8), pl.ds(self.y[b], 128)

    def before_x(self, tiles, b, halo):
        first, second = (pltpu.roll(tiles[a][b], self.x_roll, 0) for a in range(2))
        return [jnp.where(self.x_first, halo, first), jnp.where(self.x_first, first, second)]

    def before_y(self, tiles, a):
        first, second = (pltpu.roll(tiles[a][b], self.y_roll, 1) for b in range(2))
        return [jnp.where(self.y_first, 0.0, first), jnp.where(self.y_first, first, second)]

    def edge_rows(self, tiles):
        out = []
        for up, down in ((7, 0), (6, 1)):
            rows = None
            for j in range(BY):
                shift = jnp.where(self.x_up, (j - up) % 8, (j - down) % 8)
                turned = pltpu.roll(tiles[j], shift, 0)
                rows = turned if rows is None else jnp.where(self.rows == j, turned, rows)
            out.append(rows)
        return out


def load(ref, slab):
    return [[ref[slab * T + 2 * a + b] for b in range(2)] for a in range(2)]


def store(ref, slab, tiles):
    for a in range(2):
        for b in range(2):
            ref[slab * T + 2 * a + b] = tiles[a][b]


def each(fn, *grids):
    return [[fn(*(g[a][b] for g in grids)) for b in range(2)] for a in range(2)]


def row(ref, i, j, b):
    return jnp.broadcast_to(ref[i * 2 + b][j : j + 1, :], (8, 128))


def wait_all(dst, sem):
    pltpu.make_async_copy(dst, dst, sem).wait()


def shifted(h, axis, up):
    size = h.shape[axis]
    place_of = lax.broadcasted_iota(jnp.int32, h.shape, axis)
    if up:
        return jnp.where(place_of == size - 1, h, pltpu.roll(h, size - 1, axis))
    return jnp.where(place_of == 0, h, pltpu.roll(h, 1, axis))


def centre(first, i):
    return ((first + i - NKX // 2).astype(f32) + 0.5) * k_step


def lower_face(first, i):
    return (first + i - NKX // 2).astype(f32) * k_step


def wave(kx, ky):
    square = jnp.broadcast_to(kx * kx + ky * ky, (8, 128))
    inverse = lax.rsqrt(square)
    return square * inverse, inverse


def centre_rows(flow, first):
    return ((first + flow.rows - NKY // 2).astype(f32) + 0.5) * k_step


def pick(tile, j):
    return jnp.broadcast_to(tile[j : j + 1, :], (8, 128))


def group_factor(k, inverse):
    return (0.5 * X_SCALE * gravity**0.5) * inverse * lax.rsqrt(k)


def refract_factor(k):
    return (0.5 * K_SCALE * gravity**0.5) * (k * k) * lax.rsqrt(k)


def group(k, c, h):
    kh = k * h
    t = jnp.tanh(kh)
    return c * ((t + kh * (1.0 - t * t)) * lax.rsqrt(t))


def refract(k, c, h):
    t = jnp.tanh(k * h)
    return c * ((1.0 - t * t) * lax.rsqrt(t))


def first_messages(
    a_ref, depth_ref, mask_ref, inflow_ref,
    np_ref, kx_od, kx_ev, x1, depth, mask, inflow, ay, geo, sems,
):
    s, i, j, x_up, y_up = place()
    flow = Flow()
    own = np_ref.at[pl.ds(2, BX)]
    small = [
        pltpu.make_async_copy(src, dst, sems.at[n])
        for n, (src, dst) in enumerate(((depth_ref, depth), (mask_ref, mask), (inflow_ref, inflow)))
    ]
    for c in small:
        c.start()
    for a in range(2):
        for b in range(2):
            x, y = flow.natural(a, b)
            pltpu.make_async_copy(a_ref.at[:, :, x, y], own.at[:, :, 2 * a + b], sems.at[3]).start()
    for c in small:
        c.wait()
    h = depth[...].astype(f32) * 0.01
    hy = 0.5 * (h + jnp.where(y_up, shifted(h, 1, True), shifted(h, 1, False)))
    x_flip, y_flip = jnp.where(x_up, 0, 1), jnp.where(y_up, 0, 1)
    for a in range(2):
        for b in range(2):
            geo[(a ^ x_flip) * 2 + (b ^ y_flip)] = hy[8 * a : 8 * a + 8, 128 * b : 128 * b + 128]
    kx_first, ky_first = i * BX, j * BY

    def y_speeds(i, carry):
        kx, ky = centre(kx_first, i), centre_rows(flow, ky_first)
        k, inverse = wave(kx, ky)
        c = group_factor(k, inverse) * jnp.abs(ky)
        for j in range(BY):
            kj, cj = pick(k, j), pick(c, j)
            store(ay, i * BY + j, each(lambda h: group(kj, cj, h), load(geo, 0)))
        return carry

    lax.fori_loop(0, BX, y_speeds, 0)
    wait_all(own, sems.at[3])
    low, high = 2 * BY * T, BX * BY * T
    low, high = jnp.where(is_even(i), low, high), jnp.where(is_even(i), high, low)
    flat, size = np_ref.reshape((BX + 4) * BY * T, 8, 128), 2 * BY * T
    messages = [
        pltpu.make_async_copy(flat.at[pl.ds(at, size)], ref.at[pl.ds(0, size)], sems.at[n])
        for n, (at, ref) in enumerate(((low, kx_od), (high, kx_ev)), 4)
    ]
    for t in range(size, size + SPARE):
        kx_ev[t] = jnp.zeros((8, 128), f32)
    for c in messages:
        c.start()
    for b in range(2):
        y = pl.ds(flow.y[b], 128)
        first = jnp.broadcast_to(depth[0:1, y].astype(f32), (8, 128))
        last = jnp.broadcast_to(depth[BS - 1 : BS, y].astype(f32), (8, 128))
        x1[4 * BX + b] = jnp.where(x_up, last, first)

    def one_kx(i, carry):
        for b in range(2):
            rows = flow.edge_rows([np_ref[i + 2, j, 2 + b] for j in range(BY)])
            for l in range(2):
                x1[l * 2 * BX + i * 2 + b] = rows[l]
        return carry

    lax.fori_loop(0, BX, one_kx, 0)
    for c in messages:
        c.wait()


def ky_messages(np_ref, next_depth, ky_od, ky_ev, next_row, sems):
    _, _, j, x_up, _ = place()
    own = np_ref.at[pl.ds(2, BX)]
    low, high = jnp.where(is_even(j), 0, BY - 2), jnp.where(is_even(j), BY - 2, 0)
    messages = [
        pltpu.make_async_copy(own.at[:, pl.ds(at, 2)], ref, sems.at[n])
        for n, (at, ref) in enumerate(((low, ky_od), (high, ky_ev)))
    ]
    for c in messages:
        c.start()
    coming = jnp.where(x_up, next_depth[0:1, :], next_depth[BS - 1 : BS, :]).astype(f32) * 0.01
    next_row[...] = jnp.broadcast_to(coming, (8, NY))
    for c in messages:
        c.wait()


def speeds(depth, mask, inflow, ax, rkx, aky, gy, heights, hold, spec, geo):
    _, kx_place, ky_place, x_up, y_up = place()
    flow = Flow()
    kx_first, ky_first = kx_place * BX, ky_place * BY
    h = depth[...].astype(f32) * 0.01
    heights[...] = h
    y_next, y_last = shifted(h, 1, True), shifted(h, 1, False)
    hx = 0.5 * (h + jnp.where(x_up, shifted(h, 0, True), shifted(h, 0, False)))
    slope = (y_last - y_next) * (1.0 / (2.0 * spacing))
    x_flip, y_flip = jnp.where(x_up, 0, 1), jnp.where(y_up, 0, 1)
    for a in range(2):
        for b in range(2):
            at = (a ^ x_flip) * 2 + (b ^ y_flip)
            part = (slice(8 * a, 8 * a + 8), slice(128 * b, 128 * b + 128))
            gy[at] = slope[part]
            hold[at] = mask[part]
            geo[at] = h[part]
            geo[T + at] = hx[part]

    lanes = lax.broadcasted_iota(jnp.int32, (8, NKY), 1)
    for half in range(BX // 8):
        rows = inflow[pl.ds(pl.multiple_of(kx_first + 8 * half, 8), 8), :]
        for j in range(BY):
            column = jnp.sum(jnp.where(lanes == ky_first + j, rows, 0.0), axis=1, keepdims=True)
            column = jnp.broadcast_to(column, (8, 128))
            for r in range(8):
                spec[(8 * half + r) * BY + j] = jnp.broadcast_to(column[r : r + 1, :], (8, 128))

    ky = centre_rows(flow, ky_first)
    ky_face = (ky_first + flow.rows - NKY // 2).astype(f32) * k_step

    def kx_faces(i):
        k, _ = wave(lower_face(kx_first, i), ky)
        c = refract_factor(k)
        for j in range(BY):
            kj, cj = pick(k, j), pick(c, j)
            store(rkx, i * BY + j, each(lambda h: refract(kj, cj, h), load(geo, 0)))

    def one_kx(i, carry):
        kx = centre(kx_first, i)
        k, inverse = wave(kx, ky)
        c = group_factor(k, inverse) * jnp.abs(kx)
        for j in range(BY):
            kj, cj = pick(k, j), pick(c, j)
            store(ax, i * BY + j, each(lambda h: group(kj, cj, h), load(geo, 1)))
        kx_faces(i)
        k, _ = wave(kx, ky_face)
        c = refract_factor(k)
        end, _ = wave(kx, lower_face(ky_first, BY))
        end_c = refract_factor(end)
        for j in range(BY + 1):
            kj, cj = (pick(k, j), pick(c, j)) if j < BY else (end, end_c)
            store(aky, i * (BY + 1) + j, each(lambda h, g: refract(kj, cj, h) * g, load(geo, 0), load(gy, 0)))
        return carry

    lax.fori_loop(0, BX, one_kx, 0)
    kx_faces(BX)


def space_change(flow, n, ax_ref, ay_ref, i, j, edge, halo_row, halo_flux):
    slab = i * BY + j
    ax, ay = load(ax_ref, slab), load(ay_ref, slab)
    n3 = each(lambda v: 3.0 * v, n)
    total = [[None, None], [None, None]]
    for b in range(2):
        ax[1][b] = jnp.where(flow.x_last, row(edge, i, j, b), ax[1][b])
        before = flow.before_x(n, b, 0.0 if halo_row is None else row(halo_row, i, j, b))
        out = [[ax[a][b] * (n3[a][b] - before[a])] * 2 for a in range(2)]
        into = flow.before_x(out, b, 0.0 if halo_flux is None else row(halo_flux, i, j, b))
        for a in range(2):
            total[a][b] = out[a][b] - into[a]
    for a in range(2):
        before = flow.before_y(n, a)
        out = [ay[a][b] * (n3[a][b] - before[b]) for b in range(2)]
        into = flow.before_y([out, out], 0)
        for b in range(2):
            total[a][b] = total[a][b] + (out[b] - into[b])
    return total


def face(up, speed, n_2, n_1, n1, n2):
    near = jnp.where(up, n_1, n1)
    far = jnp.where(up, n_2, n2)
    return speed * (3.0 * near - far)


def kx_flux(gx, rkx, n_ref, i, j):
    n = [load(n_ref, (i + d) * BY + j) for d in range(4)]
    return each(lambda g, r, *n: face(g > 0, r * g, *n), gx, load(rkx, i * BY + j), *n)


def ky_flux(gy, aky, layers, i, f):
    return each(lambda g, w, *n: face(g > 0, w, *n), gy, load(aky, i * (BY + 1) + f), *layers[f : f + 4])


class Halo:
    def __init__(self, od, ev, axis, flip):
        p, last = lax.axis_index(axis), lax.axis_size(axis) - 1
        middle = (last + 1) // 2
        self.od, self.ev, self.even = od, ev, is_even(p)
        self.low_empty, self.high_empty = p == 0, p == last
        self.low_at = [jnp.where(p == middle, t ^ flip, t) for t in range(T)]
        self.high_at = [jnp.where(p == middle - 1, t ^ flip, t) for t in range(T)]

    def take(self, first, second, slab, at, empty):
        def tile(t):
            r = slab * T + at[t]
            return jnp.where(empty, 0.0, jnp.where(self.even, first[r], second[r]))

        return [[tile(2 * a + b) for b in range(2)] for a in range(2)]

    def low(self, slab):
        return self.take(self.od, self.ev, slab, self.low_at, self.low_empty)

    def high(self, slab):
        return self.take(self.ev, self.od, slab, self.high_at, self.high_empty)


def no_inflow(x_up):
    s = lax.axis_index("space")
    return s == jnp.where(x_up, 0, lax.axis_size("space") - 1)


def stage_one_edges(
    np_in, ax, ay, rkx, aky, heights, hold_ref, spec, kx_od, x1, kx_ev, next_row,
    np_ref, p_ref, gx, edge, halo_speed, xnear, xflux, ky2_od, ky2_ev, fk, hrow,
):
    s, kx_place, ky_place, x_up, y_up = place()
    flow = Flow()
    kx_first, ky_first = kx_place * BX, ky_place * BY
    odd_low = is_even(kx_place)
    empty = jnp.where(odd_low, kx_place == 0, kx_place == lax.axis_size("kx") - 1)
    base = jnp.where(odd_low, 0, (BX + 2) * BY)

    def odd_side(r, carry):
        tiles = [[kx_od[r * T + 2 * (1 - a) + b] for b in range(2)] for a in range(2)]
        store(np_ref, base + r, each(lambda v: jnp.where(empty, 0.0, v), tiles))
        return carry

    lax.fori_loop(0, 2 * BY, odd_side, 0)
    size = 2 * BY * T
    np_ref[pl.ds(jnp.where(odd_low, (BX + 2) * BY * T, 0), size)] = kx_ev[pl.ds(0, size)]
    h = heights[...]
    x_flip, y_flip = jnp.where(x_up, 0, 1), jnp.where(y_up, 0, 1)
    none = no_inflow(x_up)
    for b in range(2):
        y = b ^ y_flip
        at = 4 * BX + y
        mine = h[:, 128 * b : 128 * b + 128]
        last = x1[at][0:1, :] * 0.01
        coming = next_row[0:1, 128 * b : 128 * b + 128]
        low = jnp.where(s == 0, mine[0:1, :], jnp.where(x_up, last, coming))
        high = jnp.where(s == lax.axis_size("space") - 1, mine[BS - 1 : BS, :], jnp.where(x_up, coming, last))
        place_of = lax.broadcasted_iota(jnp.int32, (BS, 128), 0)
        before = jnp.where(place_of == 0, low, pltpu.roll(mine, 1, 0))
        after = jnp.where(place_of == BS - 1, high, pltpu.roll(mine, BS - 1, 0))
        slope = (before - after) * (1.0 / (2.0 * spacing))
        for a in range(2):
            gx[(a ^ x_flip) * 2 + y] = slope[8 * a : 8 * a + 8, :]
        face_low = jnp.broadcast_to(0.5 * (low + mine[0:1, :]), (8, 128))
        face_high = jnp.broadcast_to(0.5 * (high + mine[BS - 1 : BS, :]), (8, 128))
        hrow[y] = jnp.where(x_up, face_high, face_low)
        hrow[2 + y] = jnp.where(x_up, face_low, face_high)
    ky = ((ky_first + flow.rows - NKY // 2).astype(f32) + 0.5) * k_step

    def edges(i, carry):
        kx = centre(kx_first, i)
        k, inverse = wave(kx, ky)
        c = group_factor(k, inverse) * jnp.abs(kx)
        for b in range(2):
            at = i * 2 + b
            near, far = x1[at], x1[2 * BX + at]
            edge[at] = group(k, c, hrow[b])
            speed = group(k, c, hrow[2 + b])
            halo_speed[at] = speed
            xnear[at] = jnp.where(none, 0.0, near)
            xflux[at] = jnp.where(none, 0.0, speed * (3.0 * near - far))
        return carry

    lax.fori_loop(0, BX, edges, 0)

    g = load(gx, 0)
    for e, j in enumerate(EDGES):
        store(fk, e, kx_flux(g, rkx, np_ref, 0, j))

    def one_kx(i, carry):
        hold = each(lambda m: m == 1, load(hold_ref, 0))
        g = load(gx, 0)
        part = {}
        for e, j in enumerate(EDGES):
            n = load(np_ref, (i + 2) * BY + j)
            total = space_change(flow, n, ax, ay, i, j, edge, xnear, xflux)
            upper = kx_flux(g, rkx, np_ref, i + 1, j)
            lower = load(fk, e)
            store(fk, e, upper)
            part[j] = each(lambda n, t, u, v: n - (t + (u - v)), n, total, upper, lower)
            store(p_ref, i * len(EDGES) + e, part[j])

        def own(f, a, b):
            w = load(aky, i * (BY + 1) + f)
            a, b = (load(np_ref, (i + 2) * BY + j) for j in (a, b))
            return each(lambda w, a, b: w * (3.0 * a - b), w, a, b)

        def edge_layer(j, low, high):
            return each(lambda m, p, u, v: jnp.where(m, spec[i * BY + j], p - (u - v)), hold, part[j], high, low)

        f = [own(0, 0, 1), own(1, 1, 2), own(2, 2, 3)]
        down = [edge_layer(0, f[0], f[1]), edge_layer(1, f[1], f[2])]
        f = [own(BY - 2, BY - 3, BY - 4), own(BY - 1, BY - 2, BY - 3), own(BY, BY - 1, BY - 2)]
        up = [edge_layer(BY - 2, f[0], f[1]), edge_layer(BY - 1, f[1], f[2])]
        for l in range(2):
            store(ky2_od, i * 2 + l, each(lambda a, b: jnp.where(is_even(ky_place), a, b), down[l], up[l]))
            store(ky2_ev, i * 2 + l, each(lambda a, b: jnp.where(is_even(ky_place), b, a), down[l], up[l]))
        return carry

    lax.fori_loop(0, BX, one_kx, 0)


def ky_column(n_ref, halo, i):
    layers = [halo.low(i * 2 + l) for l in range(2)]
    layers += [load(n_ref, (i + 2) * BY + j) for j in range(BY)]
    return layers + [halo.high(i * 2 + l) for l in range(2)]


def stage_one_rest(
    np_ref, p_ref, ax, ay, rkx, aky, gx, gy, edge, xnear, xflux, hold_ref, spec, ky_od, ky_ev,
    sp_ref, x2, fk,
):
    s, kx_place, ky_place, x_up, y_up = place()
    flow = Flow()
    halo = Halo(ky_od, ky_ev, "ky", 1)
    g = load(gx, 0)
    for e, j in enumerate(MIDDLE):
        store(fk, e, kx_flux(g, rkx, np_ref, 0, j))

    def one_kx(i, carry):
        hold = each(lambda m: m == 1, load(hold_ref, 0))
        g, gk = load(gx, 0), load(gy, 0)
        layers = ky_column(np_ref, halo, i)
        lower_y = ky_flux(gk, aky, layers, i, 0)
        last = [[], []]
        for j in range(BY):
            n = layers[j + 2]
            if j in EDGES:
                p = load(p_ref, i * len(EDGES) + EDGES.index(j))
            else:
                e = MIDDLE.index(j)
                total = space_change(flow, n, ax, ay, i, j, edge, xnear, xflux)
                upper = kx_flux(g, rkx, np_ref, i + 1, j)
                lower = load(fk, e)
                store(fk, e, upper)
                p = each(lambda n, t, u, v: n - (t + (u - v)), n, total, upper, lower)
            upper_y = ky_flux(gk, aky, layers, i, j + 1)
            v = each(
                lambda m, p, u, v: jnp.where(m, spec[i * BY + j], p - (u - v)), hold, p, upper_y, lower_y
            )
            store(sp_ref, (i + 2) * BY + j, v)
            lower_y = upper_y
            for b in range(2):
                last[b].append(v[1][b])
        for b in range(2):
            rows = flow.edge_rows(last[b])
            for l in range(2):
                x2[l * 2 * BX + i * 2 + b] = rows[l]
        return carry

    lax.fori_loop(0, BX, one_kx, 0)


def kx_messages(sp_in, sp_ref, kx2_od, kx2_ev, sems):
    _, kx_place, _, _, _ = place()
    size = 2 * BY * T
    low, high = size, size + (BX - 2) * BY * T
    messages = [
        pltpu.make_async_copy(sp_ref.at[pl.ds(jnp.where(is_even(kx_place), *at), size)], ref, sems.at[n])
        for n, (ref, at) in enumerate(((kx2_od, (low, high)), (kx2_ev, (high, low))))
    ]
    for c in messages:
        c.start()
    sp_ref[pl.ds(0, size)] = jnp.zeros((size, 8, 128), f32)
    sp_ref[pl.ds((BX + 2) * BY * T, size)] = jnp.zeros((size, 8, 128), f32)
    for c in messages:
        c.wait()


STEP = 4


def send_out(buffer, out, sem, i):
    @pl.when(i % STEP == STEP - 1)
    def _():
        flow = Flow()
        rows = pl.ds(i - (STEP - 1), STEP)
        for a in range(2):
            for b in range(2):
                x, y = flow.natural(a, b)
                pltpu.make_async_copy(buffer.at[rows, :, 2 * a + b], out.at[rows, :, x, y], sem).start()


def stage_two_inner(np_ref, sp_ref, ax, ay, rkx, aky, gx, gy, edge, q_ref, fk):
    flow = Flow()
    nothing = each(lambda v: jnp.zeros_like(v), load(gx, 0))

    g = load(gx, 0)
    for j in range(BY):
        store(fk, j, kx_flux(g, rkx, sp_ref, 0, j))

    def one_kx(i, carry):
        g, gk = load(gx, 0), load(gy, 0)
        layers = [nothing] * 2 + [load(sp_ref, (i + 2) * BY + j) for j in range(BY)] + [nothing] * 2
        lower_y = ky_flux(gk, aky, layers, i, 0)
        for j in range(BY):
            slab = i * BY + j
            n = layers[j + 2]
            total = space_change(flow, n, ax, ay, i, j, edge, None, None)
            upper = kx_flux(g, rkx, sp_ref, i + 1, j)
            lower = load(fk, j)
            store(fk, j, upper)
            upper_y = ky_flux(gk, aky, layers, i, j + 1)
            v = each(
                lambda a, n, t, u, v, p, q: 0.5 * ((a + n) - ((t + (u - v)) + (p - q))),
                load(np_ref, (i + 2) * BY + j), n, total, upper, lower, upper_y, lower_y,
            )
            store(q_ref, slab, v)
            lower_y = upper_y
        return carry

    lax.fori_loop(0, BX, one_kx, 0)


def halo_terms(g, low_speeds, high_speeds, low, high):
    up = [each(lambda g, w: jnp.where(g > 0, 0.5 * w, 0.0), g, w) for w in low_speeds]
    down = [each(lambda g, w: jnp.where(g > 0, 0.0, 0.5 * w), g, w) for w in high_speeds]
    end = each(lambda w, a, b: w * (3.0 * a - b), up[0], low[1], low[0])
    second = each(lambda w, a: w * a, up[1], low[1])
    top = each(lambda w, a, b: w * (3.0 * a - b), down[1], high[0], high[1])
    below_top = each(lambda w, a: w * a, down[0], high[0])
    return (
        each(lambda a, b: a + b, end, second),
        each(lambda b: -b, second),
        below_top,
        each(lambda a, b: -(a + b), top, below_top),
    )


def stage_two_outer(
    q_in, ax, rkx, aky, gx, gy, halo_speed, hold_ref, spec, kx_od, kx_ev, x2, ky_od, ky_ev,
    q_ref, out, xnear, xflux, done, sem,
):
    _, _, _, x_up, _ = place()
    flow = Flow()
    none = no_inflow(x_up)
    near = jnp.where(none, 0.0, x2[pl.ds(0, 2 * BX)])
    xnear[...] = 0.5 * near
    xflux[...] = (3.0 * near - jnp.where(none, 0.0, x2[pl.ds(2 * BX, 2 * BX)])) * (0.5 * halo_speed[...])
    kx_halo, ky_halo = Halo(kx_od, kx_ev, "kx", 2), Halo(ky_od, ky_ev, "ky", 1)

    def kx_ends(j, carry):
        g = load(gx, 0)
        speed = [each(lambda r, g: r * g, load(rkx, f * BY + j), g) for f in (0, 1, BX - 1, BX)]
        low = [kx_halo.low(l * BY + j) for l in range(2)]
        high = [kx_halo.high(l * BY + j) for l in range(2)]
        terms = halo_terms(g, speed[:2], speed[2:], low, high)
        for i, term in zip((0, 1, BX - 2, BX - 1), terms):
            slab = i * BY + j
            store(q_ref, slab, each(lambda q, t: q + t, load(q_ref, slab), term))
        return carry

    lax.fori_loop(0, BY, kx_ends, 0)
    second = flow.rows == jnp.where(x_up, 1, 6)

    def one_kx(i, carry):
        hold = each(lambda m: m == 1, load(hold_ref, 0))
        gk = load(gy, 0)
        speed = [load(aky, i * (BY + 1) + f) for f in (0, 1, BY - 1, BY)]
        low = [ky_halo.low(i * 2 + l) for l in range(2)]
        high = [ky_halo.high(i * 2 + l) for l in range(2)]
        terms = dict(zip(EDGES, halo_terms(gk, speed[:2], speed[2:], low, high)))
        for j in range(BY):
            slab = i * BY + j
            q = load(q_ref, slab)
            if j in terms:
                q = each(lambda q, t: q + t, q, terms[j])
            for b in range(2):
                less = ax[slab * T + b] * row(xnear, i, j, b)
                into = less + row(xflux, i, j, b)
                q[0][b] = q[0][b] + jnp.where(
                    flow.x_first, into, jnp.where(second, -pltpu.roll(less, flow.x_roll, 0), 0.0)
                )
            for a in range(2):
                for b in range(2):
                    done[i, j, 2 * a + b] = jnp.where(hold[a][b], spec[slab], q[a][b])
        send_out(done, out, sem, i)
        return carry

    lax.fori_loop(0, BX, one_kx, 0)
    wait_all(done, sem)


def call(kernel, outs, operands, spaces, out_spaces, scratch=(), alias=None, us=1, limit=LIMIT):
    whole = {
        "v": pl.BlockSpec(memory_space=pltpu.VMEM),
        "h": pl.BlockSpec(memory_space=pltpu.HBM),
    }
    return pl.pallas_call(
        kernel,
        out_shape=tuple(outs),
        in_specs=[whole[c] for c in spaces],
        out_specs=tuple(whole[c] for c in out_spaces),
        scratch_shapes=list(scratch),
        input_output_aliases=alias or {},
        compiler_params=pltpu.CompilerParams(vmem_limit_bytes=limit),
        cost_estimate=pl.CostEstimate(flops=int(us * 1e9), bytes_accessed=0, transcendentals=0),
        name=kernel.__name__,
    )(*operands)


def per_device(action, depth_cm, inflow_mask, inflow):
    slabs, padded = BX * BY * T, (BX + 4) * BY * T
    edge_slabs, ky_tiles, kx_tiles = BX * len(EDGES) * T, BX * 2 * T, 2 * BY * T
    sizes = [lax.axis_size(axis) for axis in AXES]

    def v(*shape):
        return pltpu.VMEM(shape + (8, 128), f32)

    def swap_odd(message, axis, spare):
        return lax.ppermute(message, AXES, swaps(sizes, AXES.index(axis), 1, AXES.index(spare)))

    def swap_even(message, axis):
        return lax.ppermute(message, AXES, swaps(sizes, AXES.index(axis), 0, 0))

    sem = pltpu.SemaphoreType.DMA
    np5, kx_od, kx_ev, x1, depth, mask, spectrum, ay = call(
        first_messages,
        (v(BX + 4, BY, T), v(kx_tiles), v(kx_tiles + SPARE), v(4 * BX + 2), pltpu.VMEM((BS, NY), jnp.int32),
         pltpu.VMEM((BS, NY), jnp.int32), pltpu.VMEM((NKX, NKY), f32), v(slabs)),
        (action, depth_cm, inflow_mask, inflow),
        "hhhh",
        "v" * 8,
        [v(T), sem((6,))],
        us=0,
        limit=FIRST_LIMIT,
    )
    next_depth = lax.ppermute(depth, AXES[:2], ring(sizes, -1))
    x1 = lax.ppermute(x1, AXES[:2], ring(sizes, 1))
    kx_od, kx_ev = swap_odd(kx_od, "kx", "space"), swap_even(kx_ev, "kx")
    ky_od, ky_ev, next_row = call(
        ky_messages,
        (v(BX, 2, T), v(BX, 2, T), pltpu.VMEM((8, NY), f32)),
        (np5, next_depth),
        "v" * 2,
        "v" * 3,
        [sem((2,))],
        us=0,
    )
    ky_od = swap_odd(ky_od, "ky", "kx").reshape(ky_tiles, 8, 128)
    ky_ev = swap_even(ky_ev, "ky").reshape(ky_tiles, 8, 128)
    np3 = np5.reshape(padded, 8, 128)
    ax, rkx, aky, gy, heights, hold, spec = call(
        speeds,
        (v(slabs), v((BX + 1) * BY * T), v(BX * (BY + 1) * T), v(T), pltpu.VMEM((BS, NY), f32),
         pltpu.VMEM((T, 8, 128), jnp.int32), v(BX * BY)),
        (depth, mask, spectrum),
        "vvv",
        "v" * 7,
        [v(2 * T)],
        us=4,
    )
    np3, part, gx, edge, halo_speed, xnear, xflux, ky2_od, ky2_ev = call(
        stage_one_edges,
        (v(padded), v(edge_slabs), v(T), v(2 * BX), v(2 * BX), v(2 * BX), v(2 * BX), v(ky_tiles), v(ky_tiles)),
        (np3, ax, ay, rkx, aky, heights, hold, spec, kx_od, x1, kx_ev, next_row),
        "v" * 12,
        "v" * 9,
        [v(len(EDGES) * T), v(4)],
        alias={0: 0},
        us=0,
    )
    ky2_od, ky2_ev = swap_odd(ky2_od, "ky", "kx"), swap_even(ky2_ev, "ky")
    sp, x2 = call(
        stage_one_rest,
        (v(padded), v(4 * BX)),
        (np3, part, ax, ay, rkx, aky, gx, gy, edge, xnear, xflux, hold, spec, ky_od, ky_ev),
        "v" * 15,
        "v" * 2,
        [v(len(MIDDLE) * T)],
        us=0,
    )
    x2 = lax.ppermute(x2, AXES[:2], ring(sizes, 1))
    sp, kx2_od, kx2_ev = call(
        kx_messages,
        (v(padded), v(kx_tiles), v(kx_tiles)),
        (sp,),
        "v",
        "v" * 3,
        [sem((2,))],
        alias={0: 0},
        us=0,
    )
    kx2_od, kx2_ev = swap_odd(kx2_od, "kx", "space"), swap_even(kx2_ev, "kx")
    (q,) = call(
        stage_two_inner,
        (v(slabs),),
        (np3, sp, ax, ay, rkx, aky, gx, gy, edge),
        "v" * 9,
        "v",
        [v(BY * T)],
        us=4,
    )
    _, out = call(
        stage_two_outer,
        (v(slabs), jax.ShapeDtypeStruct(action.shape, f32)),
        (q, ax, rkx, aky, gx, gy, halo_speed, hold, spec, kx2_od, kx2_ev, x2, ky2_od, ky2_ev),
        "v" * 14,
        "vh",
        [v(2 * BX), v(2 * BX), v(BX, BY, T), sem],
        alias={0: 0},
        us=0,
    )
    return out


def solution(mesh):
    in_specs = (P("kx", "ky", "space", None), P("space", None), P("space", None), P())
    out_specs = P("kx", "ky", "space", None)
    return jax.shard_map(
        per_device, mesh=mesh, in_specs=in_specs, out_specs=out_specs, check_vma=False
    )
```

```python
import jax
import jax.numpy as jnp
from jax import lax
from jax.experimental import pallas as pl
from jax.experimental.pallas import tpu as pltpu
from jax.sharding import PartitionSpec as P

NKX = 64
NKY = 64

gravity = 9.81
spacing = 4.0
k_step = 0.04
time_step = 0.2

BX, BY, BS, NY = 16, 8, 16, 256
T = 4
f32 = jnp.float32
LIMIT = 8 * 2**20
FIRST_LIMIT = 54 * 2**20
EDGES = (0, 1, BY - 2, BY - 1)
MIDDLE = tuple(range(2, BY - 2))

X_SCALE = time_step / spacing * 0.5
K_SCALE = time_step / k_step * 0.5


AXES = ("space", "kx", "ky")


def swaps(sizes, axis, odd, spare, against=False):
    pairs = []
    for n in range(sizes[0] * sizes[1] * sizes[2]):
        at = [n // (sizes[1] * sizes[2]), n // sizes[2] % sizes[1], n % sizes[2]]
        other = ((at[axis] + odd) ^ 1) - odd
        if 0 <= other < sizes[axis]:
            at[axis] = other
        elif against:
            at[0] = (at[0] + (1 if at[1] < sizes[1] // 2 else -1)) % sizes[0]
        else:
            at[spare] ^= 1
        pairs.append((n, (at[0] * sizes[1] + at[1]) * sizes[2] + at[2]))
    return pairs


def ring(sizes):
    pairs = []
    for a in range(sizes[0]):
        for b in range(sizes[1]):
            to = (a + (1 if b >= sizes[1] // 2 else -1)) % sizes[0]
            pairs.append((a * sizes[1] + b, to * sizes[1] + b))
    return pairs


def place():
    s, i, j = lax.axis_index("space"), lax.axis_index("kx"), lax.axis_index("ky")
    return s, i, j, i >= lax.axis_size("kx") // 2, j >= lax.axis_size("ky") // 2


def is_even(i):
    return i % 2 == 0


def loop(count, body, step):
    def several(n, carry):
        for k in range(step):
            carry = body(n * step + k, carry)
        return carry

    lax.fori_loop(0, count // step, several, 0)


class Flow:
    def __init__(self):
        _, _, _, x_up, y_up = place()
        x0 = jnp.where(x_up, 0, 8)
        y0 = jnp.where(y_up, 0, 128)
        self.x_up = x_up
        self.x = (pl.multiple_of(x0, 8), pl.multiple_of(8 - x0, 8))
        self.y = (pl.multiple_of(y0, 128), pl.multiple_of(128 - y0, 128))
        self.x_roll = jnp.where(x_up, 1, 7)
        self.y_roll = jnp.where(y_up, 1, 127)
        self.rows = lax.broadcasted_iota(jnp.int32, (8, 128), 0)
        lanes = lax.broadcasted_iota(jnp.int32, (8, 128), 1)
        self.x_first = self.rows == jnp.where(x_up, 0, 7)
        self.x_last = self.rows == jnp.where(x_up, 7, 0)
        self.y_first = lanes == jnp.where(y_up, 0, 127)

    def natural(self, a, b):
        return pl.ds(self.x[a], 8), pl.ds(self.y[b], 128)

    def before_x(self, tiles, b, halo):
        first, second = (pltpu.roll(tiles[a][b], self.x_roll, 0) for a in range(2))
        return [jnp.where(self.x_first, halo, first), jnp.where(self.x_first, first, second)]

    def before_y(self, tiles, a):
        first, second = (pltpu.roll(tiles[a][b], self.y_roll, 1) for b in range(2))
        return [jnp.where(self.y_first, 0.0, first), jnp.where(self.y_first, first, second)]

    def edge_rows(self, tiles):
        out = []
        for up, down in ((7, 0), (6, 1)):
            rows = None
            for j in range(BY):
                shift = jnp.where(self.x_up, (j - up) % 8, (j - down) % 8)
                turned = pltpu.roll(tiles[j], shift, 0)
                rows = turned if rows is None else jnp.where(self.rows == j, turned, rows)
            out.append(rows)
        return out


def load(ref, slab):
    return [[ref[slab * T + 2 * a + b] for b in range(2)] for a in range(2)]


def store(ref, slab, tiles):
    for a in range(2):
        for b in range(2):
            ref[slab * T + 2 * a + b] = tiles[a][b]


def each(fn, *grids):
    return [[fn(*(g[a][b] for g in grids)) for b in range(2)] for a in range(2)]


def row(ref, i, j, b):
    return jnp.broadcast_to(ref[i * 2 + b][j : j + 1, :], (8, 128))


def wait_all(dst, sem):
    pltpu.make_async_copy(dst, dst, sem).wait()


def shifted(h, axis, up):
    size = h.shape[axis]
    place_of = lax.broadcasted_iota(jnp.int32, h.shape, axis)
    if up:
        return jnp.where(place_of == size - 1, h, pltpu.roll(h, size - 1, axis))
    return jnp.where(place_of == 0, h, pltpu.roll(h, 1, axis))


def centre(first, i):
    return ((first + i - NKX // 2).astype(f32) + 0.5) * k_step


def lower_face(first, i):
    return (first + i - NKX // 2).astype(f32) * k_step


def wave(kx, ky):
    square = jnp.broadcast_to(kx * kx + ky * ky, (8, 128))
    inverse = lax.rsqrt(square)
    return square * inverse, inverse


def centre_rows(flow, first):
    return ((first + flow.rows - NKY // 2).astype(f32) + 0.5) * k_step


def pick(tile, j):
    return jnp.broadcast_to(tile[j : j + 1, :], (8, 128))


def group_factor(k, inverse):
    return (0.5 * X_SCALE * gravity**0.5) * inverse * lax.rsqrt(k)


def refract_factor(k):
    return (0.5 * K_SCALE * gravity**0.5) * (k * k) * lax.rsqrt(k)


def group(k, c, h):
    kh = k * h
    t = jnp.tanh(kh)
    return c * ((t + kh * (1.0 - t * t)) * lax.rsqrt(t))


def refract(k, c, h):
    t = jnp.tanh(k * h)
    return c * ((1.0 - t * t) * lax.rsqrt(t))


def first_messages(
    a_ref, depth_ref, mask_ref, inflow_ref,
    np_ref, kx_od, kx_ev, x_od, x_ev, depth, mask, inflow, ay, geo, sems,
):
    s, i, j, x_up, y_up = place()
    flow = Flow()
    own = np_ref.at[pl.ds(2, BX)]
    small = [
        pltpu.make_async_copy(src, dst, sems.at[n])
        for n, (src, dst) in enumerate(((depth_ref, depth), (mask_ref, mask), (inflow_ref, inflow)))
    ]
    for c in small:
        c.start()
    for a in range(2):
        for b in range(2):
            x, y = flow.natural(a, b)
            pltpu.make_async_copy(a_ref.at[:, :, x, y], own.at[:, :, 2 * a + b], sems.at[3]).start()
    for c in small:
        c.wait()
    h = depth[...].astype(f32) * 0.01
    hy = 0.5 * (h + jnp.where(y_up, shifted(h, 1, True), shifted(h, 1, False)))
    x_flip, y_flip = jnp.where(x_up, 0, 1), jnp.where(y_up, 0, 1)
    for a in range(2):
        for b in range(2):
            geo[(a ^ x_flip) * 2 + (b ^ y_flip)] = hy[8 * a : 8 * a + 8, 128 * b : 128 * b + 128]
    kx_first, ky_first = i * BX, j * BY

    def y_speeds(i, carry):
        kx, ky = centre(kx_first, i), centre_rows(flow, ky_first)
        k, inverse = wave(kx, ky)
        c = group_factor(k, inverse) * jnp.abs(ky)
        for j in range(BY):
            kj, cj = pick(k, j), pick(c, j)
            store(ay, i * BY + j, each(lambda h: group(kj, cj, h), load(geo, 0)))
        return carry

    loop(BX, y_speeds, 4)
    wait_all(own, sems.at[3])
    low, high = jnp.where(is_even(i), 0, BX - 2), jnp.where(is_even(i), BX - 2, 0)
    messages = [
        pltpu.make_async_copy(own.at[pl.ds(at, 2)], ref, sems.at[n])
        for n, (at, ref) in enumerate(((low, kx_od), (high, kx_ev)), 4)
    ]
    for c in messages:
        c.start()
    for b in range(2):
        y = pl.ds(flow.y[b], 128)
        first = jnp.broadcast_to(depth[0:1, y].astype(f32), (8, 128))
        last = jnp.broadcast_to(depth[BS - 1 : BS, y].astype(f32), (8, 128))
        x_od[4 * BX + b] = jnp.where(is_even(s), first, last)
        x_ev[4 * BX + b] = jnp.where(is_even(s), last, first)

    def one_kx(i, carry):
        for b in range(2):
            rows = flow.edge_rows([np_ref[i + 2, j, 2 + b] for j in range(BY)])
            for l in range(2):
                x_od[l * 2 * BX + i * 2 + b] = rows[l]
                x_ev[l * 2 * BX + i * 2 + b] = rows[l]
        return carry

    loop(BX, one_kx, 4)
    for c in messages:
        c.wait()


def ky_messages(np_in, kx_ev, np_ref, ky_od, ky_ev, sems):
    s, i, j, x_up, _ = place()
    own = np_ref.reshape(BX + 4, BY, T, 8, 128).at[pl.ds(2, BX)]
    low, high = jnp.where(is_even(j), 0, BY - 2), jnp.where(is_even(j), BY - 2, 0)
    messages = [
        pltpu.make_async_copy(own.at[:, pl.ds(at, 2)], ref, sems.at[n])
        for n, (at, ref) in enumerate(((low, ky_od), (high, ky_ev)))
    ]
    for c in messages:
        c.start()
    size = 2 * BY * T
    np_ref[pl.ds(jnp.where(is_even(i), (BX + 2) * BY * T, 0), size)] = kx_ev[...]
    for c in messages:
        c.wait()


def speeds(depth, mask, inflow, ax, rkx, aky, gy, heights, hold, spec, geo):
    _, kx_place, ky_place, x_up, y_up = place()
    flow = Flow()
    kx_first, ky_first = kx_place * BX, ky_place * BY
    h = depth[...].astype(f32) * 0.01
    heights[...] = h
    y_next, y_last = shifted(h, 1, True), shifted(h, 1, False)
    hx = 0.5 * (h + jnp.where(x_up, shifted(h, 0, True), shifted(h, 0, False)))
    slope = (y_last - y_next) * (1.0 / (2.0 * spacing))
    x_flip, y_flip = jnp.where(x_up, 0, 1), jnp.where(y_up, 0, 1)
    for a in range(2):
        for b in range(2):
            at = (a ^ x_flip) * 2 + (b ^ y_flip)
            part = (slice(8 * a, 8 * a + 8), slice(128 * b, 128 * b + 128))
            gy[at] = slope[part]
            hold[at] = mask[part]
            geo[at] = h[part]
            geo[T + at] = hx[part]

    lanes = lax.broadcasted_iota(jnp.int32, (8, NKY), 1)
    for half in range(BX // 8):
        rows = inflow[pl.ds(pl.multiple_of(kx_first + 8 * half, 8), 8), :]
        for j in range(BY):
            column = jnp.sum(jnp.where(lanes == ky_first + j, rows, 0.0), axis=1, keepdims=True)
            column = jnp.broadcast_to(column, (8, 128))
            for r in range(8):
                spec[(8 * half + r) * BY + j] = jnp.broadcast_to(column[r : r + 1, :], (8, 128))

    ky = centre_rows(flow, ky_first)
    ky_face = (ky_first + flow.rows - NKY // 2).astype(f32) * k_step

    def kx_faces(i):
        k, _ = wave(lower_face(kx_first, i), ky)
        c = refract_factor(k)
        for j in range(BY):
            kj, cj = pick(k, j), pick(c, j)
            store(rkx, i * BY + j, each(lambda h: refract(kj, cj, h), load(geo, 0)))

    def one_kx(i, carry):
        kx = centre(kx_first, i)
        k, inverse = wave(kx, ky)
        c = group_factor(k, inverse) * jnp.abs(kx)
        for j in range(BY):
            kj, cj = pick(k, j), pick(c, j)
            store(ax, i * BY + j, each(lambda h: group(kj, cj, h), load(geo, 1)))
        kx_faces(i)
        k, _ = wave(kx, ky_face)
        c = refract_factor(k)
        end, _ = wave(kx, lower_face(ky_first, BY))
        end_c = refract_factor(end)
        for j in range(BY + 1):
            kj, cj = (pick(k, j), pick(c, j)) if j < BY else (end, end_c)
            store(aky, i * (BY + 1) + j, each(lambda h, g: refract(kj, cj, h) * g, load(geo, 0), load(gy, 0)))
        return carry

    loop(BX, one_kx, 4)
    kx_faces(BX)


def space_change(flow, n, ax_ref, ay_ref, i, j, edge, halo_row, halo_flux):
    slab = i * BY + j
    ax, ay = load(ax_ref, slab), load(ay_ref, slab)
    n3 = each(lambda v: 3.0 * v, n)
    total = [[None, None], [None, None]]
    for b in range(2):
        ax[1][b] = jnp.where(flow.x_last, row(edge, i, j, b), ax[1][b])
        before = flow.before_x(n, b, 0.0 if halo_row is None else row(halo_row, i, j, b))
        out = [[ax[a][b] * (n3[a][b] - before[a])] * 2 for a in range(2)]
        into = flow.before_x(out, b, 0.0 if halo_flux is None else row(halo_flux, i, j, b))
        for a in range(2):
            total[a][b] = out[a][b] - into[a]
    for a in range(2):
        before = flow.before_y(n, a)
        out = [ay[a][b] * (n3[a][b] - before[b]) for b in range(2)]
        into = flow.before_y([out, out], 0)
        for b in range(2):
            total[a][b] = total[a][b] + (out[b] - into[b])
    return total


def face(up, speed, n_2, n_1, n1, n2):
    near = jnp.where(up, n_1, n1)
    far = jnp.where(up, n_2, n2)
    return speed * (3.0 * near - far)


def kx_flux(gx, rkx, n_ref, i, j):
    n = [load(n_ref, (i + d) * BY + j) for d in range(4)]
    return each(lambda g, r, *n: face(g > 0, r * g, *n), gx, load(rkx, i * BY + j), *n)


def ky_flux(gy, aky, layers, i, f):
    return each(lambda g, w, *n: face(g > 0, w, *n), gy, load(aky, i * (BY + 1) + f), *layers[f : f + 4])


class Halo:
    def __init__(self, od, ev, axis, flip):
        p, last = lax.axis_index(axis), lax.axis_size(axis) - 1
        middle = (last + 1) // 2
        self.od, self.ev, self.even = od, ev, is_even(p)
        self.low_empty, self.high_empty = p == 0, p == last
        self.low_at = [jnp.where(p == middle, t ^ flip, t) for t in range(T)]
        self.high_at = [jnp.where(p == middle - 1, t ^ flip, t) for t in range(T)]

    def take(self, first, second, slab, at, empty):
        def tile(t):
            r = slab * T + at[t]
            return jnp.where(empty, 0.0, jnp.where(self.even, first[r], second[r]))

        return [[tile(2 * a + b) for b in range(2)] for a in range(2)]

    def low(self, slab):
        return self.take(self.od, self.ev, slab, self.low_at, self.low_empty)

    def high(self, slab):
        return self.take(self.ev, self.od, slab, self.high_at, self.high_empty)


def no_inflow(x_up):
    s = lax.axis_index("space")
    return s == jnp.where(x_up, 0, lax.axis_size("space") - 1)


def stage_one_edges(
    np_in, ax, ay, rkx, aky, heights, hold_ref, spec, kx_od, x_od, x_ev,
    np_ref, p_ref, gx, edge, halo_speed, xnear, xflux, ky2_od, ky2_ev, fk, hrow,
):
    s, kx_place, ky_place, x_up, y_up = place()
    flow = Flow()
    kx_first, ky_first = kx_place * BX, ky_place * BY
    odd_low = is_even(kx_place)
    empty = jnp.where(odd_low, kx_place == 0, kx_place == lax.axis_size("kx") - 1)
    base = jnp.where(odd_low, 0, (BX + 2) * BY)

    def odd_side(r, carry):
        tiles = [[kx_od[r * T + 2 * (1 - a) + b] for b in range(2)] for a in range(2)]
        store(np_ref, base + r, each(lambda v: jnp.where(empty, 0.0, v), tiles))
        return carry

    loop(2 * BY, odd_side, 8)
    h = heights[...]
    x_flip, y_flip = jnp.where(x_up, 0, 1), jnp.where(y_up, 0, 1)
    none = no_inflow(x_up)
    use_od = is_even(s) == x_up
    for b in range(2):
        y = b ^ y_flip
        at = 4 * BX + y
        mine = h[:, 128 * b : 128 * b + 128]
        od, ev = x_od[at][0:1, :] * 0.01, x_ev[at][0:1, :] * 0.01
        low = jnp.where(s == 0, mine[0:1, :], jnp.where(is_even(s), od, ev))
        high = jnp.where(s == lax.axis_size("space") - 1, mine[BS - 1 : BS, :], jnp.where(is_even(s), ev, od))
        place_of = lax.broadcasted_iota(jnp.int32, (BS, 128), 0)
        before = jnp.where(place_of == 0, low, pltpu.roll(mine, 1, 0))
        after = jnp.where(place_of == BS - 1, high, pltpu.roll(mine, BS - 1, 0))
        slope = (before - after) * (1.0 / (2.0 * spacing))
        for a in range(2):
            gx[(a ^ x_flip) * 2 + y] = slope[8 * a : 8 * a + 8, :]
        face_low = jnp.broadcast_to(0.5 * (low + mine[0:1, :]), (8, 128))
        face_high = jnp.broadcast_to(0.5 * (high + mine[BS - 1 : BS, :]), (8, 128))
        hrow[y] = jnp.where(x_up, face_high, face_low)
        hrow[2 + y] = jnp.where(x_up, face_low, face_high)
    ky = ((ky_first + flow.rows - NKY // 2).astype(f32) + 0.5) * k_step

    def edges(i, carry):
        kx = centre(kx_first, i)
        k, inverse = wave(kx, ky)
        c = group_factor(k, inverse) * jnp.abs(kx)
        for b in range(2):
            at = i * 2 + b
            near = jnp.where(use_od, x_od[at], x_ev[at])
            far = jnp.where(use_od, x_od[2 * BX + at], x_ev[2 * BX + at])
            edge[at] = group(k, c, hrow[b])
            speed = group(k, c, hrow[2 + b])
            halo_speed[at] = speed
            xnear[at] = jnp.where(none, 0.0, near)
            xflux[at] = jnp.where(none, 0.0, speed * (3.0 * near - far))
        return carry

    loop(BX, edges, 8)

    g = load(gx, 0)
    for e, j in enumerate(EDGES):
        store(fk, e, kx_flux(g, rkx, np_ref, 0, j))

    def one_kx(i, carry):
        hold = each(lambda m: m == 1, load(hold_ref, 0))
        g = load(gx, 0)
        part = {}
        for e, j in enumerate(EDGES):
            n = load(np_ref, (i + 2) * BY + j)
            total = space_change(flow, n, ax, ay, i, j, edge, xnear, xflux)
            upper = kx_flux(g, rkx, np_ref, i + 1, j)
            lower = load(fk, e)
            store(fk, e, upper)
            part[j] = each(lambda n, t, u, v: n - (t + (u - v)), n, total, upper, lower)
            store(p_ref, i * len(EDGES) + e, part[j])

        def own(f, a, b):
            w = load(aky, i * (BY + 1) + f)
            a, b = (load(np_ref, (i + 2) * BY + j) for j in (a, b))
            return each(lambda w, a, b: w * (3.0 * a - b), w, a, b)

        def edge_layer(j, low, high):
            return each(lambda m, p, u, v: jnp.where(m, spec[i * BY + j], p - (u - v)), hold, part[j], high, low)

        f = [own(0, 0, 1), own(1, 1, 2), own(2, 2, 3)]
        down = [edge_layer(0, f[0], f[1]), edge_layer(1, f[1], f[2])]
        f = [own(BY - 2, BY - 3, BY - 4), own(BY - 1, BY - 2, BY - 3), own(BY, BY - 1, BY - 2)]
        up = [edge_layer(BY - 2, f[0], f[1]), edge_layer(BY - 1, f[1], f[2])]
        for l in range(2):
            store(ky2_od, i * 2 + l, each(lambda a, b: jnp.where(is_even(ky_place), a, b), down[l], up[l]))
            store(ky2_ev, i * 2 + l, each(lambda a, b: jnp.where(is_even(ky_place), b, a), down[l], up[l]))
        return carry

    loop(BX, one_kx, 4)


def ky_column(n_ref, halo, i):
    layers = [halo.low(i * 2 + l) for l in range(2)]
    layers += [load(n_ref, (i + 2) * BY + j) for j in range(BY)]
    return layers + [halo.high(i * 2 + l) for l in range(2)]


def stage_one_rest(
    np_ref, p_ref, ax, ay, rkx, aky, gx, gy, edge, xnear, xflux, hold_ref, spec, ky_od, ky_ev,
    sp_ref, x2, fk,
):
    s, kx_place, ky_place, x_up, y_up = place()
    flow = Flow()
    halo = Halo(ky_od, ky_ev, "ky", 1)
    g = load(gx, 0)
    for e, j in enumerate(MIDDLE):
        store(fk, e, kx_flux(g, rkx, np_ref, 0, j))

    def one_kx(i, carry):
        hold = each(lambda m: m == 1, load(hold_ref, 0))
        g, gk = load(gx, 0), load(gy, 0)
        layers = ky_column(np_ref, halo, i)
        lower_y = ky_flux(gk, aky, layers, i, 0)
        last = [[], []]
        for j in range(BY):
            n = layers[j + 2]
            if j in EDGES:
                p = load(p_ref, i * len(EDGES) + EDGES.index(j))
            else:
                e = MIDDLE.index(j)
                total = space_change(flow, n, ax, ay, i, j, edge, xnear, xflux)
                upper = kx_flux(g, rkx, np_ref, i + 1, j)
                lower = load(fk, e)
                store(fk, e, upper)
                p = each(lambda n, t, u, v: n - (t + (u - v)), n, total, upper, lower)
            upper_y = ky_flux(gk, aky, layers, i, j + 1)
            v = each(
                lambda m, p, u, v: jnp.where(m, spec[i * BY + j], p - (u - v)), hold, p, upper_y, lower_y
            )
            store(sp_ref, (i + 2) * BY + j, v)
            lower_y = upper_y
            for b in range(2):
                last[b].append(v[1][b])
        for b in range(2):
            rows = flow.edge_rows(last[b])
            for l in range(2):
                x2[l * 2 * BX + i * 2 + b] = rows[l]
        return carry

    loop(BX, one_kx, 4)


def kx_messages(sp_in, sp_ref, kx2_od, kx2_ev, sems):
    _, kx_place, _, _, _ = place()
    size = 2 * BY * T
    low, high = size, size + (BX - 2) * BY * T
    messages = [
        pltpu.make_async_copy(sp_ref.at[pl.ds(jnp.where(is_even(kx_place), *at), size)], ref, sems.at[n])
        for n, (ref, at) in enumerate(((kx2_od, (low, high)), (kx2_ev, (high, low))))
    ]
    for c in messages:
        c.start()
    sp_ref[pl.ds(0, size)] = jnp.zeros((size, 8, 128), f32)
    sp_ref[pl.ds((BX + 2) * BY * T, size)] = jnp.zeros((size, 8, 128), f32)
    for c in messages:
        c.wait()


STEP = 4


def send_out(buffer, out, sem, i):
    @pl.when(i % STEP == STEP - 1)
    def _():
        flow = Flow()
        rows = pl.ds(i - (STEP - 1), STEP)
        for a in range(2):
            for b in range(2):
                x, y = flow.natural(a, b)
                pltpu.make_async_copy(buffer.at[rows, :, 2 * a + b], out.at[rows, :, x, y], sem).start()


def stage_two_inner(np_ref, sp_ref, ax, ay, rkx, aky, gx, gy, edge, q_ref, fk):
    flow = Flow()
    nothing = each(lambda v: jnp.zeros_like(v), load(gx, 0))

    g = load(gx, 0)
    for j in range(BY):
        store(fk, j, kx_flux(g, rkx, sp_ref, 0, j))

    def one_kx(i, carry):
        g, gk = load(gx, 0), load(gy, 0)
        layers = [nothing] * 2 + [load(sp_ref, (i + 2) * BY + j) for j in range(BY)] + [nothing] * 2
        lower_y = ky_flux(gk, aky, layers, i, 0)
        for j in range(BY):
            slab = i * BY + j
            n = layers[j + 2]
            total = space_change(flow, n, ax, ay, i, j, edge, None, None)
            upper = kx_flux(g, rkx, sp_ref, i + 1, j)
            lower = load(fk, j)
            store(fk, j, upper)
            upper_y = ky_flux(gk, aky, layers, i, j + 1)
            v = each(
                lambda a, n, t, u, v, p, q: 0.5 * ((a + n) - ((t + (u - v)) + (p - q))),
                load(np_ref, (i + 2) * BY + j), n, total, upper, lower, upper_y, lower_y,
            )
            store(q_ref, slab, v)
            lower_y = upper_y
        return carry

    loop(BX, one_kx, 2)


def halo_terms(g, low_speeds, high_speeds, low, high):
    up = [each(lambda g, w: jnp.where(g > 0, 0.5 * w, 0.0), g, w) for w in low_speeds]
    down = [each(lambda g, w: jnp.where(g > 0, 0.0, 0.5 * w), g, w) for w in high_speeds]
    end = each(lambda w, a, b: w * (3.0 * a - b), up[0], low[1], low[0])
    second = each(lambda w, a: w * a, up[1], low[1])
    top = each(lambda w, a, b: w * (3.0 * a - b), down[1], high[0], high[1])
    below_top = each(lambda w, a: w * a, down[0], high[0])
    return (
        each(lambda a, b: a + b, end, second),
        each(lambda b: -b, second),
        below_top,
        each(lambda a, b: -(a + b), top, below_top),
    )


def stage_two_outer(
    q_in, ax, rkx, aky, gx, gy, halo_speed, hold_ref, spec, kx_od, kx_ev, x2, ky_od, ky_ev,
    q_ref, out, xnear, xflux, done, sem,
):
    _, _, _, x_up, _ = place()
    flow = Flow()
    none = no_inflow(x_up)
    near = jnp.where(none, 0.0, x2[pl.ds(0, 2 * BX)])
    xnear[...] = 0.5 * near
    xflux[...] = (3.0 * near - jnp.where(none, 0.0, x2[pl.ds(2 * BX, 2 * BX)])) * (0.5 * halo_speed[...])
    kx_halo, ky_halo = Halo(kx_od, kx_ev, "kx", 2), Halo(ky_od, ky_ev, "ky", 1)

    def kx_ends(j, carry):
        g = load(gx, 0)
        speed = [each(lambda r, g: r * g, load(rkx, f * BY + j), g) for f in (0, 1, BX - 1, BX)]
        low = [kx_halo.low(l * BY + j) for l in range(2)]
        high = [kx_halo.high(l * BY + j) for l in range(2)]
        terms = halo_terms(g, speed[:2], speed[2:], low, high)
        for i, term in zip((0, 1, BX - 2, BX - 1), terms):
            slab = i * BY + j
            store(q_ref, slab, each(lambda q, t: q + t, load(q_ref, slab), term))
        return carry

    loop(BY, kx_ends, 4)
    second = flow.rows == jnp.where(x_up, 1, 6)

    def one_kx(i, carry):
        hold = each(lambda m: m == 1, load(hold_ref, 0))
        gk = load(gy, 0)
        speed = [load(aky, i * (BY + 1) + f) for f in (0, 1, BY - 1, BY)]
        low = [ky_halo.low(i * 2 + l) for l in range(2)]
        high = [ky_halo.high(i * 2 + l) for l in range(2)]
        terms = dict(zip(EDGES, halo_terms(gk, speed[:2], speed[2:], low, high)))
        for j in range(BY):
            slab = i * BY + j
            q = load(q_ref, slab)
            if j in terms:
                q = each(lambda q, t: q + t, q, terms[j])
            for b in range(2):
                less = ax[slab * T + b] * row(xnear, i, j, b)
                into = less + row(xflux, i, j, b)
                q[0][b] = q[0][b] + jnp.where(
                    flow.x_first, into, jnp.where(second, -pltpu.roll(less, flow.x_roll, 0), 0.0)
                )
            for a in range(2):
                for b in range(2):
                    done[i, j, 2 * a + b] = jnp.where(hold[a][b], spec[slab], q[a][b])
        send_out(done, out, sem, i)
        return carry

    loop(BX, one_kx, 4)
    wait_all(done, sem)


def call(kernel, outs, operands, spaces, out_spaces, scratch=(), alias=None, us=1, limit=LIMIT):
    whole = {
        "v": pl.BlockSpec(memory_space=pltpu.VMEM),
        "h": pl.BlockSpec(memory_space=pltpu.HBM),
    }
    return pl.pallas_call(
        kernel,
        out_shape=tuple(outs),
        in_specs=[whole[c] for c in spaces],
        out_specs=tuple(whole[c] for c in out_spaces),
        scratch_shapes=list(scratch),
        input_output_aliases=alias or {},
        compiler_params=pltpu.CompilerParams(vmem_limit_bytes=limit),
        cost_estimate=pl.CostEstimate(flops=int(us * 1e9), bytes_accessed=0, transcendentals=0),
        name=kernel.__name__,
    )(*operands)


def per_device(action, depth_cm, inflow_mask, inflow):
    slabs, padded = BX * BY * T, (BX + 4) * BY * T
    edge_slabs, ky_tiles, kx_tiles = BX * len(EDGES) * T, BX * 2 * T, 2 * BY * T
    sizes = [lax.axis_size(axis) for axis in AXES]

    def v(*shape):
        return pltpu.VMEM(shape + (8, 128), f32)

    def swap_odd(message, axis, spare):
        return lax.ppermute(message, AXES, swaps(sizes, AXES.index(axis), 1, AXES.index(spare)))

    def swap_even(message, axis):
        return lax.ppermute(message, AXES, swaps(sizes, AXES.index(axis), 0, 0))

    sem = pltpu.SemaphoreType.DMA
    np5, kx_od, kx_ev, x_od, x_ev, depth, mask, spectrum, ay = call(
        first_messages,
        (v(BX + 4, BY, T), v(2, BY, T), v(2, BY, T), v(4 * BX + 2), v(4 * BX + 2), pltpu.VMEM((BS, NY), jnp.int32),
         pltpu.VMEM((BS, NY), jnp.int32), pltpu.VMEM((NKX, NKY), f32), v(slabs)),
        (action, depth_cm, inflow_mask, inflow),
        "hhhh",
        "v" * 9,
        [v(T), sem((6,))],
        us=0,
        limit=FIRST_LIMIT,
    )
    kx_ev = swap_even(kx_ev, "kx").reshape(kx_tiles, 8, 128)
    x_od = swap_odd(x_od, "space", "kx")
    x_ev = swap_even(x_ev, "space")
    kx_od = swap_odd(kx_od, "kx", "space").reshape(kx_tiles, 8, 128)
    np3, ky_od, ky_ev = call(
        ky_messages,
        (v(padded), v(BX, 2, T), v(BX, 2, T)),
        (np5.reshape(padded, 8, 128), kx_ev),
        "v" * 2,
        "v" * 3,
        [sem((2,))],
        alias={0: 0},
        us=0,
    )
    ky_od = swap_odd(ky_od, "ky", "kx").reshape(ky_tiles, 8, 128)
    ky_ev = swap_even(ky_ev, "ky").reshape(ky_tiles, 8, 128)
    ax, rkx, aky, gy, heights, hold, spec = call(
        speeds,
        (v(slabs), v((BX + 1) * BY * T), v(BX * (BY + 1) * T), v(T), pltpu.VMEM((BS, NY), f32),
         pltpu.VMEM((T, 8, 128), jnp.int32), v(BX * BY)),
        (depth, mask, spectrum),
        "vvv",
        "v" * 7,
        [v(2 * T)],
        us=4,
    )
    np3, part, gx, edge, halo_speed, xnear, xflux, ky2_od, ky2_ev = call(
        stage_one_edges,
        (v(padded), v(edge_slabs), v(T), v(2 * BX), v(2 * BX), v(2 * BX), v(2 * BX), v(ky_tiles), v(ky_tiles)),
        (np3, ax, ay, rkx, aky, heights, hold, spec, kx_od, x_od, x_ev),
        "v" * 11,
        "v" * 9,
        [v(len(EDGES) * T), v(4)],
        alias={0: 0},
        us=0,
    )
    ky2_od, ky2_ev = swap_odd(ky2_od, "ky", "kx"), swap_even(ky2_ev, "ky")
    sp, x2 = call(
        stage_one_rest,
        (v(padded), v(4 * BX)),
        (np3, part, ax, ay, rkx, aky, gx, gy, edge, xnear, xflux, hold, spec, ky_od, ky_ev),
        "v" * 15,
        "v" * 2,
        [v(len(MIDDLE) * T)],
        us=0,
    )
    x2 = lax.ppermute(x2, AXES[:2], ring(sizes))
    sp, kx2_od, kx2_ev = call(
        kx_messages,
        (v(padded), v(kx_tiles), v(kx_tiles)),
        (sp,),
        "v",
        "v" * 3,
        [sem((2,))],
        alias={0: 0},
        us=0,
    )
    kx2_od, kx2_ev = lax.ppermute(kx2_od, AXES, swaps(sizes, 1, 1, 0, True)), swap_even(kx2_ev, "kx")
    (q,) = call(
        stage_two_inner,
        (v(slabs),),
        (np3, sp, ax, ay, rkx, aky, gx, gy, edge),
        "v" * 9,
        "v",
        [v(BY * T)],
        us=4,
    )
    _, out = call(
        stage_two_outer,
        (v(slabs), jax.ShapeDtypeStruct(action.shape, f32)),
        (q, ax, rkx, aky, gx, gy, halo_speed, hold, spec, kx2_od, kx2_ev, x2, ky2_od, ky2_ev),
        "v" * 14,
        "vh",
        [v(2 * BX), v(2 * BX), v(BX, BY, T), sem],
        alias={0: 0},
        us=0,
    )
    return out


def solution(mesh):
    in_specs = (P("kx", "ky", "space", None), P("space", None), P("space", None), P())
    out_specs = P("kx", "ky", "space", None)
    return jax.shard_map(
        per_device, mesh=mesh, in_specs=in_specs, out_specs=out_specs, check_vma=False
    )
```

```python
import jax
import jax.numpy as jnp
from jax import lax
from jax.experimental import pallas as pl
from jax.experimental.pallas import tpu as pltpu
from jax.sharding import PartitionSpec as P

NKX = 64
NKY = 64

gravity = 9.81
spacing = 4.0
k_step = 0.04
time_step = 0.2

BX, BY, BS, NY = 16, 8, 16, 256
T = 4
f32 = jnp.float32
LIMIT = 8 * 2**20
FIRST_LIMIT = 54 * 2**20
EDGES = (0, 1, BY - 2, BY - 1)
MIDDLE = tuple(range(2, BY - 2))

X_SCALE = time_step / spacing * 0.5
K_SCALE = time_step / k_step * 0.5


AXES = ("space", "kx", "ky")


def swaps(sizes, axis, odd, spare, against=False):
    pairs = []
    for n in range(sizes[0] * sizes[1] * sizes[2]):
        at = [n // (sizes[1] * sizes[2]), n // sizes[2] % sizes[1], n % sizes[2]]
        other = ((at[axis] + odd) ^ 1) - odd
        if 0 <= other < sizes[axis]:
            at[axis] = other
        elif against:
            at[0] = (at[0] + (1 if at[1] < sizes[1] // 2 else -1)) % sizes[0]
        else:
            at[spare] ^= 1
        pairs.append((n, (at[0] * sizes[1] + at[1]) * sizes[2] + at[2]))
    return pairs


def ring(sizes):
    pairs = []
    for a in range(sizes[0]):
        for b in range(sizes[1]):
            to = (a + (1 if b >= sizes[1] // 2 else -1)) % sizes[0]
            pairs.append((a * sizes[1] + b, to * sizes[1] + b))
    return pairs


def place():
    s, i, j = lax.axis_index("space"), lax.axis_index("kx"), lax.axis_index("ky")
    return s, i, j, i >= lax.axis_size("kx") // 2, j >= lax.axis_size("ky") // 2


def is_even(i):
    return i % 2 == 0


def loop(count, body, step):
    def several(n, carry):
        for k in range(step):
            carry = body(n * step + k, carry)
        return carry

    lax.fori_loop(0, count // step, several, 0)


class Flow:
    def __init__(self):
        _, _, _, x_up, y_up = place()
        x0 = jnp.where(x_up, 0, 8)
        y0 = jnp.where(y_up, 0, 128)
        self.x_up = x_up
        self.x = (pl.multiple_of(x0, 8), pl.multiple_of(8 - x0, 8))
        self.y = (pl.multiple_of(y0, 128), pl.multiple_of(128 - y0, 128))
        self.x_roll = jnp.where(x_up, 1, 7)
        self.y_roll = jnp.where(y_up, 1, 127)
        self.rows = lax.broadcasted_iota(jnp.int32, (8, 128), 0)
        lanes = lax.broadcasted_iota(jnp.int32, (8, 128), 1)
        self.x_first = self.rows == jnp.where(x_up, 0, 7)
        self.x_last = self.rows == jnp.where(x_up, 7, 0)
        self.y_first = lanes == jnp.where(y_up, 0, 127)

    def natural(self, a, b):
        return pl.ds(self.x[a], 8), pl.ds(self.y[b], 128)

    def before_x(self, tiles, b, halo):
        first, second = (pltpu.roll(tiles[a][b], self.x_roll, 0) for a in range(2))
        return [jnp.where(self.x_first, halo, first), jnp.where(self.x_first, first, second)]

    def before_y(self, tiles, a):
        first, second = (pltpu.roll(tiles[a][b], self.y_roll, 1) for b in range(2))
        return [jnp.where(self.y_first, 0.0, first), jnp.where(self.y_first, first, second)]

    def edge_rows(self, tiles):
        out = []
        for up, down in ((7, 0), (6, 1)):
            rows = None
            for j in range(BY):
                shift = jnp.where(self.x_up, (j - up) % 8, (j - down) % 8)
                turned = pltpu.roll(tiles[j], shift, 0)
                rows = turned if rows is None else jnp.where(self.rows == j, turned, rows)
            out.append(rows)
        return out


def load(ref, slab):
    return [[ref[slab * T + 2 * a + b] for b in range(2)] for a in range(2)]


def store(ref, slab, tiles):
    for a in range(2):
        for b in range(2):
            ref[slab * T + 2 * a + b] = tiles[a][b]


def each(fn, *grids):
    return [[fn(*(g[a][b] for g in grids)) for b in range(2)] for a in range(2)]


def row(ref, i, j, b):
    return jnp.broadcast_to(ref[i * 2 + b][j : j + 1, :], (8, 128))


def wait_all(dst, sem):
    pltpu.make_async_copy(dst, dst, sem).wait()


def shifted(h, axis, up):
    size = h.shape[axis]
    place_of = lax.broadcasted_iota(jnp.int32, h.shape, axis)
    if up:
        return jnp.where(place_of == size - 1, h, pltpu.roll(h, size - 1, axis))
    return jnp.where(place_of == 0, h, pltpu.roll(h, 1, axis))


def centre(first, i):
    return ((first + i - NKX // 2).astype(f32) + 0.5) * k_step


def lower_face(first, i):
    return (first + i - NKX // 2).astype(f32) * k_step


def wave(kx, ky):
    square = jnp.broadcast_to(kx * kx + ky * ky, (8, 128))
    inverse = lax.rsqrt(square)
    return square * inverse, inverse


def centre_rows(flow, first):
    return ((first + flow.rows - NKY // 2).astype(f32) + 0.5) * k_step


def pick(tile, j):
    return jnp.broadcast_to(tile[j : j + 1, :], (8, 128))


def group_factor(k, inverse):
    return (0.5 * X_SCALE * gravity**0.5) * inverse * lax.rsqrt(k)


def refract_factor(k):
    return (0.5 * K_SCALE * gravity**0.5) * (k * k) * lax.rsqrt(k)


def group(k, c, h):
    kh = k * h
    t = jnp.tanh(kh)
    return c * ((t + kh * (1.0 - t * t)) * lax.rsqrt(t))


def refract(k, c, h):
    t = jnp.tanh(k * h)
    return c * ((1.0 - t * t) * lax.rsqrt(t))


def first_messages(
    a_ref, depth_ref, mask_ref, inflow_ref,
    np_ref, kx_od, kx_ev, ky_od, depth, mask, inflow, sems,
):
    s, i, j, x_up, y_up = place()
    flow = Flow()
    own = np_ref.at[pl.ds(2, BX)]
    small = [
        pltpu.make_async_copy(src, dst, sems.at[n])
        for n, (src, dst) in enumerate(((depth_ref, depth), (mask_ref, mask), (inflow_ref, inflow)))
    ]
    for c in small:
        c.start()
    for a in range(2):
        for b in range(2):
            x, y = flow.natural(a, b)
            pltpu.make_async_copy(a_ref.at[:, :, x, y], own.at[:, :, 2 * a + b], sems.at[3]).start()
    wait_all(own, sems.at[3])
    low, high = jnp.where(is_even(i), 0, BX - 2), jnp.where(is_even(i), BX - 2, 0)
    messages = [
        pltpu.make_async_copy(src, ref, sems.at[n])
        for n, (src, ref) in enumerate(
            (
                (own.at[:, pl.ds(jnp.where(is_even(j), 0, BY - 2), 2)], ky_od),
                (own.at[pl.ds(low, 2)], kx_od),
                (own.at[pl.ds(high, 2)], kx_ev),
            ),
            4,
        )
    ]
    for c in messages:
        c.start()
    for c in small + messages:
        c.wait()


def more_messages(np_in, depth, kx_ev, np_ref, ky_ev, x_od, x_ev, sem):
    s, i, j, x_up, _ = place()
    flow = Flow()
    own = np_ref.reshape(BX + 4, BY, T, 8, 128).at[pl.ds(2, BX)]
    message = pltpu.make_async_copy(own.at[:, pl.ds(jnp.where(is_even(j), BY - 2, 0), 2)], ky_ev, sem)
    message.start()
    for b in range(2):
        y = pl.ds(flow.y[b], 128)
        first = jnp.broadcast_to(depth[0:1, y].astype(f32), (8, 128))
        last = jnp.broadcast_to(depth[BS - 1 : BS, y].astype(f32), (8, 128))
        x_od[4 * BX + b] = jnp.where(is_even(s), first, last)
        x_ev[4 * BX + b] = jnp.where(is_even(s), last, first)

    def one_kx(i, carry):
        for b in range(2):
            rows = flow.edge_rows([np_ref[((i + 2) * BY + j) * T + 2 + b] for j in range(BY)])
            for l in range(2):
                x_od[l * 2 * BX + i * 2 + b] = rows[l]
                x_ev[l * 2 * BX + i * 2 + b] = rows[l]
        return carry

    loop(BX, one_kx, 4)
    size = 2 * BY * T
    np_ref[pl.ds(jnp.where(is_even(i), (BX + 2) * BY * T, 0), size)] = kx_ev[...]
    message.wait()


def speeds(depth, mask, inflow, ax, ay, rkx, aky, gy, heights, hold, spec, geo):
    _, kx_place, ky_place, x_up, y_up = place()
    flow = Flow()
    kx_first, ky_first = kx_place * BX, ky_place * BY
    h = depth[...].astype(f32) * 0.01
    heights[...] = h
    y_next, y_last = shifted(h, 1, True), shifted(h, 1, False)
    hx = 0.5 * (h + jnp.where(x_up, shifted(h, 0, True), shifted(h, 0, False)))
    hy = 0.5 * (h + jnp.where(y_up, y_next, y_last))
    slope = (y_last - y_next) * (1.0 / (2.0 * spacing))
    x_flip, y_flip = jnp.where(x_up, 0, 1), jnp.where(y_up, 0, 1)
    for a in range(2):
        for b in range(2):
            at = (a ^ x_flip) * 2 + (b ^ y_flip)
            part = (slice(8 * a, 8 * a + 8), slice(128 * b, 128 * b + 128))
            gy[at] = slope[part]
            hold[at] = mask[part]
            geo[at] = h[part]
            geo[T + at] = hx[part]
            geo[2 * T + at] = hy[part]

    lanes = lax.broadcasted_iota(jnp.int32, (8, NKY), 1)
    for half in range(BX // 8):
        rows = inflow[pl.ds(pl.multiple_of(kx_first + 8 * half, 8), 8), :]
        for j in range(BY):
            column = jnp.sum(jnp.where(lanes == ky_first + j, rows, 0.0), axis=1, keepdims=True)
            column = jnp.broadcast_to(column, (8, 128))
            for r in range(8):
                spec[(8 * half + r) * BY + j] = jnp.broadcast_to(column[r : r + 1, :], (8, 128))

    ky = centre_rows(flow, ky_first)
    ky_face = (ky_first + flow.rows - NKY // 2).astype(f32) * k_step

    def kx_faces(i):
        k, _ = wave(lower_face(kx_first, i), ky)
        c = refract_factor(k)
        for j in range(BY):
            kj, cj = pick(k, j), pick(c, j)
            store(rkx, i * BY + j, each(lambda h: refract(kj, cj, h), load(geo, 0)))

    def one_kx(i, carry):
        kx = centre(kx_first, i)
        k, inverse = wave(kx, ky)
        c = group_factor(k, inverse)
        cx, cy = c * jnp.abs(kx), c * jnp.abs(ky)
        for j in range(BY):
            kj, cxj, cyj = pick(k, j), pick(cx, j), pick(cy, j)
            store(ax, i * BY + j, each(lambda h: group(kj, cxj, h), load(geo, 1)))
            store(ay, i * BY + j, each(lambda h: group(kj, cyj, h), load(geo, 2)))
        kx_faces(i)
        k, _ = wave(kx, ky_face)
        c = refract_factor(k)
        end, _ = wave(kx, lower_face(ky_first, BY))
        end_c = refract_factor(end)
        for j in range(BY + 1):
            kj, cj = (pick(k, j), pick(c, j)) if j < BY else (end, end_c)
            store(aky, i * (BY + 1) + j, each(lambda h, g: refract(kj, cj, h) * g, load(geo, 0), load(gy, 0)))
        return carry

    loop(BX, one_kx, 4)
    kx_faces(BX)


def x_change(flow, n, ax_ref, i, j, edge, halo_row, halo_flux):
    ax = load(ax_ref, i * BY + j)
    total = [[None, None], [None, None]]
    for b in range(2):
        ax[1][b] = jnp.where(flow.x_last, row(edge, i, j, b), ax[1][b])
        before = flow.before_x(n, b, 0.0 if halo_row is None else row(halo_row, i, j, b))
        out = [[ax[a][b] * (3.0 * n[a][b] - before[a])] * 2 for a in range(2)]
        into = flow.before_x(out, b, 0.0 if halo_flux is None else row(halo_flux, i, j, b))
        for a in range(2):
            total[a][b] = out[a][b] - into[a]
    return total


def y_change(flow, n, ay_ref, i, j):
    ay = load(ay_ref, i * BY + j)
    total = [[None, None], [None, None]]
    for a in range(2):
        before = flow.before_y(n, a)
        out = [ay[a][b] * (3.0 * n[a][b] - before[b]) for b in range(2)]
        into = flow.before_y([out, out], 0)
        for b in range(2):
            total[a][b] = out[b] - into[b]
    return total


def face(up, speed, n_2, n_1, n1, n2):
    near = jnp.where(up, n_1, n1)
    far = jnp.where(up, n_2, n2)
    return speed * (3.0 * near - far)


def kx_flux(gx, rkx, n_ref, i, j):
    n = [load(n_ref, (i + d) * BY + j) for d in range(4)]
    return each(lambda g, r, *n: face(g > 0, r * g, *n), gx, load(rkx, i * BY + j), *n)


def ky_flux(gy, aky, layers, i, f):
    return each(lambda g, w, *n: face(g > 0, w, *n), gy, load(aky, i * (BY + 1) + f), *layers[f : f + 4])


class Halo:
    def __init__(self, od, ev, axis, flip):
        p, last = lax.axis_index(axis), lax.axis_size(axis) - 1
        middle = (last + 1) // 2
        self.od, self.ev, self.even = od, ev, is_even(p)
        self.low_empty, self.high_empty = p == 0, p == last
        self.low_at = [jnp.where(p == middle, t ^ flip, t) for t in range(T)]
        self.high_at = [jnp.where(p == middle - 1, t ^ flip, t) for t in range(T)]

    def take(self, first, second, slab, at, empty):
        def tile(t):
            r = slab * T + at[t]
            return jnp.where(empty, 0.0, jnp.where(self.even, first[r], second[r]))

        return [[tile(2 * a + b) for b in range(2)] for a in range(2)]

    def low(self, slab):
        return self.take(self.od, self.ev, slab, self.low_at, self.low_empty)

    def high(self, slab):
        return self.take(self.ev, self.od, slab, self.high_at, self.high_empty)


def no_inflow(x_up):
    s = lax.axis_index("space")
    return s == jnp.where(x_up, 0, lax.axis_size("space") - 1)


def stage_one_y(np_ref, ay, p_ref):
    flow = Flow()

    def one_kx(i, carry):
        for j in range(BY):
            n = load(np_ref, (i + 2) * BY + j)
            store(p_ref, i * BY + j, each(lambda n, t: n - t, n, y_change(flow, n, ay, i, j)))
        return carry

    loop(BX, one_kx, 2)


def stage_one_edges(
    np_in, p_y, ax, rkx, aky, heights, hold_ref, spec, kx_od, x_od, x_ev,
    np_ref, p_ref, gx, edge, halo_speed, xnear, xflux, ky2_od, ky2_ev, fk, hrow,
):
    s, kx_place, ky_place, x_up, y_up = place()
    flow = Flow()
    kx_first, ky_first = kx_place * BX, ky_place * BY
    odd_low = is_even(kx_place)
    empty = jnp.where(odd_low, kx_place == 0, kx_place == lax.axis_size("kx") - 1)
    base = jnp.where(odd_low, 0, (BX + 2) * BY)

    def odd_side(r, carry):
        tiles = [[kx_od[r * T + 2 * (1 - a) + b] for b in range(2)] for a in range(2)]
        store(np_ref, base + r, each(lambda v: jnp.where(empty, 0.0, v), tiles))
        return carry

    loop(2 * BY, odd_side, 8)
    h = heights[...]
    x_flip, y_flip = jnp.where(x_up, 0, 1), jnp.where(y_up, 0, 1)
    none = no_inflow(x_up)
    use_od = is_even(s) == x_up
    for b in range(2):
        y = b ^ y_flip
        at = 4 * BX + y
        mine = h[:, 128 * b : 128 * b + 128]
        od, ev = x_od[at][0:1, :] * 0.01, x_ev[at][0:1, :] * 0.01
        low = jnp.where(s == 0, mine[0:1, :], jnp.where(is_even(s), od, ev))
        high = jnp.where(s == lax.axis_size("space") - 1, mine[BS - 1 : BS, :], jnp.where(is_even(s), ev, od))
        place_of = lax.broadcasted_iota(jnp.int32, (BS, 128), 0)
        before = jnp.where(place_of == 0, low, pltpu.roll(mine, 1, 0))
        after = jnp.where(place_of == BS - 1, high, pltpu.roll(mine, BS - 1, 0))
        slope = (before - after) * (1.0 / (2.0 * spacing))
        for a in range(2):
            gx[(a ^ x_flip) * 2 + y] = slope[8 * a : 8 * a + 8, :]
        face_low = jnp.broadcast_to(0.5 * (low + mine[0:1, :]), (8, 128))
        face_high = jnp.broadcast_to(0.5 * (high + mine[BS - 1 : BS, :]), (8, 128))
        hrow[y] = jnp.where(x_up, face_high, face_low)
        hrow[2 + y] = jnp.where(x_up, face_low, face_high)
    ky = ((ky_first + flow.rows - NKY // 2).astype(f32) + 0.5) * k_step

    def edges(i, carry):
        kx = centre(kx_first, i)
        k, inverse = wave(kx, ky)
        c = group_factor(k, inverse) * jnp.abs(kx)
        for b in range(2):
            at = i * 2 + b
            near = jnp.where(use_od, x_od[at], x_ev[at])
            far = jnp.where(use_od, x_od[2 * BX + at], x_ev[2 * BX + at])
            edge[at] = group(k, c, hrow[b])
            speed = group(k, c, hrow[2 + b])
            halo_speed[at] = speed
            xnear[at] = jnp.where(none, 0.0, near)
            xflux[at] = jnp.where(none, 0.0, speed * (3.0 * near - far))
        return carry

    loop(BX, edges, 8)

    g = load(gx, 0)
    for e, j in enumerate(EDGES):
        store(fk, e, kx_flux(g, rkx, np_ref, 0, j))

    def one_kx(i, carry):
        hold = each(lambda m: m == 1, load(hold_ref, 0))
        g = load(gx, 0)
        part = {}
        for e, j in enumerate(EDGES):
            n = load(np_ref, (i + 2) * BY + j)
            total = x_change(flow, n, ax, i, j, edge, xnear, xflux)
            upper = kx_flux(g, rkx, np_ref, i + 1, j)
            lower = load(fk, e)
            store(fk, e, upper)
            part[j] = each(lambda p, t, u, v: p - (t + (u - v)), load(p_y, i * BY + j), total, upper, lower)
            store(p_ref, i * len(EDGES) + e, part[j])

        def own(f, a, b):
            w = load(aky, i * (BY + 1) + f)
            a, b = (load(np_ref, (i + 2) * BY + j) for j in (a, b))
            return each(lambda w, a, b: w * (3.0 * a - b), w, a, b)

        def edge_layer(j, low, high):
            return each(lambda m, p, u, v: jnp.where(m, spec[i * BY + j], p - (u - v)), hold, part[j], high, low)

        f = [own(0, 0, 1), own(1, 1, 2), own(2, 2, 3)]
        down = [edge_layer(0, f[0], f[1]), edge_layer(1, f[1], f[2])]
        f = [own(BY - 2, BY - 3, BY - 4), own(BY - 1, BY - 2, BY - 3), own(BY, BY - 1, BY - 2)]
        up = [edge_layer(BY - 2, f[0], f[1]), edge_layer(BY - 1, f[1], f[2])]
        for l in range(2):
            store(ky2_od, i * 2 + l, each(lambda a, b: jnp.where(is_even(ky_place), a, b), down[l], up[l]))
            store(ky2_ev, i * 2 + l, each(lambda a, b: jnp.where(is_even(ky_place), b, a), down[l], up[l]))
        return carry

    loop(BX, one_kx, 4)


def ky_column(n_ref, halo, i):
    layers = [halo.low(i * 2 + l) for l in range(2)]
    layers += [load(n_ref, (i + 2) * BY + j) for j in range(BY)]
    return layers + [halo.high(i * 2 + l) for l in range(2)]


def stage_one_middle(np_ref, p_y, ax, rkx, gx, edge, xnear, xflux, p_ref, fk):
    flow = Flow()
    g = load(gx, 0)
    for e, j in enumerate(MIDDLE):
        store(fk, e, kx_flux(g, rkx, np_ref, 0, j))

    def one_kx(i, carry):
        g = load(gx, 0)
        for e, j in enumerate(MIDDLE):
            n = load(np_ref, (i + 2) * BY + j)
            total = x_change(flow, n, ax, i, j, edge, xnear, xflux)
            upper = kx_flux(g, rkx, np_ref, i + 1, j)
            lower = load(fk, e)
            store(fk, e, upper)
            p = each(lambda p, t, u, v: p - (t + (u - v)), load(p_y, i * BY + j), total, upper, lower)
            store(p_ref, i * len(MIDDLE) + e, p)
        return carry

    loop(BX, one_kx, 4)


def stage_one_rest(np_ref, p_ref, p_middle, aky, gy, hold_ref, spec, ky_od, ky_ev, sp_ref, x2):
    flow = Flow()
    halo = Halo(ky_od, ky_ev, "ky", 1)

    def one_kx(i, carry):
        hold = each(lambda m: m == 1, load(hold_ref, 0))
        gk = load(gy, 0)
        layers = ky_column(np_ref, halo, i)
        lower_y = ky_flux(gk, aky, layers, i, 0)
        last = [[], []]
        for j in range(BY):
            if j in EDGES:
                p = load(p_ref, i * len(EDGES) + EDGES.index(j))
            else:
                p = load(p_middle, i * len(MIDDLE) + MIDDLE.index(j))
            upper_y = ky_flux(gk, aky, layers, i, j + 1)
            v = each(lambda m, p, u, v: jnp.where(m, spec[i * BY + j], p - (u - v)), hold, p, upper_y, lower_y)
            store(sp_ref, (i + 2) * BY + j, v)
            lower_y = upper_y
            for b in range(2):
                last[b].append(v[1][b])
        for b in range(2):
            rows = flow.edge_rows(last[b])
            for l in range(2):
                x2[l * 2 * BX + i * 2 + b] = rows[l]
        return carry

    loop(BX, one_kx, 4)


def kx_messages(sp_in, sp_ref, kx2_od, kx2_ev, sems):
    _, kx_place, _, _, _ = place()
    size = 2 * BY * T
    low, high = size, size + (BX - 2) * BY * T
    messages = [
        pltpu.make_async_copy(sp_ref.at[pl.ds(jnp.where(is_even(kx_place), *at), size)], ref, sems.at[n])
        for n, (ref, at) in enumerate(((kx2_od, (low, high)), (kx2_ev, (high, low))))
    ]
    for c in messages:
        c.start()
    sp_ref[pl.ds(0, size)] = jnp.zeros((size, 8, 128), f32)
    sp_ref[pl.ds((BX + 2) * BY * T, size)] = jnp.zeros((size, 8, 128), f32)
    for c in messages:
        c.wait()


STEP = 4
INNER = range(2, BX - 2)


def send_out(buffer, out, sem, first, rows, layers):
    flow = Flow()
    rows, layers = pl.ds(first, rows), pl.ds(layers[0], len(layers))
    for a in range(2):
        for b in range(2):
            x, y = flow.natural(a, b)
            pltpu.make_async_copy(buffer.at[:, :, 2 * a + b], out.at[rows, layers, x, y], sem).start()


def stage_two_inner(np_ref, sp_ref, ax, ay, rkx, aky, gx, gy, edge, q_ref, fk):
    flow = Flow()
    nothing = each(lambda v: jnp.zeros_like(v), load(gx, 0))

    g = load(gx, 0)
    for j in range(BY):
        store(fk, j, kx_flux(g, rkx, sp_ref, 0, j))

    def one_kx(i, carry):
        g, gk = load(gx, 0), load(gy, 0)
        layers = [nothing] * 2 + [load(sp_ref, (i + 2) * BY + j) for j in range(BY)] + [nothing] * 2
        lower_y = ky_flux(gk, aky, layers, i, 0)
        for j in range(BY):
            slab = i * BY + j
            n = layers[j + 2]
            total = x_change(flow, n, ax, i, j, edge, None, None)
            total = each(lambda t, u: t + u, total, y_change(flow, n, ay, i, j))
            upper = kx_flux(g, rkx, sp_ref, i + 1, j)
            lower = load(fk, j)
            store(fk, j, upper)
            upper_y = ky_flux(gk, aky, layers, i, j + 1)
            v = each(
                lambda a, n, t, u, v, p, q: 0.5 * ((a + n) - ((t + (u - v)) + (p - q))),
                load(np_ref, (i + 2) * BY + j), n, total, upper, lower, upper_y, lower_y,
            )
            store(q_ref, slab, v)
            lower_y = upper_y
        return carry

    loop(BX, one_kx, 2)


def halo_terms(g, low_speeds, high_speeds, low, high):
    up = [each(lambda g, w: jnp.where(g > 0, 0.5 * w, 0.0), g, w) for w in low_speeds]
    down = [each(lambda g, w: jnp.where(g > 0, 0.0, 0.5 * w), g, w) for w in high_speeds]
    end = each(lambda w, a, b: w * (3.0 * a - b), up[0], low[1], low[0])
    second = each(lambda w, a: w * a, up[1], low[1])
    top = each(lambda w, a, b: w * (3.0 * a - b), down[1], high[0], high[1])
    below_top = each(lambda w, a: w * a, down[0], high[0])
    return (
        each(lambda a, b: a + b, end, second),
        each(lambda b: -b, second),
        below_top,
        each(lambda a, b: -(a + b), top, below_top),
    )


def stage_two_x(q_in, ax, halo_speed, hold_ref, spec, x2, q_ref, out, xnear, xflux, done, sem):
    _, _, _, x_up, _ = place()
    flow = Flow()
    none = no_inflow(x_up)
    near = jnp.where(none, 0.0, x2[pl.ds(0, 2 * BX)])
    xnear[...] = 0.5 * near
    xflux[...] = (3.0 * near - jnp.where(none, 0.0, x2[pl.ds(2 * BX, 2 * BX)])) * (0.5 * halo_speed[...])
    second = flow.rows == jnp.where(x_up, 1, 6)

    def one_kx(i, inner):
        hold = each(lambda m: m == 1, load(hold_ref, 0))
        for j in range(BY):
            slab = i * BY + j
            q = load(q_ref, slab)
            for b in range(2):
                less = ax[slab * T + b] * row(xnear, i, j, b)
                into = less + row(xflux, i, j, b)
                q[0][b] = q[0][b] + jnp.where(
                    flow.x_first, into, jnp.where(second, -pltpu.roll(less, flow.x_roll, 0), 0.0)
                )
            if inner and j in MIDDLE:
                for a in range(2):
                    for b in range(2):
                        done[i - INNER[0], j - MIDDLE[0], 2 * a + b] = jnp.where(hold[a][b], spec[slab], q[a][b])
            else:
                for b in range(2):
                    q_ref[slab * T + b] = q[0][b]

    def several(n, carry):
        first = INNER[0] + n * STEP
        for k in range(STEP):
            one_kx(first + k, True)
        send_out(done.at[pl.ds(n * STEP, STEP)], out, sem, first, STEP, MIDDLE)
        return carry

    lax.fori_loop(0, len(INNER) // STEP, several, 0)
    for i in (0, 1, BX - 2, BX - 1):
        one_kx(i, False)
    wait_all(done, sem)


def stage_two_ends(
    q_in, rkx, aky, gx, gy, hold_ref, spec, kx_od, kx_ev, ky_od, ky_ev, out_in,
    q_ref, out, done, ends, sems,
):
    kx_halo, ky_halo = Halo(kx_od, kx_ev, "kx", 2), Halo(ky_od, ky_ev, "ky", 1)

    def kx_ends(j, carry):
        g = load(gx, 0)
        speed = [each(lambda r, g: r * g, load(rkx, f * BY + j), g) for f in (0, 1, BX - 1, BX)]
        low = [kx_halo.low(l * BY + j) for l in range(2)]
        high = [kx_halo.high(l * BY + j) for l in range(2)]
        terms = halo_terms(g, speed[:2], speed[2:], low, high)
        for i, term in zip((0, 1, BX - 2, BX - 1), terms):
            slab = i * BY + j
            store(q_ref, slab, each(lambda q, t: q + t, load(q_ref, slab), term))
        return carry

    loop(BY, kx_ends, 4)
    hold = each(lambda m: m == 1, load(hold_ref, 0))
    for e, i in enumerate((0, 1, BX - 2, BX - 1)):
        for j in MIDDLE:
            slab = i * BY + j
            q = load(q_ref, slab)
            for a in range(2):
                for b in range(2):
                    ends[e, j - MIDDLE[0], 2 * a + b] = jnp.where(hold[a][b], spec[slab], q[a][b])
    send_out(ends.at[pl.ds(0, 2)], out, sems.at[0], 0, 2, MIDDLE)
    send_out(ends.at[pl.ds(2, 2)], out, sems.at[0], BX - 2, 2, MIDDLE)

    def one_kx(i):
        hold = each(lambda m: m == 1, load(hold_ref, 0))
        gk = load(gy, 0)
        speed = [load(aky, i * (BY + 1) + f) for f in (0, 1, BY - 1, BY)]
        low = [ky_halo.low(i * 2 + l) for l in range(2)]
        high = [ky_halo.high(i * 2 + l) for l in range(2)]
        for e, (j, term) in enumerate(zip(EDGES, halo_terms(gk, speed[:2], speed[2:], low, high))):
            slab = i * BY + j
            q = each(lambda q, t: q + t, load(q_ref, slab), term)
            for a in range(2):
                for b in range(2):
                    done[i, e, 2 * a + b] = jnp.where(hold[a][b], spec[slab], q[a][b])

    def several(n, carry):
        for k in range(STEP):
            one_kx(n * STEP + k)
        rows = done.at[pl.ds(n * STEP, STEP)]
        send_out(rows.at[:, pl.ds(0, 2)], out, sems.at[1], n * STEP, STEP, EDGES[:2])
        send_out(rows.at[:, pl.ds(2, 2)], out, sems.at[1], n * STEP, STEP, EDGES[2:])
        return carry

    lax.fori_loop(0, BX // STEP, several, 0)
    wait_all(ends, sems.at[0])
    wait_all(done, sems.at[1])


def call(kernel, outs, operands, spaces, out_spaces, scratch=(), alias=None, us=1, limit=LIMIT):
    whole = {
        "v": pl.BlockSpec(memory_space=pltpu.VMEM),
        "h": pl.BlockSpec(memory_space=pltpu.HBM),
    }
    return pl.pallas_call(
        kernel,
        out_shape=tuple(outs),
        in_specs=[whole[c] for c in spaces],
        out_specs=tuple(whole[c] for c in out_spaces),
        scratch_shapes=list(scratch),
        input_output_aliases=alias or {},
        compiler_params=pltpu.CompilerParams(vmem_limit_bytes=limit),
        cost_estimate=pl.CostEstimate(flops=int(us * 1e9), bytes_accessed=0, transcendentals=0),
        name=kernel.__name__,
    )(*operands)


def per_device(action, depth_cm, inflow_mask, inflow):
    slabs, padded = BX * BY * T, (BX + 4) * BY * T
    edge_slabs, ky_tiles, kx_tiles = BX * len(EDGES) * T, BX * 2 * T, 2 * BY * T
    sizes = [lax.axis_size(axis) for axis in AXES]

    def v(*shape):
        return pltpu.VMEM(shape + (8, 128), f32)

    def swap_odd(message, axis, spare):
        return lax.ppermute(message, AXES, swaps(sizes, AXES.index(axis), 1, AXES.index(spare)))

    def swap_even(message, axis):
        return lax.ppermute(message, AXES, swaps(sizes, AXES.index(axis), 0, 0))

    sem = pltpu.SemaphoreType.DMA
    np5, kx_od, kx_ev, ky_od, depth, mask, spectrum = call(
        first_messages,
        (v(BX + 4, BY, T), v(2, BY, T), v(2, BY, T), v(BX, 2, T), pltpu.VMEM((BS, NY), jnp.int32),
         pltpu.VMEM((BS, NY), jnp.int32), pltpu.VMEM((NKX, NKY), f32)),
        (action, depth_cm, inflow_mask, inflow),
        "hhhh",
        "v" * 7,
        [sem((7,))],
        us=0,
        limit=FIRST_LIMIT,
    )
    ky_od = swap_odd(ky_od, "ky", "kx").reshape(ky_tiles, 8, 128)
    kx_ev = swap_even(kx_ev, "kx").reshape(kx_tiles, 8, 128)
    kx_od = swap_odd(kx_od, "kx", "space").reshape(kx_tiles, 8, 128)
    np3, ky_ev, x_od, x_ev = call(
        more_messages,
        (v(padded), v(BX, 2, T), v(4 * BX + 2), v(4 * BX + 2)),
        (np5.reshape(padded, 8, 128), depth, kx_ev),
        "v" * 3,
        "v" * 4,
        [sem],
        alias={0: 0},
        us=0,
    )
    x_od, x_ev = swap_odd(x_od, "space", "kx"), swap_even(x_ev, "space")
    ky_ev = swap_even(ky_ev, "ky").reshape(ky_tiles, 8, 128)
    ax, ay, rkx, aky, gy, heights, hold, spec = call(
        speeds,
        (v(slabs), v(slabs), v((BX + 1) * BY * T), v(BX * (BY + 1) * T), v(T), pltpu.VMEM((BS, NY), f32),
         pltpu.VMEM((T, 8, 128), jnp.int32), v(BX * BY)),
        (depth, mask, spectrum),
        "vvv",
        "v" * 8,
        [v(3 * T)],
        us=3,
    )
    (p_y,) = call(stage_one_y, (v(slabs),), (np3, ay), "vv", "v", us=1)
    np3, part, gx, edge, halo_speed, xnear, xflux, ky2_od, ky2_ev = call(
        stage_one_edges,
        (v(padded), v(edge_slabs), v(T), v(2 * BX), v(2 * BX), v(2 * BX), v(2 * BX), v(ky_tiles), v(ky_tiles)),
        (np3, p_y, ax, rkx, aky, heights, hold, spec, kx_od, x_od, x_ev),
        "v" * 11,
        "v" * 9,
        [v(len(EDGES) * T), v(4)],
        alias={0: 0},
        us=0,
    )
    ky2_od, ky2_ev = swap_odd(ky2_od, "ky", "kx"), swap_even(ky2_ev, "ky")
    (p_middle,) = call(
        stage_one_middle,
        (v(BX * len(MIDDLE) * T),),
        (np3, p_y, ax, rkx, gx, edge, xnear, xflux),
        "v" * 8,
        "v",
        [v(len(MIDDLE) * T)],
        us=2,
    )
    sp, x2 = call(
        stage_one_rest,
        (v(padded), v(4 * BX)),
        (np3, part, p_middle, aky, gy, hold, spec, ky_od, ky_ev),
        "v" * 9,
        "v" * 2,
        us=0,
    )
    x2 = lax.ppermute(x2, AXES[:2], ring(sizes))
    sp, kx2_od, kx2_ev = call(
        kx_messages,
        (v(padded), v(kx_tiles), v(kx_tiles)),
        (sp,),
        "v",
        "v" * 3,
        [sem((2,))],
        alias={0: 0},
        us=0,
    )
    kx2_od, kx2_ev = lax.ppermute(kx2_od, AXES, swaps(sizes, 1, 1, 0, True)), swap_even(kx2_ev, "kx")
    (q,) = call(
        stage_two_inner,
        (v(slabs),),
        (np3, sp, ax, ay, rkx, aky, gx, gy, edge),
        "v" * 9,
        "v",
        [v(BY * T)],
        us=4,
    )
    q, out = call(
        stage_two_x,
        (v(slabs), jax.ShapeDtypeStruct(action.shape, f32)),
        (q, ax, halo_speed, hold, spec, x2),
        "v" * 6,
        "vh",
        [v(2 * BX), v(2 * BX), v(len(INNER), len(MIDDLE), T), sem],
        alias={0: 0},
        us=2,
    )
    _, out = call(
        stage_two_ends,
        (v(slabs), jax.ShapeDtypeStruct(action.shape, f32)),
        (q, rkx, aky, gx, gy, hold, spec, kx2_od, kx2_ev, ky2_od, ky2_ev, out),
        "v" * 11 + "h",
        "vh",
        [v(BX, len(EDGES), T), v(4, len(MIDDLE), T), sem((2,))],
        alias={0: 0, 11: 1},
        us=0,
    )
    return out


def solution(mesh):
    in_specs = (P("kx", "ky", "space", None), P("space", None), P("space", None), P())
    out_specs = P("kx", "ky", "space", None)
    return jax.shard_map(
        per_device, mesh=mesh, in_specs=in_specs, out_specs=out_specs, check_vma=False
    )
```

```python
import jax
import jax.numpy as jnp
from jax import lax
from jax.experimental import pallas as pl
from jax.experimental.pallas import tpu as pltpu
from jax.sharding import PartitionSpec as P

NKX = 64
NKY = 64

gravity = 9.81
spacing = 4.0
k_step = 0.04
time_step = 0.2

BX, BY, BS, NY = 16, 8, 16, 256
T = 4
f32 = jnp.float32
LIMIT = 8 * 2**20
FIRST_LIMIT = 54 * 2**20
EDGES = (0, 1, BY - 2, BY - 1)
MIDDLE = tuple(range(2, BY - 2))

X_SCALE = time_step / spacing * 0.5
K_SCALE = time_step / k_step * 0.5


AXES = ("space", "kx", "ky")


def swaps(sizes, axis, odd, spare, against=False):
    pairs = []
    for n in range(sizes[0] * sizes[1] * sizes[2]):
        at = [n // (sizes[1] * sizes[2]), n // sizes[2] % sizes[1], n % sizes[2]]
        other = ((at[axis] + odd) ^ 1) - odd
        if 0 <= other < sizes[axis]:
            at[axis] = other
        elif against:
            at[0] = (at[0] + (1 if at[1] < sizes[1] // 2 else -1)) % sizes[0]
        else:
            at[spare] ^= 1
        pairs.append((n, (at[0] * sizes[1] + at[1]) * sizes[2] + at[2]))
    return pairs


def ring(sizes):
    pairs = []
    for a in range(sizes[0]):
        for b in range(sizes[1]):
            to = (a + (1 if b >= sizes[1] // 2 else -1)) % sizes[0]
            pairs.append((a * sizes[1] + b, to * sizes[1] + b))
    return pairs


def place():
    s, i, j = lax.axis_index("space"), lax.axis_index("kx"), lax.axis_index("ky")
    return s, i, j, i >= lax.axis_size("kx") // 2, j >= lax.axis_size("ky") // 2


def is_even(i):
    return i % 2 == 0


def loop(count, body, step):
    def several(n, carry):
        for k in range(step):
            carry = body(n * step + k, carry)
        return carry

    lax.fori_loop(0, count // step, several, 0)


class Flow:
    def __init__(self):
        _, _, _, x_up, y_up = place()
        x0 = jnp.where(x_up, 0, 8)
        y0 = jnp.where(y_up, 0, 128)
        self.x_up = x_up
        self.x = (pl.multiple_of(x0, 8), pl.multiple_of(8 - x0, 8))
        self.y = (pl.multiple_of(y0, 128), pl.multiple_of(128 - y0, 128))
        self.x_roll = jnp.where(x_up, 1, 7)
        self.y_roll = jnp.where(y_up, 1, 127)
        self.rows = lax.broadcasted_iota(jnp.int32, (8, 128), 0)
        lanes = lax.broadcasted_iota(jnp.int32, (8, 128), 1)
        self.x_first = self.rows == jnp.where(x_up, 0, 7)
        self.x_last = self.rows == jnp.where(x_up, 7, 0)
        self.y_first = lanes == jnp.where(y_up, 0, 127)

    def natural(self, a, b):
        return pl.ds(self.x[a], 8), pl.ds(self.y[b], 128)

    def before_x(self, tiles, b, halo):
        first, second = (pltpu.roll(tiles[a][b], self.x_roll, 0) for a in range(2))
        return [jnp.where(self.x_first, halo, first), jnp.where(self.x_first, first, second)]

    def before_y(self, tiles, a):
        first, second = (pltpu.roll(tiles[a][b], self.y_roll, 1) for b in range(2))
        return [jnp.where(self.y_first, 0.0, first), jnp.where(self.y_first, first, second)]

    def edge_rows(self, tiles):
        out = []
        for up, down in ((7, 0), (6, 1)):
            rows = None
            for j in range(BY):
                shift = jnp.where(self.x_up, (j - up) % 8, (j - down) % 8)
                turned = pltpu.roll(tiles[j], shift, 0)
                rows = turned if rows is None else jnp.where(self.rows == j, turned, rows)
            out.append(rows)
        return out


def load(ref, slab):
    return [[ref[slab * T + 2 * a + b] for b in range(2)] for a in range(2)]


def store(ref, slab, tiles):
    for a in range(2):
        for b in range(2):
            ref[slab * T + 2 * a + b] = tiles[a][b]


def each(fn, *grids):
    return [[fn(*(g[a][b] for g in grids)) for b in range(2)] for a in range(2)]


def row(ref, i, j, b):
    return jnp.broadcast_to(ref[i * 2 + b][j : j + 1, :], (8, 128))


def wait_all(dst, sem):
    pltpu.make_async_copy(dst, dst, sem).wait()


def shifted(h, axis, up):
    size = h.shape[axis]
    place_of = lax.broadcasted_iota(jnp.int32, h.shape, axis)
    if up:
        return jnp.where(place_of == size - 1, h, pltpu.roll(h, size - 1, axis))
    return jnp.where(place_of == 0, h, pltpu.roll(h, 1, axis))


def centre(first, i):
    return ((first + i - NKX // 2).astype(f32) + 0.5) * k_step


def lower_face(first, i):
    return (first + i - NKX // 2).astype(f32) * k_step


def wave(kx, ky):
    square = jnp.broadcast_to(kx * kx + ky * ky, (8, 128))
    inverse = lax.rsqrt(square)
    return square * inverse, inverse


def centre_rows(flow, first):
    return ((first + flow.rows - NKY // 2).astype(f32) + 0.5) * k_step


def pick(tile, j):
    return jnp.broadcast_to(tile[j : j + 1, :], (8, 128))


def group_factor(k, inverse):
    return (0.5 * X_SCALE * gravity**0.5) * inverse * lax.rsqrt(k)


def refract_factor(k):
    return (0.5 * K_SCALE * gravity**0.5) * (k * k) * lax.rsqrt(k)


def group(k, c, h):
    kh = k * h
    t = jnp.tanh(kh)
    return c * ((t + kh * (1.0 - t * t)) * lax.rsqrt(t))


def refract(k, c, h):
    t = jnp.tanh(k * h)
    return c * ((1.0 - t * t) * lax.rsqrt(t))


def first_messages(
    a_ref, depth_ref, mask_ref, inflow_ref,
    np_ref, kx_od, kx_ev, ky_od, depth, mask, inflow, sems,
):
    s, i, j, x_up, y_up = place()
    flow = Flow()
    own = np_ref.at[pl.ds(2, BX)]
    small = [
        pltpu.make_async_copy(src, dst, sems.at[n])
        for n, (src, dst) in enumerate(((depth_ref, depth), (mask_ref, mask), (inflow_ref, inflow)))
    ]
    for c in small:
        c.start()
    for a in range(2):
        for b in range(2):
            x, y = flow.natural(a, b)
            pltpu.make_async_copy(a_ref.at[:, :, x, y], own.at[:, :, 2 * a + b], sems.at[3]).start()
    wait_all(own, sems.at[3])
    low, high = jnp.where(is_even(i), 0, BX - 2), jnp.where(is_even(i), BX - 2, 0)
    messages = [
        pltpu.make_async_copy(src, ref, sems.at[n])
        for n, (src, ref) in enumerate(
            (
                (own.at[:, pl.ds(jnp.where(is_even(j), 0, BY - 2), 2)], ky_od),
                (own.at[pl.ds(low, 2)], kx_od),
                (own.at[pl.ds(high, 2)], kx_ev),
            ),
            4,
        )
    ]
    for c in messages:
        c.start()
    for c in small + messages:
        c.wait()


def more_messages(np_in, depth, kx_ev, np_ref, ky_ev, x_od, x_ev, sem):
    s, i, j, x_up, _ = place()
    flow = Flow()
    own = np_ref.reshape(BX + 4, BY, T, 8, 128).at[pl.ds(2, BX)]
    message = pltpu.make_async_copy(own.at[:, pl.ds(jnp.where(is_even(j), BY - 2, 0), 2)], ky_ev, sem)
    message.start()
    for b in range(2):
        y = pl.ds(flow.y[b], 128)
        first = jnp.broadcast_to(depth[0:1, y].astype(f32), (8, 128))
        last = jnp.broadcast_to(depth[BS - 1 : BS, y].astype(f32), (8, 128))
        x_od[4 * BX + b] = jnp.where(is_even(s), first, last)
        x_ev[4 * BX + b] = jnp.where(is_even(s), last, first)

    def one_kx(i, carry):
        for b in range(2):
            rows = flow.edge_rows([np_ref[((i + 2) * BY + j) * T + 2 + b] for j in range(BY)])
            for l in range(2):
                x_od[l * 2 * BX + i * 2 + b] = rows[l]
                x_ev[l * 2 * BX + i * 2 + b] = rows[l]
        return carry

    loop(BX, one_kx, 4)
    size = 2 * BY * T
    np_ref[pl.ds(jnp.where(is_even(i), (BX + 2) * BY * T, 0), size)] = kx_ev[...]
    message.wait()


def speeds(depth, mask, inflow, ax, ay, rkx, aky, gy, heights, hold, spec, geo):
    _, kx_place, ky_place, x_up, y_up = place()
    flow = Flow()
    kx_first, ky_first = kx_place * BX, ky_place * BY
    h = depth[...].astype(f32) * 0.01
    heights[...] = h
    y_next, y_last = shifted(h, 1, True), shifted(h, 1, False)
    hx = 0.5 * (h + jnp.where(x_up, shifted(h, 0, True), shifted(h, 0, False)))
    hy = 0.5 * (h + jnp.where(y_up, y_next, y_last))
    slope = (y_last - y_next) * (1.0 / (2.0 * spacing))
    x_flip, y_flip = jnp.where(x_up, 0, 1), jnp.where(y_up, 0, 1)
    for a in range(2):
        for b in range(2):
            at = (a ^ x_flip) * 2 + (b ^ y_flip)
            part = (slice(8 * a, 8 * a + 8), slice(128 * b, 128 * b + 128))
            gy[at] = slope[part]
            hold[at] = mask[part]
            geo[at] = h[part]
            geo[T + at] = hx[part]
            geo[2 * T + at] = hy[part]

    lanes = lax.broadcasted_iota(jnp.int32, (8, NKY), 1)
    for half in range(BX // 8):
        rows = inflow[pl.ds(pl.multiple_of(kx_first + 8 * half, 8), 8), :]
        for j in range(BY):
            column = jnp.sum(jnp.where(lanes == ky_first + j, rows, 0.0), axis=1, keepdims=True)
            column = jnp.broadcast_to(column, (8, 128))
            for r in range(8):
                spec[(8 * half + r) * BY + j] = jnp.broadcast_to(column[r : r + 1, :], (8, 128))

    ky = centre_rows(flow, ky_first)
    ky_face = (ky_first + flow.rows - NKY // 2).astype(f32) * k_step

    def kx_faces(i):
        k, _ = wave(lower_face(kx_first, i), ky)
        c = refract_factor(k)
        for j in range(BY):
            kj, cj = pick(k, j), pick(c, j)
            store(rkx, i * BY + j, each(lambda h: refract(kj, cj, h), load(geo, 0)))

    def one_kx(i, carry):
        kx = centre(kx_first, i)
        k, inverse = wave(kx, ky)
        c = group_factor(k, inverse)
        cx, cy = c * jnp.abs(kx), c * jnp.abs(ky)
        for j in range(BY):
            kj, cxj, cyj = pick(k, j), pick(cx, j), pick(cy, j)
            store(ax, i * BY + j, each(lambda h: group(kj, cxj, h), load(geo, 1)))
            store(ay, i * BY + j, each(lambda h: group(kj, cyj, h), load(geo, 2)))
        kx_faces(i)
        k, _ = wave(kx, ky_face)
        c = refract_factor(k)
        end, _ = wave(kx, lower_face(ky_first, BY))
        end_c = refract_factor(end)
        for j in range(BY + 1):
            kj, cj = (pick(k, j), pick(c, j)) if j < BY else (end, end_c)
            store(aky, i * (BY + 1) + j, each(lambda h, g: refract(kj, cj, h) * g, load(geo, 0), load(gy, 0)))
        return carry

    loop(BX, one_kx, 4)
    kx_faces(BX)


def x_change(flow, n, ax_ref, i, j, edge, halo_row, halo_flux):
    ax = load(ax_ref, i * BY + j)
    total = [[None, None], [None, None]]
    for b in range(2):
        ax[1][b] = jnp.where(flow.x_last, row(edge, i, j, b), ax[1][b])
        before = flow.before_x(n, b, 0.0 if halo_row is None else row(halo_row, i, j, b))
        out = [[ax[a][b] * (3.0 * n[a][b] - before[a])] * 2 for a in range(2)]
        into = flow.before_x(out, b, 0.0 if halo_flux is None else row(halo_flux, i, j, b))
        for a in range(2):
            total[a][b] = out[a][b] - into[a]
    return total


def y_change(flow, n, ay_ref, i, j):
    ay = load(ay_ref, i * BY + j)
    total = [[None, None], [None, None]]
    for a in range(2):
        before = flow.before_y(n, a)
        out = [ay[a][b] * (3.0 * n[a][b] - before[b]) for b in range(2)]
        into = flow.before_y([out, out], 0)
        for b in range(2):
            total[a][b] = out[b] - into[b]
    return total


def face(up, speed, n_2, n_1, n1, n2):
    near = jnp.where(up, n_1, n1)
    far = jnp.where(up, n_2, n2)
    return speed * (3.0 * near - far)


def kx_flux(gx, rkx, n_ref, i, j):
    n = [load(n_ref, (i + d) * BY + j) for d in range(4)]
    return each(lambda g, r, *n: face(g > 0, r * g, *n), gx, load(rkx, i * BY + j), *n)


def ky_flux(gy, aky, layers, i, f):
    return each(lambda g, w, *n: face(g > 0, w, *n), gy, load(aky, i * (BY + 1) + f), *layers[f : f + 4])


class Halo:
    def __init__(self, od, ev, axis, flip):
        p, last = lax.axis_index(axis), lax.axis_size(axis) - 1
        middle = (last + 1) // 2
        self.od, self.ev, self.even = od, ev, is_even(p)
        self.low_empty, self.high_empty = p == 0, p == last
        self.low_at = [jnp.where(p == middle, t ^ flip, t) for t in range(T)]
        self.high_at = [jnp.where(p == middle - 1, t ^ flip, t) for t in range(T)]

    def take(self, first, second, slab, at, empty):
        def tile(t):
            r = slab * T + at[t]
            return jnp.where(empty, 0.0, jnp.where(self.even, first[r], second[r]))

        return [[tile(2 * a + b) for b in range(2)] for a in range(2)]

    def low(self, slab):
        return self.take(self.od, self.ev, slab, self.low_at, self.low_empty)

    def high(self, slab):
        return self.take(self.ev, self.od, slab, self.high_at, self.high_empty)


def no_inflow(x_up):
    s = lax.axis_index("space")
    return s == jnp.where(x_up, 0, lax.axis_size("space") - 1)


def stage_one_y(np_ref, ay, p_ref):
    flow = Flow()

    def one_kx(i, carry):
        for j in range(BY):
            n = load(np_ref, (i + 2) * BY + j)
            store(p_ref, i * BY + j, each(lambda n, t: n - t, n, y_change(flow, n, ay, i, j)))
        return carry

    loop(BX, one_kx, 2)


def stage_one_edges(
    np_in, p_y, ax, rkx, aky, heights, hold_ref, spec, kx_od, x_od, x_ev,
    np_ref, p_ref, gx, edge, halo_speed, xnear, xflux, ky2_od, ky2_ev, fk, hrow,
):
    s, kx_place, ky_place, x_up, y_up = place()
    flow = Flow()
    kx_first, ky_first = kx_place * BX, ky_place * BY
    odd_low = is_even(kx_place)
    empty = jnp.where(odd_low, kx_place == 0, kx_place == lax.axis_size("kx") - 1)
    base = jnp.where(odd_low, 0, (BX + 2) * BY)

    def odd_side(r, carry):
        tiles = [[kx_od[r * T + 2 * (1 - a) + b] for b in range(2)] for a in range(2)]
        store(np_ref, base + r, each(lambda v: jnp.where(empty, 0.0, v), tiles))
        return carry

    loop(2 * BY, odd_side, 8)
    h = heights[...]
    x_flip, y_flip = jnp.where(x_up, 0, 1), jnp.where(y_up, 0, 1)
    none = no_inflow(x_up)
    use_od = is_even(s) == x_up
    for b in range(2):
        y = b ^ y_flip
        at = 4 * BX + y
        mine = h[:, 128 * b : 128 * b + 128]
        od, ev = x_od[at][0:1, :] * 0.01, x_ev[at][0:1, :] * 0.01
        low = jnp.where(s == 0, mine[0:1, :], jnp.where(is_even(s), od, ev))
        high = jnp.where(s == lax.axis_size("space") - 1, mine[BS - 1 : BS, :], jnp.where(is_even(s), ev, od))
        place_of = lax.broadcasted_iota(jnp.int32, (BS, 128), 0)
        before = jnp.where(place_of == 0, low, pltpu.roll(mine, 1, 0))
        after = jnp.where(place_of == BS - 1, high, pltpu.roll(mine, BS - 1, 0))
        slope = (before - after) * (1.0 / (2.0 * spacing))
        for a in range(2):
            gx[(a ^ x_flip) * 2 + y] = slope[8 * a : 8 * a + 8, :]
        face_low = jnp.broadcast_to(0.5 * (low + mine[0:1, :]), (8, 128))
        face_high = jnp.broadcast_to(0.5 * (high + mine[BS - 1 : BS, :]), (8, 128))
        hrow[y] = jnp.where(x_up, face_high, face_low)
        hrow[2 + y] = jnp.where(x_up, face_low, face_high)
    ky = ((ky_first + flow.rows - NKY // 2).astype(f32) + 0.5) * k_step

    def edges(i, carry):
        kx = centre(kx_first, i)
        k, inverse = wave(kx, ky)
        c = group_factor(k, inverse) * jnp.abs(kx)
        for b in range(2):
            at = i * 2 + b
            near = jnp.where(use_od, x_od[at], x_ev[at])
            far = jnp.where(use_od, x_od[2 * BX + at], x_ev[2 * BX + at])
            edge[at] = group(k, c, hrow[b])
            speed = group(k, c, hrow[2 + b])
            halo_speed[at] = speed
            xnear[at] = jnp.where(none, 0.0, near)
            xflux[at] = jnp.where(none, 0.0, speed * (3.0 * near - far))
        return carry

    loop(BX, edges, 8)

    g = load(gx, 0)
    for e, j in enumerate(EDGES):
        store(fk, e, kx_flux(g, rkx, np_ref, 0, j))

    def one_kx(i, carry):
        hold = each(lambda m: m == 1, load(hold_ref, 0))
        g = load(gx, 0)
        part = {}
        for e, j in enumerate(EDGES):
            n = load(np_ref, (i + 2) * BY + j)
            total = x_change(flow, n, ax, i, j, edge, xnear, xflux)
            upper = kx_flux(g, rkx, np_ref, i + 1, j)
            lower = load(fk, e)
            store(fk, e, upper)
            part[j] = each(lambda p, t, u, v: p - (t + (u - v)), load(p_y, i * BY + j), total, upper, lower)
            store(p_ref, i * len(EDGES) + e, part[j])

        def own(f, a, b):
            w = load(aky, i * (BY + 1) + f)
            a, b = (load(np_ref, (i + 2) * BY + j) for j in (a, b))
            return each(lambda w, a, b: w * (3.0 * a - b), w, a, b)

        def edge_layer(j, low, high):
            return each(lambda m, p, u, v: jnp.where(m, spec[i * BY + j], p - (u - v)), hold, part[j], high, low)

        f = [own(0, 0, 1), own(1, 1, 2), own(2, 2, 3)]
        down = [edge_layer(0, f[0], f[1]), edge_layer(1, f[1], f[2])]
        f = [own(BY - 2, BY - 3, BY - 4), own(BY - 1, BY - 2, BY - 3), own(BY, BY - 1, BY - 2)]
        up = [edge_layer(BY - 2, f[0], f[1]), edge_layer(BY - 1, f[1], f[2])]
        for l in range(2):
            store(ky2_od, i * 2 + l, each(lambda a, b: jnp.where(is_even(ky_place), a, b), down[l], up[l]))
            store(ky2_ev, i * 2 + l, each(lambda a, b: jnp.where(is_even(ky_place), b, a), down[l], up[l]))
        return carry

    loop(BX, one_kx, 4)


def ky_column(n_ref, halo, i):
    layers = [halo.low(i * 2 + l) for l in range(2)]
    layers += [load(n_ref, (i + 2) * BY + j) for j in range(BY)]
    return layers + [halo.high(i * 2 + l) for l in range(2)]


def stage_one_middle(np_ref, p_y, ax, rkx, gx, edge, xnear, xflux, p_ref, fk):
    flow = Flow()
    g = load(gx, 0)
    for e, j in enumerate(MIDDLE):
        store(fk, e, kx_flux(g, rkx, np_ref, 0, j))

    def one_kx(i, carry):
        g = load(gx, 0)
        for e, j in enumerate(MIDDLE):
            n = load(np_ref, (i + 2) * BY + j)
            total = x_change(flow, n, ax, i, j, edge, xnear, xflux)
            upper = kx_flux(g, rkx, np_ref, i + 1, j)
            lower = load(fk, e)
            store(fk, e, upper)
            p = each(lambda p, t, u, v: p - (t + (u - v)), load(p_y, i * BY + j), total, upper, lower)
            store(p_ref, i * len(MIDDLE) + e, p)
        return carry

    loop(BX, one_kx, 4)


def stage_one_rest(np_ref, p_ref, p_middle, aky, gy, hold_ref, spec, ky_od, ky_ev, sp_ref, x2):
    flow = Flow()
    halo = Halo(ky_od, ky_ev, "ky", 1)

    def one_kx(i, carry):
        hold = each(lambda m: m == 1, load(hold_ref, 0))
        gk = load(gy, 0)
        layers = ky_column(np_ref, halo, i)
        lower_y = ky_flux(gk, aky, layers, i, 0)
        last = [[], []]
        for j in range(BY):
            if j in EDGES:
                p = load(p_ref, i * len(EDGES) + EDGES.index(j))
            else:
                p = load(p_middle, i * len(MIDDLE) + MIDDLE.index(j))
            upper_y = ky_flux(gk, aky, layers, i, j + 1)
            v = each(lambda m, p, u, v: jnp.where(m, spec[i * BY + j], p - (u - v)), hold, p, upper_y, lower_y)
            store(sp_ref, (i + 2) * BY + j, v)
            lower_y = upper_y
            for b in range(2):
                last[b].append(v[1][b])
        for b in range(2):
            rows = flow.edge_rows(last[b])
            for l in range(2):
                x2[l * 2 * BX + i * 2 + b] = rows[l]
        return carry

    loop(BX, one_kx, 4)


def kx_messages(sp_in, sp_ref, kx2_od, kx2_ev, sems):
    _, kx_place, _, _, _ = place()
    size = 2 * BY * T
    low, high = size, size + (BX - 2) * BY * T
    messages = [
        pltpu.make_async_copy(sp_ref.at[pl.ds(jnp.where(is_even(kx_place), *at), size)], ref, sems.at[n])
        for n, (ref, at) in enumerate(((kx2_od, (low, high)), (kx2_ev, (high, low))))
    ]
    for c in messages:
        c.start()
    sp_ref[pl.ds(0, size)] = jnp.zeros((size, 8, 128), f32)
    sp_ref[pl.ds((BX + 2) * BY * T, size)] = jnp.zeros((size, 8, 128), f32)
    for c in messages:
        c.wait()


STEP = 4
INNER = range(2, BX - 2)


def send_out(buffer, out, sem, first, rows, layers):
    flow = Flow()
    rows, layers = pl.ds(first, rows), pl.ds(layers[0], len(layers))
    for a in range(2):
        for b in range(2):
            x, y = flow.natural(a, b)
            pltpu.make_async_copy(buffer.at[:, :, 2 * a + b], out.at[rows, layers, x, y], sem).start()


def stage_two_inner(np_ref, sp_ref, ax, ay, rkx, aky, gx, gy, edge, q_ref, fk):
    flow = Flow()
    nothing = each(lambda v: jnp.zeros_like(v), load(gx, 0))

    g = load(gx, 0)
    for j in range(BY):
        store(fk, j, kx_flux(g, rkx, sp_ref, 0, j))

    def one_kx(i, carry):
        g, gk = load(gx, 0), load(gy, 0)
        layers = [nothing] * 2 + [load(sp_ref, (i + 2) * BY + j) for j in range(BY)] + [nothing] * 2
        lower_y = ky_flux(gk, aky, layers, i, 0)
        for j in range(BY):
            slab = i * BY + j
            n = layers[j + 2]
            total = x_change(flow, n, ax, i, j, edge, None, None)
            total = each(lambda t, u: t + u, total, y_change(flow, n, ay, i, j))
            upper = kx_flux(g, rkx, sp_ref, i + 1, j)
            lower = load(fk, j)
            store(fk, j, upper)
            upper_y = ky_flux(gk, aky, layers, i, j + 1)
            v = each(
                lambda a, n, t, u, v, p, q: 0.5 * ((a + n) - ((t + (u - v)) + (p - q))),
                load(np_ref, (i + 2) * BY + j), n, total, upper, lower, upper_y, lower_y,
            )
            store(q_ref, slab, v)
            lower_y = upper_y
        return carry

    loop(BX, one_kx, 2)


def halo_terms(g, low_speeds, high_speeds, low, high):
    up = [each(lambda g, w: jnp.where(g > 0, 0.5 * w, 0.0), g, w) for w in low_speeds]
    down = [each(lambda g, w: jnp.where(g > 0, 0.0, 0.5 * w), g, w) for w in high_speeds]
    end = each(lambda w, a, b: w * (3.0 * a - b), up[0], low[1], low[0])
    second = each(lambda w, a: w * a, up[1], low[1])
    top = each(lambda w, a, b: w * (3.0 * a - b), down[1], high[0], high[1])
    below_top = each(lambda w, a: w * a, down[0], high[0])
    return (
        each(lambda a, b: a + b, end, second),
        each(lambda b: -b, second),
        below_top,
        each(lambda a, b: -(a + b), top, below_top),
    )


def stage_two_x(q_in, ax, halo_speed, hold_ref, spec, x2, q_ref, out, xnear, xflux, done, sem):
    _, _, _, x_up, _ = place()
    flow = Flow()
    none = no_inflow(x_up)
    near = jnp.where(none, 0.0, x2[pl.ds(0, 2 * BX)])
    xnear[...] = 0.5 * near
    xflux[...] = (3.0 * near - jnp.where(none, 0.0, x2[pl.ds(2 * BX, 2 * BX)])) * (0.5 * halo_speed[...])
    second = flow.rows == jnp.where(x_up, 1, 6)

    def one_kx(i, inner):
        hold = each(lambda m: m == 1, load(hold_ref, 0))
        for j in range(BY):
            slab = i * BY + j
            q = load(q_ref, slab)
            for b in range(2):
                less = ax[slab * T + b] * row(xnear, i, j, b)
                into = less + row(xflux, i, j, b)
                q[0][b] = q[0][b] + jnp.where(
                    flow.x_first, into, jnp.where(second, -pltpu.roll(less, flow.x_roll, 0), 0.0)
                )
            if inner and j in MIDDLE:
                for a in range(2):
                    for b in range(2):
                        done[i - INNER[0], j - MIDDLE[0], 2 * a + b] = jnp.where(hold[a][b], spec[slab], q[a][b])
            else:
                for b in range(2):
                    q_ref[slab * T + b] = q[0][b]

    def several(n, carry):
        first = INNER[0] + n * STEP
        for k in range(STEP):
            one_kx(first + k, True)
        send_out(done.at[pl.ds(n * STEP, STEP)], out, sem, first, STEP, MIDDLE)
        return carry

    lax.fori_loop(0, len(INNER) // STEP, several, 0)
    for i in (0, 1, BX - 2, BX - 1):
        one_kx(i, False)
    wait_all(done, sem)


def stage_two_kx(q_in, rkx, gx, kx_od, kx_ev, q_ref):
    kx_halo = Halo(kx_od, kx_ev, "kx", 2)

    def kx_ends(j, carry):
        g = load(gx, 0)
        speed = [each(lambda r, g: r * g, load(rkx, f * BY + j), g) for f in (0, 1, BX - 1, BX)]
        low = [kx_halo.low(l * BY + j) for l in range(2)]
        high = [kx_halo.high(l * BY + j) for l in range(2)]
        terms = halo_terms(g, speed[:2], speed[2:], low, high)
        for i, term in zip((0, 1, BX - 2, BX - 1), terms):
            slab = i * BY + j
            store(q_ref, slab, each(lambda q, t: q + t, load(q_ref, slab), term))
        return carry

    loop(BY, kx_ends, 4)


def stage_two_ky(q_ref, aky, gy, hold_ref, spec, ky_od, ky_ev, out_in, out, done, ends, sems):
    ky_halo = Halo(ky_od, ky_ev, "ky", 1)
    hold = each(lambda m: m == 1, load(hold_ref, 0))
    for e, i in enumerate((0, 1, BX - 2, BX - 1)):
        for j in MIDDLE:
            slab = i * BY + j
            q = load(q_ref, slab)
            for a in range(2):
                for b in range(2):
                    ends[e, j - MIDDLE[0], 2 * a + b] = jnp.where(hold[a][b], spec[slab], q[a][b])
    send_out(ends.at[pl.ds(0, 2)], out, sems.at[0], 0, 2, MIDDLE)
    send_out(ends.at[pl.ds(2, 2)], out, sems.at[0], BX - 2, 2, MIDDLE)

    def one_kx(i):
        hold = each(lambda m: m == 1, load(hold_ref, 0))
        gk = load(gy, 0)
        speed = [load(aky, i * (BY + 1) + f) for f in (0, 1, BY - 1, BY)]
        low = [ky_halo.low(i * 2 + l) for l in range(2)]
        high = [ky_halo.high(i * 2 + l) for l in range(2)]
        for e, (j, term) in enumerate(zip(EDGES, halo_terms(gk, speed[:2], speed[2:], low, high))):
            slab = i * BY + j
            q = each(lambda q, t: q + t, load(q_ref, slab), term)
            for a in range(2):
                for b in range(2):
                    done[i, e, 2 * a + b] = jnp.where(hold[a][b], spec[slab], q[a][b])

    def several(n, carry):
        for k in range(STEP):
            one_kx(n * STEP + k)
        rows = done.at[pl.ds(n * STEP, STEP)]
        send_out(rows.at[:, pl.ds(0, 2)], out, sems.at[1], n * STEP, STEP, EDGES[:2])
        send_out(rows.at[:, pl.ds(2, 2)], out, sems.at[1], n * STEP, STEP, EDGES[2:])
        return carry

    lax.fori_loop(0, BX // STEP, several, 0)
    wait_all(ends, sems.at[0])
    wait_all(done, sems.at[1])


def call(kernel, outs, operands, spaces, out_spaces, scratch=(), alias=None, us=1, limit=LIMIT):
    whole = {
        "v": pl.BlockSpec(memory_space=pltpu.VMEM),
        "h": pl.BlockSpec(memory_space=pltpu.HBM),
    }
    return pl.pallas_call(
        kernel,
        out_shape=tuple(outs),
        in_specs=[whole[c] for c in spaces],
        out_specs=tuple(whole[c] for c in out_spaces),
        scratch_shapes=list(scratch),
        input_output_aliases=alias or {},
        compiler_params=pltpu.CompilerParams(vmem_limit_bytes=limit),
        cost_estimate=pl.CostEstimate(flops=int(us * 1e9), bytes_accessed=0, transcendentals=0),
        name=kernel.__name__,
    )(*operands)


def per_device(action, depth_cm, inflow_mask, inflow):
    slabs, padded = BX * BY * T, (BX + 4) * BY * T
    edge_slabs, ky_tiles, kx_tiles = BX * len(EDGES) * T, BX * 2 * T, 2 * BY * T
    sizes = [lax.axis_size(axis) for axis in AXES]

    def v(*shape):
        return pltpu.VMEM(shape + (8, 128), f32)

    def swap_odd(message, axis, spare):
        return lax.ppermute(message, AXES, swaps(sizes, AXES.index(axis), 1, AXES.index(spare)))

    def swap_even(message, axis):
        return lax.ppermute(message, AXES, swaps(sizes, AXES.index(axis), 0, 0))

    sem = pltpu.SemaphoreType.DMA
    np5, kx_od, kx_ev, ky_od, depth, mask, spectrum = call(
        first_messages,
        (v(BX + 4, BY, T), v(2, BY, T), v(2, BY, T), v(BX, 2, T), pltpu.VMEM((BS, NY), jnp.int32),
         pltpu.VMEM((BS, NY), jnp.int32), pltpu.VMEM((NKX, NKY), f32)),
        (action, depth_cm, inflow_mask, inflow),
        "hhhh",
        "v" * 7,
        [sem((7,))],
        us=0,
        limit=FIRST_LIMIT,
    )
    ky_od = swap_odd(ky_od, "ky", "kx").reshape(ky_tiles, 8, 128)
    kx_ev = swap_even(kx_ev, "kx").reshape(kx_tiles, 8, 128)
    kx_od = swap_odd(kx_od, "kx", "space").reshape(kx_tiles, 8, 128)
    np3, ky_ev, x_od, x_ev = call(
        more_messages,
        (v(padded), v(BX, 2, T), v(4 * BX + 2), v(4 * BX + 2)),
        (np5.reshape(padded, 8, 128), depth, kx_ev),
        "v" * 3,
        "v" * 4,
        [sem],
        alias={0: 0},
        us=0,
    )
    x_od, x_ev = swap_odd(x_od, "space", "kx"), swap_even(x_ev, "space")
    ky_ev = swap_even(ky_ev, "ky").reshape(ky_tiles, 8, 128)
    ax, ay, rkx, aky, gy, heights, hold, spec = call(
        speeds,
        (v(slabs), v(slabs), v((BX + 1) * BY * T), v(BX * (BY + 1) * T), v(T), pltpu.VMEM((BS, NY), f32),
         pltpu.VMEM((T, 8, 128), jnp.int32), v(BX * BY)),
        (depth, mask, spectrum),
        "vvv",
        "v" * 8,
        [v(3 * T)],
        us=3,
    )
    (p_y,) = call(stage_one_y, (v(slabs),), (np3, ay), "vv", "v", us=1)
    np3, part, gx, edge, halo_speed, xnear, xflux, ky2_od, ky2_ev = call(
        stage_one_edges,
        (v(padded), v(edge_slabs), v(T), v(2 * BX), v(2 * BX), v(2 * BX), v(2 * BX), v(ky_tiles), v(ky_tiles)),
        (np3, p_y, ax, rkx, aky, heights, hold, spec, kx_od, x_od, x_ev),
        "v" * 11,
        "v" * 9,
        [v(len(EDGES) * T), v(4)],
        alias={0: 0},
        us=0,
    )
    ky2_od, ky2_ev = swap_odd(ky2_od, "ky", "kx"), swap_even(ky2_ev, "ky")
    (p_middle,) = call(
        stage_one_middle,
        (v(BX * len(MIDDLE) * T),),
        (np3, p_y, ax, rkx, gx, edge, xnear, xflux),
        "v" * 8,
        "v",
        [v(len(MIDDLE) * T)],
        us=2,
    )
    sp, x2 = call(
        stage_one_rest,
        (v(padded), v(4 * BX)),
        (np3, part, p_middle, aky, gy, hold, spec, ky_od, ky_ev),
        "v" * 9,
        "v" * 2,
        us=0,
    )
    x2 = lax.ppermute(x2, AXES[:2], ring(sizes))
    sp, kx2_od, kx2_ev = call(
        kx_messages,
        (v(padded), v(kx_tiles), v(kx_tiles)),
        (sp,),
        "v",
        "v" * 3,
        [sem((2,))],
        alias={0: 0},
        us=0,
    )
    kx2_od, kx2_ev = lax.ppermute(kx2_od, AXES, swaps(sizes, 1, 1, 0, True)), swap_even(kx2_ev, "kx")
    (q,) = call(
        stage_two_inner,
        (v(slabs),),
        (np3, sp, ax, ay, rkx, aky, gx, gy, edge),
        "v" * 9,
        "v",
        [v(BY * T)],
        us=4,
    )
    q, out = call(
        stage_two_x,
        (v(slabs), jax.ShapeDtypeStruct(action.shape, f32)),
        (q, ax, halo_speed, hold, spec, x2),
        "v" * 6,
        "vh",
        [v(2 * BX), v(2 * BX), v(len(INNER), len(MIDDLE), T), sem],
        alias={0: 0},
        us=2,
    )
    (q,) = call(
        stage_two_kx,
        (v(slabs),),
        (q, rkx, gx, kx2_od, kx2_ev),
        "v" * 5,
        "v",
        alias={0: 0},
        us=1,
    )
    (out,) = call(
        stage_two_ky,
        (jax.ShapeDtypeStruct(action.shape, f32),),
        (q, aky, gy, hold, spec, ky2_od, ky2_ev, out),
        "v" * 7 + "h",
        "h",
        [v(BX, len(EDGES), T), v(4, len(MIDDLE), T), sem((2,))],
        alias={7: 0},
        us=0,
    )
    return out


def solution(mesh):
    in_specs = (P("kx", "ky", "space", None), P("space", None), P("space", None), P())
    out_specs = P("kx", "ky", "space", None)
    return jax.shard_map(
        per_device, mesh=mesh, in_specs=in_specs, out_specs=out_specs, check_vma=False
    )
```

```python
import jax
import jax.numpy as jnp
from jax import lax
from jax.experimental import pallas as pl
from jax.experimental.pallas import tpu as pltpu
from jax.sharding import PartitionSpec as P

NKX = 64
NKY = 64

gravity = 9.81
spacing = 4.0
k_step = 0.04
time_step = 0.2

BX, BY, BS, NY = 16, 8, 16, 256
T = 4
f32 = jnp.float32
LIMIT = 8 * 2**20
FIRST_LIMIT = 54 * 2**20
EDGES = (0, 1, BY - 2, BY - 1)
MIDDLE = tuple(range(2, BY - 2))

X_SCALE = time_step / spacing * 0.5
K_SCALE = time_step / k_step * 0.5


AXES = ("space", "kx", "ky")


def swaps(sizes, axis, odd, spare, against=False):
    pairs = []
    for n in range(sizes[0] * sizes[1] * sizes[2]):
        at = [n // (sizes[1] * sizes[2]), n // sizes[2] % sizes[1], n % sizes[2]]
        other = ((at[axis] + odd) ^ 1) - odd
        if 0 <= other < sizes[axis]:
            at[axis] = other
        elif against:
            at[0] = (at[0] + (1 if at[1] < sizes[1] // 2 else -1)) % sizes[0]
        else:
            at[spare] ^= 1
        pairs.append((n, (at[0] * sizes[1] + at[1]) * sizes[2] + at[2]))
    return pairs


def ring(sizes):
    pairs = []
    for a in range(sizes[0]):
        for b in range(sizes[1]):
            to = (a + (1 if b >= sizes[1] // 2 else -1)) % sizes[0]
            pairs.append((a * sizes[1] + b, to * sizes[1] + b))
    return pairs


def place():
    s, i, j = lax.axis_index("space"), lax.axis_index("kx"), lax.axis_index("ky")
    return s, i, j, i >= lax.axis_size("kx") // 2, j >= lax.axis_size("ky") // 2


def is_even(i):
    return i % 2 == 0


def loop(count, body, step):
    def several(n, carry):
        for k in range(step):
            carry = body(n * step + k, carry)
        return carry

    lax.fori_loop(0, count // step, several, 0)


class Flow:
    def __init__(self):
        _, _, _, x_up, y_up = place()
        x0 = jnp.where(x_up, 0, 8)
        y0 = jnp.where(y_up, 0, 128)
        self.x_up = x_up
        self.x = (pl.multiple_of(x0, 8), pl.multiple_of(8 - x0, 8))
        self.y = (pl.multiple_of(y0, 128), pl.multiple_of(128 - y0, 128))
        self.x_roll = jnp.where(x_up, 1, 7)
        self.y_roll = jnp.where(y_up, 1, 127)
        self.rows = lax.broadcasted_iota(jnp.int32, (8, 128), 0)
        lanes = lax.broadcasted_iota(jnp.int32, (8, 128), 1)
        self.x_first = self.rows == jnp.where(x_up, 0, 7)
        self.x_last = self.rows == jnp.where(x_up, 7, 0)
        self.y_first = lanes == jnp.where(y_up, 0, 127)

    def natural(self, a, b):
        return pl.ds(self.x[a], 8), pl.ds(self.y[b], 128)

    def before_x(self, tiles, b, halo):
        first, second = (pltpu.roll(tiles[a][b], self.x_roll, 0) for a in range(2))
        return [jnp.where(self.x_first, halo, first), jnp.where(self.x_first, first, second)]

    def before_y(self, tiles, a):
        first, second = (pltpu.roll(tiles[a][b], self.y_roll, 1) for b in range(2))
        return [jnp.where(self.y_first, 0.0, first), jnp.where(self.y_first, first, second)]

    def edge_rows(self, tiles):
        out = []
        for up, down in ((7, 0), (6, 1)):
            rows = None
            for j in range(BY):
                shift = jnp.where(self.x_up, (j - up) % 8, (j - down) % 8)
                turned = pltpu.roll(tiles[j], shift, 0)
                rows = turned if rows is None else jnp.where(self.rows == j, turned, rows)
            out.append(rows)
        return out


def load(ref, slab):
    return [[ref[slab * T + 2 * a + b] for b in range(2)] for a in range(2)]


def store(ref, slab, tiles):
    for a in range(2):
        for b in range(2):
            ref[slab * T + 2 * a + b] = tiles[a][b]


def each(fn, *grids):
    return [[fn(*(g[a][b] for g in grids)) for b in range(2)] for a in range(2)]


def row(ref, i, j, b):
    return jnp.broadcast_to(ref[i * 2 + b][j : j + 1, :], (8, 128))


def wait_all(dst, sem):
    pltpu.make_async_copy(dst, dst, sem).wait()


def shifted(h, axis, up):
    size = h.shape[axis]
    place_of = lax.broadcasted_iota(jnp.int32, h.shape, axis)
    if up:
        return jnp.where(place_of == size - 1, h, pltpu.roll(h, size - 1, axis))
    return jnp.where(place_of == 0, h, pltpu.roll(h, 1, axis))


def centre(first, i):
    return ((first + i - NKX // 2).astype(f32) + 0.5) * k_step


def lower_face(first, i):
    return (first + i - NKX // 2).astype(f32) * k_step


def wave(kx, ky):
    square = jnp.broadcast_to(kx * kx + ky * ky, (8, 128))
    inverse = lax.rsqrt(square)
    return square * inverse, inverse


def centre_rows(flow, first):
    return ((first + flow.rows - NKY // 2).astype(f32) + 0.5) * k_step


def pick(tile, j):
    return jnp.broadcast_to(tile[j : j + 1, :], (8, 128))


def group_factor(k, inverse):
    return (0.5 * X_SCALE * gravity**0.5) * inverse * lax.rsqrt(k)


def refract_factor(k):
    return (0.5 * K_SCALE * gravity**0.5) * (k * k) * lax.rsqrt(k)


def group(k, c, h):
    kh = k * h
    t = jnp.tanh(kh)
    return c * ((t + kh * (1.0 - t * t)) * lax.rsqrt(t))


def refract(k, c, h):
    t = jnp.tanh(k * h)
    return c * ((1.0 - t * t) * lax.rsqrt(t))


def first_messages(
    a_ref, depth_ref, mask_ref, inflow_ref,
    np_ref, kx_od, kx_ev, ky_od, ky_ev, depth, mask, inflow, sems,
):
    s, i, j, x_up, y_up = place()
    flow = Flow()
    own = np_ref.at[pl.ds(2, BX)]
    small = [
        pltpu.make_async_copy(src, dst, sems.at[n])
        for n, (src, dst) in enumerate(((depth_ref, depth), (mask_ref, mask), (inflow_ref, inflow)))
    ]
    for c in small:
        c.start()
    for a in range(2):
        for b in range(2):
            x, y = flow.natural(a, b)
            pltpu.make_async_copy(a_ref.at[:, :, x, y], own.at[:, :, 2 * a + b], sems.at[3]).start()
    wait_all(own, sems.at[3])
    low, high = jnp.where(is_even(i), 0, BX - 2), jnp.where(is_even(i), BX - 2, 0)
    messages = [
        pltpu.make_async_copy(src, ref, sems.at[n])
        for n, (src, ref) in enumerate(
            (
                (own.at[:, pl.ds(jnp.where(is_even(j), 0, BY - 2), 2)], ky_od),
                (own.at[:, pl.ds(jnp.where(is_even(j), BY - 2, 0), 2)], ky_ev),
                (own.at[pl.ds(low, 2)], kx_od),
                (own.at[pl.ds(high, 2)], kx_ev),
            ),
            4,
        )
    ]
    for c in messages:
        c.start()
    for c in small + messages:
        c.wait()


def x_messages(np_in, depth, kx_ev, np_ref, x_od, x_ev):
    s, i, j, x_up, _ = place()
    flow = Flow()
    for b in range(2):
        y = pl.ds(flow.y[b], 128)
        first = jnp.broadcast_to(depth[0:1, y].astype(f32), (8, 128))
        last = jnp.broadcast_to(depth[BS - 1 : BS, y].astype(f32), (8, 128))
        x_od[4 * BX + b] = jnp.where(is_even(s), first, last)
        x_ev[4 * BX + b] = jnp.where(is_even(s), last, first)

    def one_kx(i, carry):
        for b in range(2):
            rows = flow.edge_rows([np_ref[((i + 2) * BY + j) * T + 2 + b] for j in range(BY)])
            for l in range(2):
                x_od[l * 2 * BX + i * 2 + b] = rows[l]
                x_ev[l * 2 * BX + i * 2 + b] = rows[l]
        return carry

    loop(BX, one_kx, 4)
    size = 2 * BY * T
    np_ref[pl.ds(jnp.where(is_even(i), (BX + 2) * BY * T, 0), size)] = kx_ev[...]


def speeds(depth, mask, inflow, ax, ay, rkx, aky, gy, heights, hold, spec, geo):
    _, kx_place, ky_place, x_up, y_up = place()
    flow = Flow()
    kx_first, ky_first = kx_place * BX, ky_place * BY
    h = depth[...].astype(f32) * 0.01
    heights[...] = h
    y_next, y_last = shifted(h, 1, True), shifted(h, 1, False)
    hx = 0.5 * (h + jnp.where(x_up, shifted(h, 0, True), shifted(h, 0, False)))
    hy = 0.5 * (h + jnp.where(y_up, y_next, y_last))
    slope = (y_last - y_next) * (1.0 / (2.0 * spacing))
    x_flip, y_flip = jnp.where(x_up, 0, 1), jnp.where(y_up, 0, 1)
    for a in range(2):
        for b in range(2):
            at = (a ^ x_flip) * 2 + (b ^ y_flip)
            part = (slice(8 * a, 8 * a + 8), slice(128 * b, 128 * b + 128))
            gy[at] = slope[part]
            hold[at] = mask[part]
            geo[at] = h[part]
            geo[T + at] = hx[part]
            geo[2 * T + at] = hy[part]

    lanes = lax.broadcasted_iota(jnp.int32, (8, NKY), 1)
    for half in range(BX // 8):
        rows = inflow[pl.ds(pl.multiple_of(kx_first + 8 * half, 8), 8), :]
        for j in range(BY):
            column = jnp.sum(jnp.where(lanes == ky_first + j, rows, 0.0), axis=1, keepdims=True)
            column = jnp.broadcast_to(column, (8, 128))
            for r in range(8):
                spec[(8 * half + r) * BY + j] = jnp.broadcast_to(column[r : r + 1, :], (8, 128))

    ky = centre_rows(flow, ky_first)
    ky_face = (ky_first + flow.rows - NKY // 2).astype(f32) * k_step

    def kx_faces(i):
        k, _ = wave(lower_face(kx_first, i), ky)
        c = refract_factor(k)
        for j in range(BY):
            kj, cj = pick(k, j), pick(c, j)
            store(rkx, i * BY + j, each(lambda h: refract(kj, cj, h), load(geo, 0)))

    def one_kx(i, carry):
        kx = centre(kx_first, i)
        k, inverse = wave(kx, ky)
        c = group_factor(k, inverse)
        cx, cy = c * jnp.abs(kx), c * jnp.abs(ky)
        for j in range(BY):
            kj, cxj, cyj = pick(k, j), pick(cx, j), pick(cy, j)
            store(ax, i * BY + j, each(lambda h: group(kj, cxj, h), load(geo, 1)))
            store(ay, i * BY + j, each(lambda h: group(kj, cyj, h), load(geo, 2)))
        kx_faces(i)
        k, _ = wave(kx, ky_face)
        c = refract_factor(k)
        end, _ = wave(kx, lower_face(ky_first, BY))
        end_c = refract_factor(end)
        for j in range(BY + 1):
            kj, cj = (pick(k, j), pick(c, j)) if j < BY else (end, end_c)
            store(aky, i * (BY + 1) + j, each(lambda h, g: refract(kj, cj, h) * g, load(geo, 0), load(gy, 0)))
        return carry

    loop(BX, one_kx, 4)
    kx_faces(BX)


def x_change(flow, n, ax_ref, i, j, edge, halo_row, halo_flux):
    ax = load(ax_ref, i * BY + j)
    total = [[None, None], [None, None]]
    for b in range(2):
        ax[1][b] = jnp.where(flow.x_last, row(edge, i, j, b), ax[1][b])
        before = flow.before_x(n, b, 0.0 if halo_row is None else row(halo_row, i, j, b))
        out = [[ax[a][b] * (3.0 * n[a][b] - before[a])] * 2 for a in range(2)]
        into = flow.before_x(out, b, 0.0 if halo_flux is None else row(halo_flux, i, j, b))
        for a in range(2):
            total[a][b] = out[a][b] - into[a]
    return total


def y_change(flow, n, ay_ref, i, j):
    ay = load(ay_ref, i * BY + j)
    total = [[None, None], [None, None]]
    for a in range(2):
        before = flow.before_y(n, a)
        out = [ay[a][b] * (3.0 * n[a][b] - before[b]) for b in range(2)]
        into = flow.before_y([out, out], 0)
        for b in range(2):
            total[a][b] = out[b] - into[b]
    return total


def face(up, speed, n_2, n_1, n1, n2):
    near = jnp.where(up, n_1, n1)
    far = jnp.where(up, n_2, n2)
    return speed * (3.0 * near - far)


def kx_flux(gx, rkx, n_ref, i, j):
    n = [load(n_ref, (i + d) * BY + j) for d in range(4)]
    return each(lambda g, r, *n: face(g > 0, r * g, *n), gx, load(rkx, i * BY + j), *n)


def ky_flux(gy, aky, layers, i, f):
    return each(lambda g, w, *n: face(g > 0, w, *n), gy, load(aky, i * (BY + 1) + f), *layers[f : f + 4])


class Halo:
    def __init__(self, od, ev, axis, flip):
        p, last = lax.axis_index(axis), lax.axis_size(axis) - 1
        middle = (last + 1) // 2
        self.od, self.ev, self.even = od, ev, is_even(p)
        self.low_empty, self.high_empty = p == 0, p == last
        self.low_at = [jnp.where(p == middle, t ^ flip, t) for t in range(T)]
        self.high_at = [jnp.where(p == middle - 1, t ^ flip, t) for t in range(T)]

    def take(self, first, second, slab, at, empty):
        def tile(t):
            r = slab * T + at[t]
            return jnp.where(empty, 0.0, jnp.where(self.even, first[r], second[r]))

        return [[tile(2 * a + b) for b in range(2)] for a in range(2)]

    def low(self, slab):
        return self.take(self.od, self.ev, slab, self.low_at, self.low_empty)

    def high(self, slab):
        return self.take(self.ev, self.od, slab, self.high_at, self.high_empty)


def no_inflow(x_up):
    s = lax.axis_index("space")
    return s == jnp.where(x_up, 0, lax.axis_size("space") - 1)


def stage_one_y(np_ref, ay, p_ref):
    flow = Flow()

    def one_kx(i, carry):
        for j in range(BY):
            n = load(np_ref, (i + 2) * BY + j)
            store(p_ref, i * BY + j, each(lambda n, t: n - t, n, y_change(flow, n, ay, i, j)))
        return carry

    loop(BX, one_kx, 2)


def stage_one_edges(
    np_in, p_y, ax, rkx, aky, heights, hold_ref, spec, kx_od, x_od, x_ev,
    np_ref, p_ref, gx, edge, halo_speed, xnear, xflux, ky2_od, ky2_ev, fk, hrow,
):
    s, kx_place, ky_place, x_up, y_up = place()
    flow = Flow()
    kx_first, ky_first = kx_place * BX, ky_place * BY
    odd_low = is_even(kx_place)
    empty = jnp.where(odd_low, kx_place == 0, kx_place == lax.axis_size("kx") - 1)
    base = jnp.where(odd_low, 0, (BX + 2) * BY)

    def odd_side(r, carry):
        tiles = [[kx_od[r * T + 2 * (1 - a) + b] for b in range(2)] for a in range(2)]
        store(np_ref, base + r, each(lambda v: jnp.where(empty, 0.0, v), tiles))
        return carry

    loop(2 * BY, odd_side, 8)
    h = heights[...]
    x_flip, y_flip = jnp.where(x_up, 0, 1), jnp.where(y_up, 0, 1)
    none = no_inflow(x_up)
    use_od = is_even(s) == x_up
    for b in range(2):
        y = b ^ y_flip
        at = 4 * BX + y
        mine = h[:, 128 * b : 128 * b + 128]
        od, ev = x_od[at][0:1, :] * 0.01, x_ev[at][0:1, :] * 0.01
        low = jnp.where(s == 0, mine[0:1, :], jnp.where(is_even(s), od, ev))
        high = jnp.where(s == lax.axis_size("space") - 1, mine[BS - 1 : BS, :], jnp.where(is_even(s), ev, od))
        place_of = lax.broadcasted_iota(jnp.int32, (BS, 128), 0)
        before = jnp.where(place_of == 0, low, pltpu.roll(mine, 1, 0))
        after = jnp.where(place_of == BS - 1, high, pltpu.roll(mine, BS - 1, 0))
        slope = (before - after) * (1.0 / (2.0 * spacing))
        for a in range(2):
            gx[(a ^ x_flip) * 2 + y] = slope[8 * a : 8 * a + 8, :]
        face_low = jnp.broadcast_to(0.5 * (low + mine[0:1, :]), (8, 128))
        face_high = jnp.broadcast_to(0.5 * (high + mine[BS - 1 : BS, :]), (8, 128))
        hrow[y] = jnp.where(x_up, face_high, face_low)
        hrow[2 + y] = jnp.where(x_up, face_low, face_high)
    ky = ((ky_first + flow.rows - NKY // 2).astype(f32) + 0.5) * k_step

    def edges(i, carry):
        kx = centre(kx_first, i)
        k, inverse = wave(kx, ky)
        c = group_factor(k, inverse) * jnp.abs(kx)
        for b in range(2):
            at = i * 2 + b
            near = jnp.where(use_od, x_od[at], x_ev[at])
            far = jnp.where(use_od, x_od[2 * BX + at], x_ev[2 * BX + at])
            edge[at] = group(k, c, hrow[b])
            speed = group(k, c, hrow[2 + b])
            halo_speed[at] = speed
            xnear[at] = jnp.where(none, 0.0, near)
            xflux[at] = jnp.where(none, 0.0, speed * (3.0 * near - far))
        return carry

    loop(BX, edges, 8)

    g = load(gx, 0)
    for e, j in enumerate(EDGES):
        store(fk, e, kx_flux(g, rkx, np_ref, 0, j))

    def one_kx(i, carry):
        hold = each(lambda m: m == 1, load(hold_ref, 0))
        g = load(gx, 0)
        part = {}
        for e, j in enumerate(EDGES):
            n = load(np_ref, (i + 2) * BY + j)
            total = x_change(flow, n, ax, i, j, edge, xnear, xflux)
            upper = kx_flux(g, rkx, np_ref, i + 1, j)
            lower = load(fk, e)
            store(fk, e, upper)
            part[j] = each(lambda p, t, u, v: p - (t + (u - v)), load(p_y, i * BY + j), total, upper, lower)
            store(p_ref, i * len(EDGES) + e, part[j])

        def own(f, a, b):
            w = load(aky, i * (BY + 1) + f)
            a, b = (load(np_ref, (i + 2) * BY + j) for j in (a, b))
            return each(lambda w, a, b: w * (3.0 * a - b), w, a, b)

        def edge_layer(j, low, high):
            return each(lambda m, p, u, v: jnp.where(m, spec[i * BY + j], p - (u - v)), hold, part[j], high, low)

        f = [own(0, 0, 1), own(1, 1, 2), own(2, 2, 3)]
        down = [edge_layer(0, f[0], f[1]), edge_layer(1, f[1], f[2])]
        f = [own(BY - 2, BY - 3, BY - 4), own(BY - 1, BY - 2, BY - 3), own(BY, BY - 1, BY - 2)]
        up = [edge_layer(BY - 2, f[0], f[1]), edge_layer(BY - 1, f[1], f[2])]
        for l in range(2):
            store(ky2_od, i * 2 + l, each(lambda a, b: jnp.where(is_even(ky_place), a, b), down[l], up[l]))
            store(ky2_ev, i * 2 + l, each(lambda a, b: jnp.where(is_even(ky_place), b, a), down[l], up[l]))
        return carry

    loop(BX, one_kx, 4)


def ky_column(n_ref, halo, i):
    layers = [halo.low(i * 2 + l) for l in range(2)]
    layers += [load(n_ref, (i + 2) * BY + j) for j in range(BY)]
    return layers + [halo.high(i * 2 + l) for l in range(2)]


def stage_one_middle(np_ref, p_y, ax, rkx, gx, edge, xnear, xflux, p_ref, fk):
    flow = Flow()
    g = load(gx, 0)
    for e, j in enumerate(MIDDLE):
        store(fk, e, kx_flux(g, rkx, np_ref, 0, j))

    def one_kx(i, carry):
        g = load(gx, 0)
        for e, j in enumerate(MIDDLE):
            n = load(np_ref, (i + 2) * BY + j)
            total = x_change(flow, n, ax, i, j, edge, xnear, xflux)
            upper = kx_flux(g, rkx, np_ref, i + 1, j)
            lower = load(fk, e)
            store(fk, e, upper)
            p = each(lambda p, t, u, v: p - (t + (u - v)), load(p_y, i * BY + j), total, upper, lower)
            store(p_ref, i * len(MIDDLE) + e, p)
        return carry

    loop(BX, one_kx, 4)


def stage_one_rest(np_ref, p_ref, p_middle, aky, gy, hold_ref, spec, ky_od, ky_ev, sp_ref, x2):
    flow = Flow()
    halo = Halo(ky_od, ky_ev, "ky", 1)

    def one_kx(i, carry):
        hold = each(lambda m: m == 1, load(hold_ref, 0))
        gk = load(gy, 0)
        layers = ky_column(np_ref, halo, i)
        lower_y = ky_flux(gk, aky, layers, i, 0)
        last = [[], []]
        for j in range(BY):
            if j in EDGES:
                p = load(p_ref, i * len(EDGES) + EDGES.index(j))
            else:
                p = load(p_middle, i * len(MIDDLE) + MIDDLE.index(j))
            upper_y = ky_flux(gk, aky, layers, i, j + 1)
            v = each(lambda m, p, u, v: jnp.where(m, spec[i * BY + j], p - (u - v)), hold, p, upper_y, lower_y)
            store(sp_ref, (i + 2) * BY + j, v)
            lower_y = upper_y
            for b in range(2):
                last[b].append(v[1][b])
        for b in range(2):
            rows = flow.edge_rows(last[b])
            for l in range(2):
                x2[l * 2 * BX + i * 2 + b] = rows[l]
        return carry

    loop(BX, one_kx, 4)


def kx_messages(sp_in, sp_ref, kx2_od, kx2_ev, sems):
    _, kx_place, _, _, _ = place()
    size = 2 * BY * T
    low, high = size, size + (BX - 2) * BY * T
    messages = [
        pltpu.make_async_copy(sp_ref.at[pl.ds(jnp.where(is_even(kx_place), *at), size)], ref, sems.at[n])
        for n, (ref, at) in enumerate(((kx2_od, (low, high)), (kx2_ev, (high, low))))
    ]
    for c in messages:
        c.start()
    sp_ref[pl.ds(0, size)] = jnp.zeros((size, 8, 128), f32)
    sp_ref[pl.ds((BX + 2) * BY * T, size)] = jnp.zeros((size, 8, 128), f32)
    for c in messages:
        c.wait()


STEP = 4
INNER = range(2, BX - 2)


def send_out(buffer, out, sem, first, rows, layers):
    flow = Flow()
    rows, layers = pl.ds(first, rows), pl.ds(layers[0], len(layers))
    for a in range(2):
        for b in range(2):
            x, y = flow.natural(a, b)
            pltpu.make_async_copy(buffer.at[:, :, 2 * a + b], out.at[rows, layers, x, y], sem).start()


def stage_two_inner(np_ref, sp_ref, ax, ay, rkx, aky, gx, gy, edge, q_ref, fk):
    flow = Flow()
    nothing = each(lambda v: jnp.zeros_like(v), load(gx, 0))

    g = load(gx, 0)
    for j in range(BY):
        store(fk, j, kx_flux(g, rkx, sp_ref, 0, j))

    def one_kx(i, carry):
        g, gk = load(gx, 0), load(gy, 0)
        layers = [nothing] * 2 + [load(sp_ref, (i + 2) * BY + j) for j in range(BY)] + [nothing] * 2
        lower_y = ky_flux(gk, aky, layers, i, 0)
        for j in range(BY):
            slab = i * BY + j
            n = layers[j + 2]
            total = x_change(flow, n, ax, i, j, edge, None, None)
            total = each(lambda t, u: t + u, total, y_change(flow, n, ay, i, j))
            upper = kx_flux(g, rkx, sp_ref, i + 1, j)
            lower = load(fk, j)
            store(fk, j, upper)
            upper_y = ky_flux(gk, aky, layers, i, j + 1)
            v = each(
                lambda a, n, t, u, v, p, q: 0.5 * ((a + n) - ((t + (u - v)) + (p - q))),
                load(np_ref, (i + 2) * BY + j), n, total, upper, lower, upper_y, lower_y,
            )
            store(q_ref, slab, v)
            lower_y = upper_y
        return carry

    loop(BX, one_kx, 2)


def halo_terms(g, low_speeds, high_speeds, low, high):
    up = [each(lambda g, w: jnp.where(g > 0, 0.5 * w, 0.0), g, w) for w in low_speeds]
    down = [each(lambda g, w: jnp.where(g > 0, 0.0, 0.5 * w), g, w) for w in high_speeds]
    end = each(lambda w, a, b: w * (3.0 * a - b), up[0], low[1], low[0])
    second = each(lambda w, a: w * a, up[1], low[1])
    top = each(lambda w, a, b: w * (3.0 * a - b), down[1], high[0], high[1])
    below_top = each(lambda w, a: w * a, down[0], high[0])
    return (
        each(lambda a, b: a + b, end, second),
        each(lambda b: -b, second),
        below_top,
        each(lambda a, b: -(a + b), top, below_top),
    )


def stage_two_x(q_in, ax, halo_speed, hold_ref, spec, x2, q_ref, out, xnear, xflux, done, sem):
    _, _, _, x_up, _ = place()
    flow = Flow()
    none = no_inflow(x_up)
    near = jnp.where(none, 0.0, x2[pl.ds(0, 2 * BX)])
    xnear[...] = 0.5 * near
    xflux[...] = (3.0 * near - jnp.where(none, 0.0, x2[pl.ds(2 * BX, 2 * BX)])) * (0.5 * halo_speed[...])
    second = flow.rows == jnp.where(x_up, 1, 6)

    def one_kx(i, inner):
        hold = each(lambda m: m == 1, load(hold_ref, 0))
        for j in range(BY):
            slab = i * BY + j
            q = load(q_ref, slab)
            for b in range(2):
                less = ax[slab * T + b] * row(xnear, i, j, b)
                into = less + row(xflux, i, j, b)
                q[0][b] = q[0][b] + jnp.where(
                    flow.x_first, into, jnp.where(second, -pltpu.roll(less, flow.x_roll, 0), 0.0)
                )
            if inner and j in MIDDLE:
                for a in range(2):
                    for b in range(2):
                        done[i - INNER[0], j - MIDDLE[0], 2 * a + b] = jnp.where(hold[a][b], spec[slab], q[a][b])
            else:
                for b in range(2):
                    q_ref[slab * T + b] = q[0][b]

    def several(n, carry):
        first = INNER[0] + n * STEP
        for k in range(STEP):
            one_kx(first + k, True)
        send_out(done.at[pl.ds(n * STEP, STEP)], out, sem, first, STEP, MIDDLE)
        return carry

    lax.fori_loop(0, len(INNER) // STEP, several, 0)
    for i in (0, 1, BX - 2, BX - 1):
        one_kx(i, False)
    wait_all(done, sem)


def stage_two_kx(q_in, rkx, gx, kx_od, kx_ev, q_ref):
    kx_halo = Halo(kx_od, kx_ev, "kx", 2)

    def kx_ends(j, carry):
        g = load(gx, 0)
        speed = [each(lambda r, g: r * g, load(rkx, f * BY + j), g) for f in (0, 1, BX - 1, BX)]
        low = [kx_halo.low(l * BY + j) for l in range(2)]
        high = [kx_halo.high(l * BY + j) for l in range(2)]
        terms = halo_terms(g, speed[:2], speed[2:], low, high)
        for i, term in zip((0, 1, BX - 2, BX - 1), terms):
            slab = i * BY + j
            store(q_ref, slab, each(lambda q, t: q + t, load(q_ref, slab), term))
        return carry

    loop(BY, kx_ends, 4)


def stage_two_ky(q_ref, aky, gy, hold_ref, spec, ky_od, ky_ev, out_in, out, done, ends, sems):
    ky_halo = Halo(ky_od, ky_ev, "ky", 1)
    hold = each(lambda m: m == 1, load(hold_ref, 0))
    for e, i in enumerate((0, 1, BX - 2, BX - 1)):
        for j in MIDDLE:
            slab = i * BY + j
            q = load(q_ref, slab)
            for a in range(2):
                for b in range(2):
                    ends[e, j - MIDDLE[0], 2 * a + b] = jnp.where(hold[a][b], spec[slab], q[a][b])
    send_out(ends.at[pl.ds(0, 2)], out, sems.at[0], 0, 2, MIDDLE)
    send_out(ends.at[pl.ds(2, 2)], out, sems.at[0], BX - 2, 2, MIDDLE)

    def one_kx(i):
        hold = each(lambda m: m == 1, load(hold_ref, 0))
        gk = load(gy, 0)
        speed = [load(aky, i * (BY + 1) + f) for f in (0, 1, BY - 1, BY)]
        low = [ky_halo.low(i * 2 + l) for l in range(2)]
        high = [ky_halo.high(i * 2 + l) for l in range(2)]
        for e, (j, term) in enumerate(zip(EDGES, halo_terms(gk, speed[:2], speed[2:], low, high))):
            slab = i * BY + j
            q = each(lambda q, t: q + t, load(q_ref, slab), term)
            for a in range(2):
                for b in range(2):
                    done[i, e, 2 * a + b] = jnp.where(hold[a][b], spec[slab], q[a][b])

    def several(n, carry):
        for k in range(STEP):
            one_kx(n * STEP + k)
        rows = done.at[pl.ds(n * STEP, STEP)]
        send_out(rows.at[:, pl.ds(0, 2)], out, sems.at[1], n * STEP, STEP, EDGES[:2])
        send_out(rows.at[:, pl.ds(2, 2)], out, sems.at[1], n * STEP, STEP, EDGES[2:])
        return carry

    lax.fori_loop(0, BX // STEP, several, 0)
    wait_all(ends, sems.at[0])
    wait_all(done, sems.at[1])


def call(kernel, outs, operands, spaces, out_spaces, scratch=(), alias=None, us=1, limit=LIMIT):
    whole = {
        "v": pl.BlockSpec(memory_space=pltpu.VMEM),
        "h": pl.BlockSpec(memory_space=pltpu.HBM),
    }
    return pl.pallas_call(
        kernel,
        out_shape=tuple(outs),
        in_specs=[whole[c] for c in spaces],
        out_specs=tuple(whole[c] for c in out_spaces),
        scratch_shapes=list(scratch),
        input_output_aliases=alias or {},
        compiler_params=pltpu.CompilerParams(vmem_limit_bytes=limit),
        cost_estimate=pl.CostEstimate(flops=int(us * 1e9), bytes_accessed=0, transcendentals=0),
        name=kernel.__name__,
    )(*operands)


def per_device(action, depth_cm, inflow_mask, inflow):
    slabs, padded = BX * BY * T, (BX + 4) * BY * T
    edge_slabs, ky_tiles, kx_tiles = BX * len(EDGES) * T, BX * 2 * T, 2 * BY * T
    sizes = [lax.axis_size(axis) for axis in AXES]

    def v(*shape):
        return pltpu.VMEM(shape + (8, 128), f32)

    def swap_odd(message, axis, spare):
        return lax.ppermute(message, AXES, swaps(sizes, AXES.index(axis), 1, AXES.index(spare)))

    def swap_even(message, axis):
        return lax.ppermute(message, AXES, swaps(sizes, AXES.index(axis), 0, 0))

    sem = pltpu.SemaphoreType.DMA
    np5, kx_od, kx_ev, ky_od, ky_ev, depth, mask, spectrum = call(
        first_messages,
        (v(BX + 4, BY, T), v(2, BY, T), v(2, BY, T), v(BX, 2, T), v(BX, 2, T), pltpu.VMEM((BS, NY), jnp.int32),
         pltpu.VMEM((BS, NY), jnp.int32), pltpu.VMEM((NKX, NKY), f32)),
        (action, depth_cm, inflow_mask, inflow),
        "hhhh",
        "v" * 8,
        [sem((8,))],
        us=0,
        limit=FIRST_LIMIT,
    )
    ky_od = swap_odd(ky_od, "ky", "kx").reshape(ky_tiles, 8, 128)
    kx_ev = swap_even(kx_ev, "kx").reshape(kx_tiles, 8, 128)
    kx_od = swap_odd(kx_od, "kx", "space").reshape(kx_tiles, 8, 128)
    np3, x_od, x_ev = call(
        x_messages,
        (v(padded), v(4 * BX + 2), v(4 * BX + 2)),
        (np5.reshape(padded, 8, 128), depth, kx_ev),
        "v" * 3,
        "v" * 3,
        alias={0: 0},
        us=0,
    )
    x_od, x_ev = swap_odd(x_od, "space", "kx"), swap_even(x_ev, "space")
    ky_ev = swap_even(ky_ev, "ky").reshape(ky_tiles, 8, 128)
    ax, ay, rkx, aky, gy, heights, hold, spec = call(
        speeds,
        (v(slabs), v(slabs), v((BX + 1) * BY * T), v(BX * (BY + 1) * T), v(T), pltpu.VMEM((BS, NY), f32),
         pltpu.VMEM((T, 8, 128), jnp.int32), v(BX * BY)),
        (depth, mask, spectrum),
        "vvv",
        "v" * 8,
        [v(3 * T)],
        us=3,
    )
    (p_y,) = call(stage_one_y, (v(slabs),), (np3, ay), "vv", "v", us=1)
    np3, part, gx, edge, halo_speed, xnear, xflux, ky2_od, ky2_ev = call(
        stage_one_edges,
        (v(padded), v(edge_slabs), v(T), v(2 * BX), v(2 * BX), v(2 * BX), v(2 * BX), v(ky_tiles), v(ky_tiles)),
        (np3, p_y, ax, rkx, aky, heights, hold, spec, kx_od, x_od, x_ev),
        "v" * 11,
        "v" * 9,
        [v(len(EDGES) * T), v(4)],
        alias={0: 0},
        us=0,
    )
    ky2_od, ky2_ev = swap_odd(ky2_od, "ky", "kx"), swap_even(ky2_ev, "ky")
    (p_middle,) = call(
        stage_one_middle,
        (v(BX * len(MIDDLE) * T),),
        (np3, p_y, ax, rkx, gx, edge, xnear, xflux),
        "v" * 8,
        "v",
        [v(len(MIDDLE) * T)],
        us=2,
    )
    sp, x2 = call(
        stage_one_rest,
        (v(padded), v(4 * BX)),
        (np3, part, p_middle, aky, gy, hold, spec, ky_od, ky_ev),
        "v" * 9,
        "v" * 2,
        us=0,
    )
    x2 = lax.ppermute(x2, AXES[:2], ring(sizes))
    sp, kx2_od, kx2_ev = call(
        kx_messages,
        (v(padded), v(kx_tiles), v(kx_tiles)),
        (sp,),
        "v",
        "v" * 3,
        [sem((2,))],
        alias={0: 0},
        us=0,
    )
    kx2_od, kx2_ev = lax.ppermute(kx2_od, AXES, swaps(sizes, 1, 1, 0, True)), swap_even(kx2_ev, "kx")
    (q,) = call(
        stage_two_inner,
        (v(slabs),),
        (np3, sp, ax, ay, rkx, aky, gx, gy, edge),
        "v" * 9,
        "v",
        [v(BY * T)],
        us=0,
    )
    q, out = call(
        stage_two_x,
        (v(slabs), jax.ShapeDtypeStruct(action.shape, f32)),
        (q, ax, halo_speed, hold, spec, x2),
        "v" * 6,
        "vh",
        [v(2 * BX), v(2 * BX), v(len(INNER), len(MIDDLE), T), sem],
        alias={0: 0},
        us=2,
    )
    (q,) = call(
        stage_two_kx,
        (v(slabs),),
        (q, rkx, gx, kx2_od, kx2_ev),
        "v" * 5,
        "v",
        alias={0: 0},
        us=1,
    )
    (out,) = call(
        stage_two_ky,
        (jax.ShapeDtypeStruct(action.shape, f32),),
        (q, aky, gy, hold, spec, ky2_od, ky2_ev, out),
        "v" * 7 + "h",
        "h",
        [v(BX, len(EDGES), T), v(4, len(MIDDLE), T), sem((2,))],
        alias={7: 0},
        us=0,
    )
    return out


def solution(mesh):
    in_specs = (P("kx", "ky", "space", None), P("space", None), P("space", None), P())
    out_specs = P("kx", "ky", "space", None)
    return jax.shard_map(
        per_device, mesh=mesh, in_specs=in_specs, out_specs=out_specs, check_vma=False
    )
```
